32 devices in a mesh: grp: 2 (over x), row: 4 (over y, core), col: 4 (over z).
Axes of the slice: x: 2, y: 2, z: 4, core: 2. Of those that a mesh axis runs over, the one named last changes fastest.
Arguments:
- tokens: bfloat16 [16384, 512], P(('grp', 'row'), 'col'), may hold values from -6 to 6
- cotangent: bfloat16 [16384, 512], P(('grp', 'row'), 'col'), may hold values from -6 to 6
- norm1_gain: bfloat16 [512], P('col'), may hold values from 0.5 to 1.5
- norm1_bias: bfloat16 [512], P('col'), may hold values from -1 to 1
- qkv_weight: bfloat16 [512, 1536], P('col', 'row'), may hold values from -0.25 to 0.25
- out_weight: bfloat16 [512, 512], P('row', 'col'), may hold values from -1.5 to 1.5
- gate1_weight: bfloat16 [512, 512], P('row', 'col'), may hold values from -0.25 to 0.25
- gate1_bias: bfloat16 [512], P('col'), may hold values from -2.5 to 2.5
- norm2_gain: bfloat16 [512], P('col'), may hold values from 0.5 to 1.5
- norm2_bias: bfloat16 [512], P('col'), may hold values from -1 to 1
- up_weight: bfloat16 [512, 2048], P('col', 'row'), may hold values from -0.25 to 0.25
- up_bias: bfloat16 [2048], P('row'), may hold values from -1.5 to 1.5
- down_weight: bfloat16 [2048, 512], P('row', 'col'), may hold values from -0.1875 to 0.1875
- down_bias: bfloat16 [512], P('col'), may hold values from -1.5 to 1.5
- gate2_weight: bfloat16 [2048, 512], P('row', 'col'), may hold values from -0.125 to 0.125
- gate2_bias: bfloat16 [512], P('col'), may hold values from -2.5 to 2.5
Outputs:
- output: bfloat16 [16384, 512], P(('grp', 'row'), 'col')
- input_grad: bfloat16 [16384, 512], P(('grp', 'row'), 'col')
- grad_norm1_gain: float32 [512], P('col')
- grad_norm1_bias: float32 [512], P('col')
- grad_qkv: float32 [512, 1536], P('col', 'row')
- grad_out: float32 [512, 512], P('row', 'col')
- grad_gate1: float32 [512, 512], P('row', 'col')
- grad_gate1_bias: float32 [512], P('col')
- grad_norm2_gain: float32 [512], P('col')
- grad_norm2_bias: float32 [512], P('col')
- grad_up: float32 [512, 2048], P('col', 'row')
- grad_up_bias: float32 [2048], P('row')
- grad_down: float32 [2048, 512], P('row', 'col')
- grad_down_bias: float32 [512], P('col')
- grad_gate2: float32 [2048, 512], P('row', 'col')
- grad_gate2_bias: float32 [512], P('col')
The draws below stay inside these ranges and needn't reach their ends.
All inputs are finite; a program needn't handle non-finite values.
Results may differ from the reference program's by a relative error of at most 0.014.
Values may be sent and summed in bfloat16 or wider, within the bound.
A program may use at most 128 MiB of HBM per device.

```python
import jax
import jax.numpy as jnp
from jax import lax

D = 512
HEADS = 8
FF = 2048
HD = 64
PROMPT = 1024
CONT = 128
GTOK = 2048
GROUPS = 8
TOKENS = 16384


def shard_levels(stream_key, shape, split, least, top_value):
    def one(axis_at, parts):
        heights = jax.random.uniform(jax.random.fold_in(jax.random.fold_in(stream_key, 6), axis_at), (parts,), jnp.float32, least / len(split), top_value / len(split))
        return jnp.repeat(jnp.exp(heights), shape[axis_at] // parts).reshape((-1,) + (1,) * (len(shape) - axis_at - 1))

    level = one(*split[0])
    for cut in split[1:]:
        level = level * one(*cut)
    return level


def normal_values(rng, dims, deviation, limit, split=(), dtype=jnp.bfloat16):
    entries = jax.random.normal(rng, dims, jnp.float32) * deviation
    if len(split) > 0:
        entries = shard_levels(rng, dims, split, -0.22, 0.18) * entries
    return jnp.clip(entries, min=-limit, max=limit).astype(dtype)


def setup_inputs(seed: int = 0) -> dict:
    keys = jax.random.split(jax.random.key(seed), 17)
    return {
        "tokens": normal_values(keys[0], (TOKENS, D), 1.0, 6.0, ((0, 8), (1, 4))),
        "cotangent": normal_values(keys[1], (TOKENS, D), 1.0, 6.0, ((0, 8), (1, 4))),
        "norm1_gain": jnp.clip(1.0 + 0.1 * jax.random.normal(keys[2], (D,), jnp.float32), 0.5, 1.5).astype(jnp.bfloat16),
        "norm1_bias": normal_values(keys[3], (D,), 0.2, 1.0, ((0, 4),)),
        "qkv_weight": normal_values(keys[4], (D, 3 * D), D ** -0.5, 0.25, ((0, 4), (1, 4))),
        "out_weight": normal_values(keys[5], (D, D), (max(D // 32, 16)) ** -0.5, 1.5, ((0, 4), (1, 4))),
        "gate1_weight": normal_values(keys[6], (D, D), D ** -0.5, 0.25, ((0, 4), (1, 4))),
        "gate1_bias": normal_values(keys[7], (D,), 0.5, 2.5, ((0, 4),)),
        "norm2_gain": jnp.clip(1.0 + 0.1 * jax.random.normal(keys[8], (D,), jnp.float32), 0.5, 1.5).astype(jnp.bfloat16),
        "norm2_bias": normal_values(keys[9], (D,), 0.2, 1.0, ((0, 4),)),
        "up_weight": normal_values(keys[10], (D, FF), D ** -0.5, 0.25, ((0, 4), (1, 4))),
        "up_bias": normal_values(keys[11], (FF,), 0.3, 1.5, ((0, 4),)),
        "down_weight": normal_values(keys[12], (FF, D), (FF // 2) ** -0.5, 0.1875, ((0, 4), (1, 4))),
        "down_bias": normal_values(keys[13], (D,), 0.3, 1.5, ((0, 4),)),
        "gate2_weight": normal_values(keys[14], (FF, D), FF ** -0.5, 0.125, ((0, 4), (1, 4))),
        "gate2_bias": normal_values(keys[15], (D,), 0.5, 2.5, ((0, 4),)),
    }


@jax.custom_vjp
def low(v):
    return lax.optimization_barrier(v.astype(jnp.bfloat16)).astype(jnp.float32)

@jax.custom_vjp
def low_back(v):
    return v

def low_keep(v):
    return (low(v), None)

def low_pass(kept, grad):
    return (grad,)

def back_keep(v):
    return (v, None)

def back_low(kept, grad):
    return (low(grad),)
low.defvjp(low_keep, low_pass)
low_back.defvjp(back_keep, back_low)
HIGHEST = lax.Precision.HIGHEST
NORM_EPSILON = 1e-05
MASKED_SCORE = -1e+30

def layer_norm(residual, gain, shift):
    average = lax.optimization_barrier(jnp.mean(residual, axis=-1, keepdims=True))
    centred = residual - average
    variance = lax.optimization_barrier(jnp.mean(centred * centred, axis=-1, keepdims=True))
    return centred * lax.rsqrt(variance + NORM_EPSILON) * gain + shift

def allowed_pairs():
    query_pos = lax.broadcasted_iota(jnp.int32, (GTOK, GTOK), 0)
    key_pos = lax.broadcasted_iota(jnp.int32, (GTOK, GTOK), 1)
    query_doc = jnp.where(query_pos < PROMPT, 0, 1 + (query_pos - PROMPT) // CONT)
    key_doc = jnp.where(key_pos < PROMPT, 0, 1 + (key_pos - PROMPT) // CONT)
    return (key_pos <= query_pos) & ((key_pos < PROMPT) | (key_doc == query_doc))

def group_attention(qkv_group):
    shaped = qkv_group.reshape(GTOK, HEADS, 3, HD)
    raw_scores = jnp.einsum('qhe,khe->hqk', shaped[:, :, 0], shaped[:, :, 1], precision=HIGHEST) * HD ** (-0.5)
    raw_scores = low_back(raw_scores)
    masked = jnp.where(allowed_pairs()[None], raw_scores, MASKED_SCORE)
    softmax_rows = jax.nn.softmax(masked, axis=-1)
    attended = jnp.einsum('hqk,khe->qhe', low(softmax_rows), shaped[:, :, 2], precision=HIGHEST)
    return attended.reshape(GTOK, D)

def highway_layer(residual, gain_one, shift_one, qkv_w, out_w, gate_one_w, gate_one_b, gain_two, shift_two, up_w, up_b, down_w, down_b, gate_two_w, gate_two_b):
    normed_one = low(layer_norm(residual, gain_one, shift_one))
    qkv_rows = low(low_back(jnp.dot(normed_one, qkv_w, precision=HIGHEST)))
    attended = lax.map(jax.checkpoint(group_attention), qkv_rows.reshape(-1, GTOK, 3 * D))
    attended = low(low_back(attended.reshape(-1, D)))
    attn_out = low_back(jnp.dot(attended, out_w, precision=HIGHEST))
    gate_one = jax.nn.sigmoid(low_back(jnp.dot(attended, gate_one_w, precision=HIGHEST) + gate_one_b))
    middle = residual + gate_one * attn_out
    normed_two = low(layer_norm(middle, gain_two, shift_two))
    hidden = low(jax.nn.silu(low_back(jnp.dot(normed_two, up_w, precision=HIGHEST) + up_b)))
    ffn_out = low_back(jnp.dot(hidden, down_w, precision=HIGHEST) + down_b)
    gate_two = jax.nn.sigmoid(low_back(jnp.dot(hidden, gate_two_w, precision=HIGHEST) + gate_two_b))
    return middle + gate_two * ffn_out

def reference(tokens, cotangent, norm1_gain, norm1_bias, qkv_weight, out_weight, gate1_weight, gate1_bias, norm2_gain, norm2_bias, up_weight, up_bias, down_weight, down_bias, gate2_weight, gate2_bias):
    params = (norm1_gain.astype(jnp.float32), norm1_bias.astype(jnp.float32), qkv_weight.astype(jnp.float32), out_weight.astype(jnp.float32), gate1_weight.astype(jnp.float32), gate1_bias.astype(jnp.float32), norm2_gain.astype(jnp.float32), norm2_bias.astype(jnp.float32), up_weight.astype(jnp.float32), up_bias.astype(jnp.float32), down_weight.astype(jnp.float32), down_bias.astype(jnp.float32), gate2_weight.astype(jnp.float32), gate2_bias.astype(jnp.float32))
    group_rows = tokens.astype(jnp.float32).reshape(GROUPS, GTOK, D)
    group_cots = cotangent.astype(jnp.float32).reshape(GROUPS, GTOK, D)

    def one_group(totals, item):
        rows, cots = item
        result, pullback = jax.vjp(highway_layer, rows, *params)
        gradients = pullback(cots)
        totals = tuple((total + grad for total, grad in zip(totals, gradients[1:])))
        return (totals, (result.astype(jnp.bfloat16), gradients[0].astype(jnp.bfloat16)))
    initial = tuple((jnp.zeros_like(param) for param in params))
    sums, (results, input_grads) = lax.scan(one_group, initial, (group_rows, group_cots))
    return (results.reshape(TOKENS, D), input_grads.reshape(TOKENS, D), sums[0], sums[1], sums[2], sums[3], sums[4], sums[5], sums[6], sums[7], sums[8], sums[9], sums[10], sums[11], sums[12], sums[13])
```

```python
from functools import partial

import jax
import jax.numpy as jnp
from jax import lax
from jax.experimental import pallas as pl
from jax.experimental.pallas import tpu as pltpu
from jax.sharding import PartitionSpec as P

bf16 = jnp.bfloat16
f32 = jnp.float32
EPS = 1e-05
MASKED = -1e30
MESH = pl.DeviceIdType.MESH

T = 512
D = 512
BLOCK = {"qkv": (128, 384), "og": (128, 256), "up": (128, 512), "dg": (512, 256)}
NAMES = ("qkv", "og", "up", "dg")


def dot(a, b, ca, cb):
    return lax.dot_general(a, b, (((ca,), (cb,)), ((), ())), preferred_element_type=f32)


def loop(count, step):
    lax.fori_loop(0, count, lambda i, z: (step(i), z)[1], 0)


def cat(parts, axis=1):
    return jnp.concatenate(parts, axis=axis)


def sigmoid(v):
    return 1.0 / (1.0 + jnp.exp(-v))


def kernel(use_x, names_in, names_out, names_scr, *refs):
    ref = dict(zip(names_in + names_out + names_scr, refs))
    R = type("R", (), ref)
    a = lax.axis_index("grp")
    r = lax.axis_index("row")
    c = lax.axis_index("col")
    y, k = r // 2, r % 2
    ah = a % 2
    q = 2 * (c % 2) + k
    core = (a, 2 * y + 1 - k, c)
    yside = (a, 2 * (1 - y) + k, c)
    xside = (a + 1 - 2 * ah, r, c)
    zside = (a, r, c + 1 - 2 * (c % 2))
    owner_row = 2 * y + c // 2
    lo_row = pl.multiple_of(q * 128, 128)
    hi_row = pl.multiple_of((7 - q) * 128, 128)

    counter = [0]
    pending = []

    def send(src, dst, dev):
        i = counter[0]
        counter[0] += 1
        cp = pltpu.make_async_remote_copy(
            src_ref=src, dst_ref=dst, send_sem=R.ssem.at[i], recv_sem=R.rsem.at[i],
            device_id=dev, device_id_type=MESH)
        cp.start()
        pending.append(cp)
        return cp

    local = []

    def fetch(src, dst):
        cp = pltpu.make_async_copy(src, dst, R.lsem.at[len(local)])
        cp.start()
        local.append(cp)

    fetch(R.i_qkv, R.qstage)
    for t in range(2):
        for name, sources in (("og", ("out", "gate1")), ("up", ("up",)), ("dg", ("down", "gate2"))):
            rows, cols = BLOCK[name]
            rq = rows // 4
            w = getattr(R, "w_" + name)
            width = cols // len(sources)
            for j, s in enumerate(sources):
                at = pl.multiple_of((2 * t + ah) * rq, 32)
                fetch(getattr(R, "i_" + s).at[pl.ds(at, rq), :],
                      w.at[y, k, c, t, ah, :, pl.ds(j * width, width)])

    barrier = pltpu.get_barrier_semaphore()
    friends = [(a, 2 * y + kk, cc) for kk in range(2) for cc in range(4)]
    for kk in range(2):
        for cc in range(4):
            me = (k == kk) & (c == cc)

            @pl.when(jnp.logical_not(me))
            def _():
                pl.semaphore_signal(barrier, inc=1, device_id=(a, 2 * y + kk, cc), device_id_type=MESH)
    diag = (a, 2 * (1 - y) + 1 - k, c)
    for dev in (yside, xside, diag):
        pl.semaphore_signal(barrier, inc=1, device_id=dev, device_id_type=MESH)

    local[0].wait()
    for t in range(2):
        blk = R.qstage[pl.ds(pl.multiple_of((2 * t + ah) * 32, 32), 32), :].astype(f32)
        parts = [blk[:, (3 * h + j) * 64:(3 * h + j + 1) * 64] for j in range(3) for h in range(2)]
        R.w_qkv[y, k, c, t, ah] = cat(parts).astype(bf16)
    pl.semaphore_wait(barrier, 10)

    def rows_in(src, dst, which):
        sends = []
        for qq in range(4):
            kq, cq = qq % 2, 2 * k + qq // 2
            me = (k == kq) & (c == cq)
            for j, (s0, d0, n) in enumerate(((qq * 128, 0, 128), ((7 - qq) * 128, 128, 128), ((8 + 2 * qq) * 128, 256, 256))):
                s = src.at[pl.ds(s0, n), :]
                d = dst.at[c, pl.ds(d0, n), :]
                rs = R.irsem.at[which, c, j]
                cp = pltpu.make_async_remote_copy(
                    src_ref=s, dst_ref=d, send_sem=R.issem.at[which, qq, j], recv_sem=rs,
                    device_id=(a, 2 * y + kq, cq), device_id_type=MESH)
                sends.append((me, cp))

                @pl.when(jnp.logical_not(me))
                def _():
                    cp.start()

                @pl.when(me)
                def _():
                    pltpu.make_async_copy(s, d, rs).start()

        def wait():
            for cc in range(4):
                for j, (d0, n) in enumerate(((0, 128), (128, 128), (256, 256))):
                    d = dst.at[cc, pl.ds(d0, n), :]
                    pltpu.make_async_copy(d, d, R.irsem.at[which, cc, j]).wait()
        return sends, wait

    def rows_out(src, dst, which):
        sends = []
        for cc in range(4):
            me = (c // 2 == k) & (c == cc)
            for j, (s0, d0, n) in enumerate(((0, lo_row, 128), (128, hi_row, 128), (256, 1024 + pl.multiple_of(q * 256, 256), 256))):
                s = src.at[cc, pl.ds(s0, n), :]
                d = dst.at[pl.ds(d0, n), :]
                rs = R.irsem.at[which, q, j]
                cp = pltpu.make_async_remote_copy(
                    src_ref=s, dst_ref=d, send_sem=R.issem.at[which, cc, j], recv_sem=rs,
                    device_id=(a, owner_row, cc), device_id_type=MESH)
                sends.append((me, cp))

                @pl.when(jnp.logical_not(me))
                def _():
                    cp.start()

                @pl.when(me)
                def _():
                    pltpu.make_async_copy(s, d, rs).start()

        def wait():
            for qq in range(4):
                for j, (d0, n) in enumerate(((qq * 128, 128), ((7 - qq) * 128, 128), ((8 + 2 * qq) * 128, 256))):
                    d = dst.at[pl.ds(d0, n), :]
                    pltpu.make_async_copy(d, d, R.irsem.at[which, qq, j]).wait()
        return sends, wait

    def finish_sends(sends):
        for me, cp in sends:
            @pl.when(jnp.logical_not(me))
            def _():
                cp.wait_send()

    wst = {}

    def w_z(name):
        w = getattr(R, "w_" + name)
        here = w.at[y, k, c, :, ah]
        wst[name, "z"] = [send(here, here, (a, r, (c + i) % 4)) for i in range(1, 4)]

    def w_1(name):
        w = getattr(R, "w_" + name)
        for cp in wst[name, "z"]:
            cp.wait_recv()
        s = w.at[y, k, :, 0, ah]
        wst[name, "x1"] = send(s, s, xside)
        s = w.at[y, k, :, 1, ah]
        wst[name, "y1"] = send(s, s, yside)

    def w_2(name):
        w = getattr(R, "w_" + name)
        wst[name, "x1"].wait_recv()
        s = w.at[y, k, :, 0]
        wst[name, "y2"] = send(s, s, yside)
        wst[name, "y1"].wait_recv()
        s = w.at[:, k, :, 1, ah]
        wst[name, "x2"] = send(s, s, xside)

    def w_3(name):
        w = getattr(R, "w_" + name)
        wst[name, "y2"].wait_recv()
        wst[name, "x2"].wait_recv()
        s = w.at[:, k]
        wst[name, "core"] = send(s, s, core)

    def w_4(name):
        wst[name, "core"].wait_recv()

    gst = {}

    def add_into(dst, other, lead):
        for_index = [()]
        for n in lead:
            for_index = [ix + (i,) for ix in for_index for i in range(n)]
        for ix in for_index:
            dst[ix] = (dst[ix].astype(f32) + other(ix).astype(f32)).astype(bf16)

    def g_0(name):
        g, b0 = getattr(R, "g_" + name), getattr(R, "b0_" + name)
        gst[name, "core"] = send(g.at[:, 1 - k], b0, core)

    def g_1(name):
        g, b0, b1 = getattr(R, "g_" + name), getattr(R, "b0_" + name), getattr(R, "b1_" + name)
        gst[name, "core"].wait_recv()

        def one(i):
            yy, cc = i // 4, i % 4
            b0[yy, cc] = (b0[yy, cc].astype(f32) + g[yy, k, cc].astype(f32)).astype(bf16)
        loop(8, one)
        if use_x:
            b2 = getattr(R, "b2_" + name)
            gst[name, "y1"] = send(b0.at[1 - y, :, 0], b1, yside)
            gst[name, "x1"] = send(b0.at[:, :, 1, 1 - ah], b2, xside)
        else:
            gst[name, "y1"] = send(b0.at[1 - y], b1, yside)

    def g_2(name):
        b0, b1 = getattr(R, "b0_" + name), getattr(R, "b1_" + name)
        gst[name, "y1"].wait_recv()
        if not use_x:
            def one(cc):
                b1[cc] = (b1[cc].astype(f32) + b0[y, cc].astype(f32)).astype(bf16)
            loop(4, one)
            return
        b2, b3, b4 = (getattr(R, "b%d_%s" % (i, name)) for i in (2, 3, 4))

        def one(cc):
            b1[cc] = (b1[cc].astype(f32) + b0[y, cc, 0].astype(f32)).astype(bf16)
        loop(4, one)
        gst[name, "x2"] = send(b1.at[:, 1 - ah], b3, xside)
        gst[name, "x1"].wait_recv()

        def two(i):
            yy, cc = i // 4, i % 4
            b2[yy, cc] = (b2[yy, cc].astype(f32) + b0[yy, cc, 1, ah].astype(f32)).astype(bf16)
        loop(8, two)
        gst[name, "y2"] = send(b2.at[1 - y], b4, yside)

    def g_3(name):
        b1, z, b5 = (getattr(R, "%s_%s" % (i, name)) for i in ("b1", "z" if use_x else "b1", "b5"))
        if use_x:
            b2, b3, b4 = (getattr(R, "b%d_%s" % (i, name)) for i in (2, 3, 4))
            gst[name, "x2"].wait_recv()
            gst[name, "y2"].wait_recv()

            def one(cc):
                z[cc, 0] = (b1[cc, ah].astype(f32) + b3[cc].astype(f32)).astype(bf16)
                z[cc, 1] = (b2[y, cc].astype(f32) + b4[cc].astype(f32)).astype(bf16)
            loop(4, one)
        gst[name, "z"] = [send(z.at[(c + i) % 4], b5.at[i - 1], (a, r, (c + i) % 4)) for i in range(1, 4)]

    def g_4(name):
        z, b5, fin = (getattr(R, "%s_%s" % (i, name)) for i in ("z" if use_x else "b1", "b5", "fin"))
        for cp in gst[name, "z"]:
            cp.wait_recv()
        if use_x:
            for t in range(2):
                total = z[c, t].astype(f32)
                for i in range(3):
                    total = total + b5[i, t].astype(f32)
                fin[t, ah] = total.astype(bf16)
            s = fin.at[:, ah]
            gst[name, "x3"] = send(s, s, xside)
        else:
            for t in range(2):
                for i2 in range(2):
                    total = z[c, t, i2].astype(f32)
                    for i in range(3):
                        total = total + b5[i, t, i2].astype(f32)
                    fin[t, i2] = total.astype(bf16)

    def g_5(name):
        fin = getattr(R, "fin_" + name)
        if use_x:
            gst[name, "x3"].wait_recv()
        rows, cols = BLOCK[name]
        return fin[...].reshape(rows, cols).astype(f32)

    def weight(name, rr):
        w = getattr(R, "w_" + name)
        return w[rr // 2, rr % 2].reshape(4 * BLOCK[name][0], BLOCK[name][1])

    R.vecs[c] = R.vec[...]
    R.vecr[r] = R.vec[...]
    vec_cp = [send(R.vec, R.vecs.at[c], (a, r, (c + i) % 4)) for i in range(1, 4)]
    vec_cp += [send(R.vec, R.vecr.at[r], dev) for dev in (core, yside, diag)]
    w_z("qkv")
    tok_sends, tok_wait = rows_in(R.tok, R.xo, 0)
    for cp in local[1:]:
        cp.wait()
    w_z("og")
    w_1("qkv")
    w_z("up")
    w_2("qkv")
    w_z("dg")
    for cp in vec_cp:
        cp.wait_recv()

    def vec_row(i):
        return cat([R.vecs[cc, i:i + 1, :] for cc in range(4)])

    tok_wait()

    def xrows():
        return cat([R.xo[cc] for cc in range(4)]).astype(f32)

    def norm_parts(v):
        mean = jnp.sum(v, axis=1, keepdims=True) * (1.0 / D)
        cen = v - mean
        var = jnp.sum(cen * cen, axis=1, keepdims=True) * (1.0 / D)
        inv = lax.rsqrt(var + EPS)
        return cen * inv, inv

    standard, _ = norm_parts(xrows())
    n1 = (standard * vec_row(0) + vec_row(1)).astype(bf16)
    R.n1[...] = n1
    R.xn[pl.ds(lo_row, 128), :] = n1[0:128]
    R.xn[pl.ds(hi_row, 128), :] = n1[128:256]
    R.xn[1024:1280, :] = n1[256:512]
    here = [R.xn.at[pl.ds(lo_row, 128), :], R.xn.at[pl.ds(hi_row, 128), :]]
    to_z = [send(s, s, zside) for s in here]
    to_core = [send(s, s, core) for s in here]
    w_3("qkv")
    w_1("og")
    w_2("og")
    cot_sends, cot_wait = rows_in(R.cot, R.co, 1)
    qz = q + 2 - 4 * (q // 2)
    for cp in to_z:
        cp.wait_recv()
    there = [R.xn.at[pl.ds(pl.multiple_of(qz * 128, 128), 128), :],
             R.xn.at[pl.ds(pl.multiple_of((7 - qz) * 128, 128), 128), :]]
    to_core += [send(s, s, core) for s in there]
    w_4("qkv")
    for cp in to_core:
        cp.wait_recv()

    def qkv_pair(p):
        w = weight("qkv", p)
        R.qp[p] = (dot(R.n1[...], w[:, 0:128], 1, 0).astype(bf16).astype(f32) * 0.125).astype(bf16)
        R.kv[p] = dot(R.xn[...], w[:, 128:384], 1, 0).astype(bf16)
    loop(4, qkv_pair)
    w_3("og")
    w_1("up")
    w_1("dg")

    lane = lax.broadcasted_iota(jnp.int32, (T, 128), 1)
    key_at = lax.broadcasted_iota(jnp.int32, (512, 128), 0)
    col_at = lax.broadcasted_iota(jnp.int32, (512, 128), 1)
    lo_ok = key_at <= col_at + q * 128
    hi_ok = key_at + 512 <= col_at + (7 - q) * 128
    own_ok = (key_at <= col_at)[0:128]

    def attend_pair(p):
        for h in range(2):
            keys = R.kv[p, :, 0:128]
            vals = R.kv[p, :, 128:256]
            qm = jnp.where(lane // 64 == h, R.qp[p], jnp.zeros((), bf16))
            s1 = dot(keys[0:512], qm, 1, 1)
            s2 = dot(keys[512:1024], qm[128:512], 1, 1)
            sa = jnp.where(own_ok, dot(keys[1024:1152], qm[256:384], 1, 1), MASKED)
            sb = jnp.where(own_ok, dot(keys[1152:1280], qm[384:512], 1, 1), MASKED)
            s1 = cat([jnp.where(lo_ok, s1[:, 0:128], MASKED), s1[:, 128:512]])
            s2 = cat([jnp.where(hi_ok, s2[:, 0:128], MASKED), s2[:, 128:384]])
            top = lambda v: jnp.max(v, axis=0, keepdims=True)
            add = lambda v: jnp.sum(v, axis=0, keepdims=True)
            m1 = top(s1)
            m2 = jnp.maximum(m1[:, 128:512], top(s2))
            m = cat([m1[:, 0:128], m2[:, 0:128], jnp.maximum(m2[:, 128:384], cat([top(sa), top(sb)]))])
            e1 = jnp.exp(s1 - m)
            e2 = jnp.exp(s2 - m[:, 128:512])
            ea = jnp.exp(sa - m[:, 256:384])
            eb = jnp.exp(sb - m[:, 384:512])
            l1 = add(e1)
            l2 = l1[:, 128:512] + add(e2)
            total = cat([l1[:, 0:128], l2[:, 0:128], l2[:, 128:384] + cat([add(ea), add(eb)])])
            e1, e2, ea, eb = (v.astype(bf16) for v in (e1, e2, ea, eb))
            R.p1[2 * p + h] = e1
            R.p2[2 * p + h] = e2
            R.po[2 * p + h, :, 0:128] = ea
            R.po[2 * p + h, :, 128:256] = eb
            o1 = dot(vals[0:512], e1, 0, 0)
            o2 = dot(vals[512:1024], e2, 0, 0)
            oa = dot(vals[1024:1152], ea, 0, 0)
            ob = dot(vals[1152:1280], eb, 0, 0)
            o2 = o1[:, 128:512] + o2
            o = cat([o1[:, 0:128], o2[:, 0:128], o2[:, 128:384] + cat([oa, ob])])
            inv = 1.0 / total
            R.li[p, h:h + 1, :] = inv
            R.att[p, 64 * h:64 * h + 64, :] = (o[64 * h:64 * h + 64] * inv).astype(bf16)
    loop(4, attend_pair)
    w_4("og")
    w_2("up")
    w_2("dg")

    def lanes(cc):
        return pl.ds(pl.multiple_of(cc * 128, 128), 128)

    def wide(cc):
        return pl.ds(pl.multiple_of(cc * 256, 256), 256)

    def out_block(cc):
        w = R.w_og[:, :, cc].reshape(512, 256)
        br = dot(R.att[...].reshape(512, T), w, 0, 0)
        ao = br[:, 0:128]
        gate = sigmoid(br[:, 128:256] + R.vecs[cc, 2:3, :])
        R.ao[cc] = ao
        R.g1[cc] = gate
        R.mid[cc] = R.xo[cc].astype(f32) + gate * ao
    loop(4, out_block)

    def midrows():
        return cat([R.mid[cc] for cc in range(4)])

    standard, _ = norm_parts(midrows())
    R.n2[...] = (standard * vec_row(3) + vec_row(4)).astype(bf16)
    w_3("up")
    w_3("dg")
    w_4("up")

    def up_block(rr):
        pre = dot(R.n2[...], weight("up", rr), 1, 0) + cat([R.vecr[rr, 8 + i:9 + i, :] for i in range(4)])
        s = sigmoid(pre)
        R.hid[rr] = (pre * s).astype(bf16)
        R.slp[rr] = (s * (1.0 + pre * (1.0 - s))).astype(bf16)
    loop(4, up_block)
    w_4("dg")
    cot_wait()

    def down_block(cc):
        br = dot(R.hid[0], R.w_dg[0, 0, cc].reshape(512, 256), 1, 0)
        for rr in range(1, 4):
            br = br + dot(R.hid[rr], R.w_dg[rr // 2, rr % 2, cc].reshape(512, 256), 1, 0)
        ffn = br[:, 0:128] + R.vecs[cc, 5:6, :]
        gate = sigmoid(br[:, 128:256] + R.vecs[cc, 6:7, :])
        R.out[cc] = (R.mid[cc] + gate * ffn).astype(bf16)
        g = R.co[cc].astype(f32)
        gf = (g * gate).astype(bf16)
        gg = (g * ffn * gate * (1.0 - gate)).astype(bf16)
        R.pair[cc, :, 0:128] = gf
        R.pair[cc, :, 128:256] = gg
        R.sv[5, pl.ds(cc, 1), :] = jnp.sum(gf.astype(f32), axis=0, keepdims=True)
        R.sv[6, pl.ds(cc, 1), :] = jnp.sum(gg.astype(f32), axis=0, keepdims=True)
    loop(4, down_block)
    out_sends, out_wait = rows_out(R.out, R.out_o, 2)

    def grad_down(i):
        rr, cc = i // 4, i % 4
        R.g_dg[rr // 2, rr % 2, cc] = dot(R.hid[rr], R.pair[cc], 0, 0).astype(bf16).reshape(2, 2, 128, 256)
    loop(16, grad_down)
    g_0("dg")

    def back_up(rr):
        gh = dot(R.pair[0], R.w_dg[rr // 2, rr % 2, 0].reshape(512, 256), 1, 1)
        for cc in range(1, 4):
            gh = gh + dot(R.pair[cc], R.w_dg[rr // 2, rr % 2, cc].reshape(512, 256), 1, 1)
        gp = (gh * R.slp[rr].astype(f32)).astype(bf16)
        R.slp[rr] = gp
        tot = jnp.sum(gp.astype(f32), axis=0, keepdims=True)
        for i in range(4):
            R.sv[8 + rr, i:i + 1, :] = tot[:, 128 * i:128 * i + 128]
    loop(4, back_up)
    g_1("dg")

    def grad_up(rr):
        R.g_up[rr // 2, rr % 2] = dot(R.n2[...], R.slp[rr], 0, 0).astype(bf16).reshape(4, 2, 2, 32, 512)
    loop(4, grad_up)
    g_0("up")

    gn = dot(R.slp[0], weight("up", 0), 1, 1)
    for rr in range(1, 4):
        gn = gn + dot(R.slp[rr], weight("up", rr), 1, 1)

    def norm_back(v, grad, gain_row, at):
        std, inv = norm_parts(v)
        gs = jnp.sum(grad * std, axis=0, keepdims=True)
        gb = jnp.sum(grad, axis=0, keepdims=True)
        for cc in range(4):
            R.sv[at, cc:cc + 1, :] = gs[:, 128 * cc:128 * cc + 128]
            R.sv[at + 1, cc:cc + 1, :] = gb[:, 128 * cc:128 * cc + 128]
        s = grad * vec_row(gain_row)
        f = jnp.sum(s, axis=1, keepdims=True) * (1.0 / D)
        e = jnp.sum(s * std, axis=1, keepdims=True) * (1.0 / D)
        return inv * (s - f - std * e)

    gm = norm_back(midrows(), gn, 3, 2)
    for cc in range(4):
        g_mid = R.co[cc].astype(f32) + gm[:, 128 * cc:128 * cc + 128]
        R.gm[cc] = g_mid
        gate = R.g1[cc]
        ga = (g_mid * gate).astype(bf16)
        gg = (g_mid * R.ao[cc] * gate * (1.0 - gate)).astype(bf16)
        R.pair[cc, :, 0:128] = ga
        R.pair[cc, :, 128:256] = gg
        R.sv[4, cc:cc + 1, :] = jnp.sum(gg.astype(f32), axis=0, keepdims=True)
    g_1("up")

    def grad_out(cc):
        R.g_og[:, :, cc] = dot(R.att[...].reshape(512, T), R.pair[cc], 1, 0).astype(bf16).reshape(2, 2, 2, 2, 32, 256)
    loop(4, grad_out)
    g_0("og")
    g_2("dg")
    do = dot(R.w_og[:, :, 0].reshape(512, 256), R.pair[0], 1, 1)
    for cc in range(1, 4):
        do = do + dot(R.w_og[:, :, cc].reshape(512, 256), R.pair[cc], 1, 1)
    for cc in range(4):
        R.mid[cc] = do[:, 128 * cc:128 * cc + 128]
    g_1("og")
    g_2("up")
    g_3("dg")

    row_of = lax.broadcasted_iota(jnp.int32, (128, T), 0)

    def back_pair(p):
        rows = pl.ds(pl.multiple_of(p * 128, 128), 128)
        dot_t = cat([R.mid[cc, rows, :] for cc in range(4)])
        dot_t = dot_t * jnp.where(row_of < 64, R.li[p, 0:1, :], R.li[p, 1:2, :])
        prod = dot_t * R.att[p].astype(f32)
        dot_t = dot_t.astype(bf16)
        dot_n = dot_t.T
        keys = R.kv[p, :, 0:128]
        vals = R.kv[p, :, 128:256]
        grads = []
        queries = []
        for h in range(2):
            delta = jnp.sum(prod[64 * h:64 * h + 64], axis=0, keepdims=True)
            qm = jnp.where(lane // 64 == h, R.qp[p], jnp.zeros((), bf16))
            om = jnp.where(lane // 64 == h, dot_n, jnp.zeros((), bf16))
            omt = jnp.where(row_of // 64 == h, dot_t, jnp.zeros((), bf16))
            e1, e2 = R.p1[2 * p + h], R.p2[2 * p + h]
            ea, eb = R.po[2 * p + h, :, 0:128], R.po[2 * p + h, :, 128:256]
            d1 = (e1.astype(f32) * (dot(vals[0:512], omt, 1, 0) - delta)).astype(bf16)
            d2 = (e2.astype(f32) * (dot(vals[512:1024], omt[:, 128:512], 1, 0) - delta[:, 128:512])).astype(bf16)
            da = (ea.astype(f32) * (dot(vals[1024:1152], omt[:, 256:384], 1, 0) - delta[:, 256:384])).astype(bf16)
            db = (eb.astype(f32) * (dot(vals[1152:1280], omt[:, 384:512], 1, 0) - delta[:, 384:512])).astype(bf16)
            dk = cat([dot(d1, qm, 1, 0), dot(d2, qm[128:512], 1, 0), dot(da, qm[256:384], 1, 0), dot(db, qm[384:512], 1, 0)], 0)
            dv = cat([dot(e1, om, 1, 0), dot(e2, om[128:512], 1, 0), dot(ea, om[256:384], 1, 0), dot(eb, om[384:512], 1, 0)], 0)
            grads.append((dk, dv))
            x1 = dot(keys[0:512], d1, 0, 0)
            x2 = x1[:, 128:512] + dot(keys[512:1024], d2, 0, 0)
            xab = cat([dot(keys[1024:1152], da, 0, 0), dot(keys[1152:1280], db, 0, 0)])
            dq = cat([x1[:, 0:128], x2[:, 0:128], x2[:, 128:384] + xab])
            queries.append(dq[64 * h:64 * h + 64])
        R.kv[p, :, 0:128] = (grads[0][0] + grads[1][0]).astype(bf16)
        R.kv[p, :, 128:256] = (grads[0][1] + grads[1][1]).astype(bf16)
        R.qp[p] = (cat(queries, 0) * 0.125).astype(bf16).T
    loop(4, back_pair)
    g_2("og")
    g_3("up")
    g_4("dg")

    def back_rows(first, count):
        rows = pl.ds(first, count)
        total = dot(R.kv[0, rows, :], weight("qkv", 0)[:, 128:384], 1, 1)
        for p in range(1, 4):
            total = total + dot(R.kv[p, rows, :], weight("qkv", p)[:, 128:384], 1, 1)
        return total

    def chunk_rows(qq):
        return (pl.multiple_of(qq * 128, 128), pl.multiple_of((7 - qq) * 128, 128))

    q1 = q + 1 - 2 * k
    q2 = qz
    q3 = q2 + 1 - 2 * k
    for i, row in enumerate(chunk_rows(q1)):
        R.ex[0, 128 * i:128 * i + 128, :] = back_rows(row, 128).astype(bf16)
    for i, row in enumerate(chunk_rows(q3)):
        R.ex[1, 128 * i:128 * i + 128, :] = back_rows(row, 128).astype(bf16)
    part_core = send(R.ex, R.exr, core)
    mine2 = [back_rows(row, 128) for row in chunk_rows(q2)]
    part_core.wait_recv()
    for i in range(2):
        R.ez[128 * i:128 * i + 128, :] = (mine2[i] + R.exr[1, 128 * i:128 * i + 128, :].astype(f32)).astype(bf16)
    part_z = send(R.ez, R.ezr, zside)

    def grad_qkv(p):
        g = cat([dot(R.n1[...], R.qp[p], 0, 0), dot(R.xn[...], R.kv[p], 0, 0)]).astype(bf16)
        R.g_qkv[p // 2, p % 2] = g.reshape(4, 2, 2, 32, 384)
    loop(4, grad_qkv)
    g_0("qkv")
    g_3("og")
    g_4("up")

    for row, n, at in ((lo_row, 128, 0), (hi_row, 128, 128), (1024, 256, 256)):
        own = back_rows(row, n)
        for cc in range(4):
            R.mid[cc, at:at + n, :] = own[:, 128 * cc:128 * cc + 128]

    def add_queries(p):
        more = dot(R.qp[p], weight("qkv", p)[:, 0:128], 1, 1)
        for cc in range(4):
            R.mid[cc] = R.mid[cc] + more[:, 128 * cc:128 * cc + 128]
    loop(4, add_queries)
    g_1("qkv")
    part_z.wait_recv()
    for cc in range(4):
        here = slice(128 * cc, 128 * cc + 128)
        R.mid[cc, 0:256, :] = R.mid[cc, 0:256, :] + (R.exr[0, :, here].astype(f32) + R.ezr[:, here].astype(f32))
    gx = norm_back(xrows(), midrows(), 0, 0)
    for cc in range(4):
        R.ing[cc] = (R.gm[cc] + gx[:, 128 * cc:128 * cc + 128]).astype(bf16)
    ing_sends, ing_wait = rows_out(R.ing, R.ing_o, 3)
    g_2("qkv")
    g_3("qkv")

    s1 = send(R.sv, R.svr.at[0], core)
    s1.wait_recv()
    R.sv2[...] = R.sv[...] + R.svr[0]
    s2 = send(R.sv2, R.svr.at[1], yside)
    g_4("og")
    s2.wait_recv()
    R.sv3[...] = R.sv2[...] + R.svr[1]
    if use_x:
        s3 = send(R.sv3, R.svr.at[2], xside)
        g_4("qkv")
        s3.wait_recv()
        R.sv4[...] = R.sv3[...] + R.svr[2]
    else:
        g_4("qkv")
        R.sv4[...] = R.sv3[...]
    s4 = [send(R.sv4, R.svr.at[2 + i], (a, r, (c + i) % 4)) for i in range(1, 4)]

    R.dg_o[...] = g_5("dg")
    R.up_o[...] = g_5("up")
    R.og_o[...] = g_5("og")
    g = g_5("qkv")
    R.qkv_o[...] = cat([g[:, (2 * j + h) * 64:(2 * j + h + 1) * 64] for h in range(2) for j in range(3)])
    for cp in s4:
        cp.wait_recv()
    R.svr[2] = R.sv4[...]
    R.small_o[...] = jnp.zeros((16, 128), f32)
    order = [2 + lax.rem(c - cc + 4, 4) for cc in range(4)]

    def total_of(i, j):
        v = R.svr[order[0], i, pl.ds(j, 1), :]
        for cc in range(1, 4):
            v = v + R.svr[order[cc], i, pl.ds(j, 1), :]
        return v
    for i in range(7):
        R.small_o[i:i + 1, :] = total_of(i, c)
    for i in range(4):
        R.small_o[8 + i:9 + i, :] = total_of(8 + r, i)

    out_wait()
    ing_wait()
    for cp in pending:
        cp.wait_send()
    for sends in (tok_sends, cot_sends, out_sends, ing_sends):
        finish_sends(sends)


def body(use_x, tokens, cotangent, norm1_gain, norm1_bias, qkv_weight, out_weight, gate1_weight,
         gate1_bias, norm2_gain, norm2_bias, up_weight, up_bias, down_weight, down_bias,
         gate2_weight, gate2_bias):
    vec = jnp.concatenate([norm1_gain, norm1_bias, gate1_bias, norm2_gain, norm2_bias, down_bias,
                           gate2_bias, jnp.zeros_like(gate2_bias), up_bias,
                           jnp.zeros((512,), bf16)]).astype(f32).reshape(16, 128)
    hbm = pl.BlockSpec(memory_space=pl.ANY)
    vmem = pl.BlockSpec(memory_space=pltpu.VMEM)
    ins = {"tok": tokens, "cot": cotangent, "i_qkv": qkv_weight, "i_out": out_weight, "i_gate1": gate1_weight,
           "i_up": up_weight, "i_down": down_weight, "i_gate2": gate2_weight, "vec": vec}
    outs = {"out_o": ((2048, 128), bf16, hbm), "ing_o": ((2048, 128), bf16, hbm),
            "qkv_o": ((128, 384), f32, vmem), "og_o": ((128, 256), f32, vmem),
            "up_o": ((128, 512), f32, vmem), "dg_o": ((512, 256), f32, vmem),
            "small_o": ((16, 128), f32, vmem)}
    scr = {}
    for name in NAMES:
        rows, cols = BLOCK[name]
        rq = rows // 4
        scr["w_" + name] = ((2, 2, 4, 2, 2, rq, cols), bf16)
        scr["g_" + name] = ((2, 2, 4, 2, 2, rq, cols), bf16)
        scr["b0_" + name] = ((2, 4, 2, 2, rq, cols), bf16)
        if use_x:
            scr["b1_" + name] = ((4, 2, rq, cols), bf16)
            scr["b2_" + name] = ((2, 4, rq, cols), bf16)
            scr["b3_" + name] = ((4, rq, cols), bf16)
            scr["b4_" + name] = ((4, rq, cols), bf16)
            scr["z_" + name] = ((4, 2, rq, cols), bf16)
            scr["b5_" + name] = ((3, 2, rq, cols), bf16)
        else:
            scr["b1_" + name] = ((4, 2, 2, rq, cols), bf16)
            scr["b5_" + name] = ((3, 2, 2, rq, cols), bf16)
        scr["fin_" + name] = ((2, 2, rq, cols), bf16)
    scr.update({
        "qstage": ((128, 384), bf16), "vecs": ((4, 16, 128), f32), "vecr": ((4, 16, 128), f32),
        "xo": ((4, T, 128), bf16), "co": ((4, T, 128), bf16), "n1": ((T, D), bf16),
        "xn": ((1280, D), bf16), "qp": ((4, T, 128), bf16), "kv": ((4, 1280, 256), bf16),
        "p1": ((8, 512, 512), bf16), "p2": ((8, 512, 384), bf16), "po": ((8, 128, 256), bf16),
        "li": ((4, 8, T), f32), "att": ((4, 128, T), bf16), "ao": ((4, T, 128), f32),
        "g1": ((4, T, 128), f32), "mid": ((4, T, 128), f32), "n2": ((T, D), bf16),
        "hid": ((4, T, 512), bf16), "slp": ((4, T, 512), bf16), "out": ((4, T, 128), bf16),
        "pair": ((4, T, 256), bf16), "gm": ((4, T, 128), f32), "ing": ((4, T, 128), bf16),
        "ex": ((2, 256, D), bf16), "exr": ((2, 256, D), bf16), "ez": ((256, D), bf16), "ezr": ((256, D), bf16),
        "sv": ((12, 8, 128), f32), "sv2": ((12, 8, 128), f32), "sv3": ((12, 8, 128), f32),
        "sv4": ((12, 8, 128), f32), "svr": ((6, 12, 8, 128), f32),
    })
    shapes = [pltpu.VMEM(s, d) for s, d in scr.values()]
    names_scr = tuple(scr) + ("ssem", "rsem", "issem", "irsem", "lsem")
    n_sem = 104
    dma = pltpu.SemaphoreType.DMA
    shapes += [dma((n_sem,)), dma((n_sem,)), dma((4, 4, 3)), dma((4, 4, 3)), dma((16,))]
    res = pl.pallas_call(
        partial(kernel, use_x, tuple(ins), tuple(outs), names_scr),
        out_shape=[jax.ShapeDtypeStruct(s, d) for s, d, _ in outs.values()],
        in_specs=[hbm] * 8 + [vmem],
        out_specs=[sp for _, _, sp in outs.values()],
        scratch_shapes=shapes,
        compiler_params=pltpu.CompilerParams(collective_id=0, has_side_effects=True, vmem_limit_bytes=60 * 1024 * 1024),
    )(*ins.values())
    output, input_grad, gq, gog, gup, gdg, small = res
    if not use_x:
        gq, gog, gup, gdg, small = lax.psum((gq, gog, gup, gdg, small), "grp")
    return (output, input_grad, small[0], small[1], gq, gog[:, :128], gog[:, 128:], small[4], small[2],
            small[3], gup, small[8:12].reshape(512), gdg[:, :128], small[5], gdg[:, 128:], small[6])


def solution(mesh):
    act = P(("grp", "row"), "col")
    col, row = P("col"), P("row")
    cr, rc = P("col", "row"), P("row", "col")
    return jax.shard_map(
        partial(body, mesh.shape["grp"] == 2),
        mesh=mesh,
        in_specs=(act, act, col, col, cr, rc, rc, col, col, col, cr, row, rc, col, rc, col),
        out_specs=(act, act, col, col, cr, rc, rc, col, col, col, cr, row, rc, col, rc, col),
        check_vma=False,
    )
```

```python
from functools import partial

import jax
import jax.numpy as jnp
from jax import lax
from jax.experimental import pallas as pl
from jax.experimental.pallas import tpu as pltpu
from jax.sharding import PartitionSpec as P

bf16 = jnp.bfloat16
f32 = jnp.float32
EPS = 1e-05
MASKED = -1e30
MESH = pl.DeviceIdType.MESH

T = 512
D = 512
BLOCK = {"qkv": (128, 384), "og": (128, 256), "up": (128, 512), "d0": (256, 256), "d1": (256, 256)}
NAMES = ("qkv", "og", "up", "d0", "d1")
VECTORS = ("norm1_gain", "norm1_bias", "gate1_bias", "norm2_gain", "norm2_bias", "down_bias", "gate2_bias")


def dot(a, b, ca, cb):
    return lax.dot_general(a, b, (((ca,), (cb,)), ((), ())), preferred_element_type=f32)


def loop(count, step):
    lax.fori_loop(0, count, lambda i, z: (step(i), z)[1], 0)


def cat(parts, axis=1):
    return jnp.concatenate(parts, axis=axis)


class Waiter:
    def __init__(self, make):
        self.make = make

    def wait_recv(self):
        self.make().wait_recv()

    def wait_send(self):
        self.make().wait_send()


def sigmoid(v):
    return 1.0 / (1.0 + jnp.exp(-v))


def kernel(use_x, names_in, names_out, names_scr, *refs):
    ref = dict(zip(names_in + names_out + names_scr, refs))
    R = type("R", (), ref)
    a = lax.axis_index("grp")
    r = lax.axis_index("row")
    c = lax.axis_index("col")
    y, k = r // 2, r % 2
    ah = a % 2
    q = 2 * (c % 2) + k
    y_, k_, a_ = 1 - y, 1 - k, 1 - ah
    others = [lax.rem(c + i, 4) for i in range(1, 4)]
    core = (a, 2 * y + 1 - k, c)
    yside = (a, 2 * (1 - y) + k, c)
    xside = (a + 1 - 2 * ah, r, c)
    zside = (a, r, c + 1 - 2 * (c % 2))
    owner_row = 2 * y + c // 2
    lo_row = pl.multiple_of(q * 128, 128)
    hi_row = pl.multiple_of((7 - q) * 128, 128)

    counter = [0]
    pending = []

    def send(src, dst, dev):
        i = counter[0]
        counter[0] += 1

        def make():
            return pltpu.make_async_remote_copy(
                src_ref=src() if callable(src) else src, dst_ref=dst() if callable(dst) else dst,
                send_sem=R.ssem.at[i], recv_sem=R.rsem.at[i], device_id=dev, device_id_type=MESH)
        make().start()
        pending.append(Waiter(make))
        return pending[-1]

    local = []

    def fetch(src, dst):
        cp = pltpu.make_async_copy(src, dst, R.lsem.at[len(local)])
        cp.start()
        local.append(cp)

    fetch(R.i_qkv, R.qstage)
    for t in range(2):
        for name, sources, skip in (("og", ("out", "gate1"), 0), ("up", ("up",), 0),
                                    ("d0", ("down", "gate2"), 0), ("d1", ("down", "gate2"), 256)):
            rows, cols = BLOCK[name]
            rq = rows // 4
            w = getattr(R, "w_" + name)
            width = cols // len(sources)
            for j, s in enumerate(sources):
                at = pl.multiple_of((2 * t + ah) * rq + skip, 32)
                fetch(getattr(R, "i_" + s).at[pl.ds(at, rq), :],
                      w.at[y, k, c, t, ah, :, pl.ds(j * width, width)])

    barrier = pltpu.get_barrier_semaphore()
    for kk in range(2):
        for cc in range(4):
            me = (k == kk) & (c == cc)

            @pl.when(jnp.logical_not(me))
            def _():
                pl.semaphore_signal(barrier, inc=1, device_id=(a, 2 * y + kk, cc), device_id_type=MESH)
    diag = (a, 2 * (1 - y) + 1 - k, c)
    corners = [(g, rr, c) for g in ((a, a + 1 - 2 * ah) if use_x else (a,))
               for rr in (r, 2 * y + 1 - k, 2 * (1 - y) + k, 2 * (1 - y) + 1 - k)][1:]
    for dev in (corners[1:] if use_x else corners[1:] + [xside]):
        pl.semaphore_signal(barrier, inc=1, device_id=dev, device_id_type=MESH)

    local[0].wait()
    for t in range(2):
        blk = R.qstage[pl.ds(pl.multiple_of((2 * t + ah) * 32, 32), 32), :].astype(f32)
        parts = [blk[:, (3 * h + j) * 64:(3 * h + j + 1) * 64] for j in range(3) for h in range(2)]
        R.w_qkv[y, k, c, t, ah] = cat(parts).astype(bf16)
    R.vec[...] = jnp.zeros((16, 128), f32)
    for i, name in enumerate(VECTORS):
        R.vec[i:i + 1, :] = getattr(R, name)[...].astype(f32).reshape(1, 128)
    for i in range(4):
        R.vec[8 + i:9 + i, :] = R.up_bias[128 * i:128 * i + 128].astype(f32).reshape(1, 128)
    pl.semaphore_wait(barrier, 13 if use_x else 10)

    def rows_in(src, dst, which):
        sends = []
        for qq in range(4):
            kq, cq = qq % 2, 2 * k + qq // 2
            me = (k == kq) & (c == cq)
            for j, (s0, d0, n) in enumerate(((qq * 128, 0, 128), ((7 - qq) * 128, 128, 128), ((8 + 2 * qq) * 128, 256, 256))):
                s = src.at[pl.ds(s0, n), :]
                d = dst.at[c, pl.ds(d0, n), :]
                rs = R.irsem.at[which, c, j]
                cp = pltpu.make_async_remote_copy(
                    src_ref=s, dst_ref=d, send_sem=R.issem.at[which, qq, j], recv_sem=rs,
                    device_id=(a, 2 * y + kq, cq), device_id_type=MESH)
                sends.append((me, cp))

                @pl.when(jnp.logical_not(me))
                def _():
                    cp.start()

                @pl.when(me)
                def _():
                    pltpu.make_async_copy(s, d, rs).start()

        def wait():
            for cc in range(4):
                for j, (d0, n) in enumerate(((0, 128), (128, 128), (256, 256))):
                    d = dst.at[cc, pl.ds(d0, n), :]
                    pltpu.make_async_copy(d, d, R.irsem.at[which, cc, j]).wait()
        return sends, wait

    def rows_out(src, dst, which):
        sends = []
        for cc in range(4):
            me = (c // 2 == k) & (c == cc)
            for j, (s0, d0, n) in enumerate(((0, lo_row, 128), (128, hi_row, 128), (256, 1024 + pl.multiple_of(q * 256, 256), 256))):
                s = src.at[cc, pl.ds(s0, n), :]
                d = dst.at[pl.ds(d0, n), :]
                rs = R.irsem.at[which, q, j]
                cp = pltpu.make_async_remote_copy(
                    src_ref=s, dst_ref=d, send_sem=R.issem.at[which, cc, j], recv_sem=rs,
                    device_id=(a, owner_row, cc), device_id_type=MESH)
                sends.append((me, cp))

                @pl.when(jnp.logical_not(me))
                def _():
                    cp.start()

                @pl.when(me)
                def _():
                    pltpu.make_async_copy(s, d, rs).start()

        def wait():
            for qq in range(4):
                for j, (d0, n) in enumerate(((qq * 128, 128), ((7 - qq) * 128, 128), ((8 + 2 * qq) * 128, 256))):
                    d = dst.at[pl.ds(d0, n), :]
                    pltpu.make_async_copy(d, d, R.irsem.at[which, qq, j]).wait()
        return sends, wait

    def finish_sends(sends):
        for me, cp in sends:
            @pl.when(jnp.logical_not(me))
            def _():
                cp.wait_send()

    wst = {}

    def w_z(name):
        w = getattr(R, "w_" + name)
        here = lambda: w.at[y, k, c, :, ah]
        wst[name, "z"] = [send(here, here, (a, r, cc)) for cc in others]

    def to_sibling(name, s):
        wst.setdefault((name, "core"), []).append(send(s, s, core))

    def w_1(name):
        w = getattr(R, "w_" + name)
        for cp in wst[name, "z"]:
            cp.wait_recv()
        s = lambda: w.at[y, k, :, 0, ah]
        wst[name, "x1"] = send(s, s, xside)
        s = lambda: w.at[y, k, :, 1, ah]
        wst[name, "y1"] = send(s, s, yside)
        to_sibling(name, lambda: w.at[y, k, :, :, ah])

    def w_2(name):
        w = getattr(R, "w_" + name)
        wst[name, "x1"].wait_recv()
        s = lambda: w.at[y, k, :, 0]
        wst[name, "y2"] = send(s, s, yside)
        to_sibling(name, lambda: w.at[y, k, :, 0, a_])
        wst[name, "y1"].wait_recv()
        s = lambda: w.at[:, k, :, 1, ah]
        wst[name, "x2"] = send(s, s, xside)
        to_sibling(name, lambda: w.at[y_, k, :, 1, ah])

    def w_3(name):
        w = getattr(R, "w_" + name)
        wst[name, "y2"].wait_recv()
        to_sibling(name, lambda: w.at[y_, k, :, 0])
        wst[name, "x2"].wait_recv()
        to_sibling(name, lambda: w.at[:, k, :, 1, a_])

    def w_4(name):
        for cp in wst[name, "core"]:
            cp.wait_recv()

    gst = {}

    def g_0(name):
        g, b0 = getattr(R, "g_" + name), getattr(R, "b0_" + name)
        gst[name, "core"] = send(lambda: g.at[:, k_], b0, core)

    def g_1(name):
        g, b0, b1 = getattr(R, "g_" + name), getattr(R, "b0_" + name), getattr(R, "b1_" + name)
        if name != "qkv":
            gst[name, "core"].wait_recv()

        def one(i):
            yy, cc = i // 4, i % 4
            b0[yy, cc] = (b0[yy, cc].astype(f32) + g[yy, k, cc].astype(f32)).astype(bf16)
        loop(8, one)
        if use_x:
            b2 = getattr(R, "b2_" + name)
            gst[name, "y1"] = send(lambda: b0.at[y_, :, 0], b1, yside)
            gst[name, "x1"] = send(lambda: b0.at[:, :, 1, a_], b2, xside)
        else:
            gst[name, "y1"] = send(lambda: b0.at[y_], b1, yside)

    def g_2(name):
        b0, b1 = getattr(R, "b0_" + name), getattr(R, "b1_" + name)
        gst[name, "y1"].wait_recv()
        if not use_x:
            def one(cc):
                b1[cc] = (b1[cc].astype(f32) + b0[y, cc].astype(f32)).astype(bf16)
            loop(4, one)
            return
        b2, b3, b4 = (getattr(R, "b%d_%s" % (i, name)) for i in (2, 3, 4))

        def one(cc):
            b1[cc] = (b1[cc].astype(f32) + b0[y, cc, 0].astype(f32)).astype(bf16)
        loop(4, one)
        gst[name, "x2"] = send(lambda: b1.at[:, a_], b3, xside)
        gst[name, "x1"].wait_recv()

        def two(i):
            yy, cc = i // 4, i % 4
            b2[yy, cc] = (b2[yy, cc].astype(f32) + b0[yy, cc, 1, ah].astype(f32)).astype(bf16)
        loop(8, two)
        gst[name, "y2"] = send(lambda: b2.at[y_], b4, yside)

    def g_3(name):
        b1, z, b5 = (getattr(R, "%s_%s" % (i, name)) for i in ("b1", "z" if use_x else "b1", "b5"))
        if use_x:
            b2, b3, b4 = (getattr(R, "b%d_%s" % (i, name)) for i in (2, 3, 4))
            gst[name, "x2"].wait_recv()
            gst[name, "y2"].wait_recv()

            def one(cc):
                z[cc, 0] = (b1[cc, ah].astype(f32) + b3[cc].astype(f32)).astype(bf16)
                z[cc, 1] = (b2[y, cc].astype(f32) + b4[cc].astype(f32)).astype(bf16)
            loop(4, one)
        gst[name, "z"] = [send(lambda cc=cc: z.at[cc], lambda i=i: b5.at[i], (a, r, cc)) for i, cc in enumerate(others)]

    def g_4(name):
        z, b5, fin = (getattr(R, "%s_%s" % (i, name)) for i in ("z" if use_x else "b1", "b5", "fin"))
        for cp in gst[name, "z"]:
            cp.wait_recv()
        if use_x:
            for t in range(2):
                total = z[c, t].astype(f32)
                for i in range(3):
                    total = total + b5[i, t].astype(f32)
                fin[t, ah] = total.astype(bf16)
            s = lambda: fin.at[:, ah]
            gst[name, "x3"] = send(s, s, xside)
        else:
            for t in range(2):
                for i2 in range(2):
                    total = z[c, t, i2].astype(f32)
                    for i in range(3):
                        total = total + b5[i, t, i2].astype(f32)
                    fin[t, i2] = total.astype(bf16)

    def g_5(name):
        if use_x:
            gst[name, "x3"].wait_recv()
        rows, cols = BLOCK[name]
        getattr(R, name + "_o")[...] = getattr(R, "fin_" + name)[...].reshape(rows, cols)

    def weight(name, rr):
        w = getattr(R, "w_" + name)
        return w[rr // 2, rr % 2].reshape(4 * BLOCK[name][0], BLOCK[name][1])

    R.vecs[c] = R.vec[...]
    R.vecr[r] = R.vec[...]
    vec_cp = [send(R.vec, R.vecs.at[c], (a, r, (c + i) % 4)) for i in range(1, 4)]
    vec_cp += [send(R.vec, R.vecr.at[r], dev) for dev in (core, yside, diag)]
    w_z("qkv")
    for cp in local[1:]:
        cp.wait()
    w_z("og")
    w_z("up")
    tok_sends, tok_wait = rows_in(R.tok, R.xo, 0)
    w_z("d0")
    w_1("qkv")
    w_1("og")
    w_2("qkv")
    w_1("up")
    w_2("og")
    w_3("qkv")
    w_2("up")
    w_3("og")
    for cp in vec_cp:
        cp.wait_recv()

    def vec_row(i):
        return cat([R.vecs[cc, i:i + 1, :] for cc in range(4)])

    tok_wait()

    def xrows():
        return cat([R.xo[cc] for cc in range(4)]).astype(f32)

    def norm_parts(v):
        mean = jnp.sum(v, axis=1, keepdims=True) * (1.0 / D)
        cen = v - mean
        var = jnp.sum(cen * cen, axis=1, keepdims=True) * (1.0 / D)
        inv = lax.rsqrt(var + EPS)
        return cen * inv, inv

    standard, _ = norm_parts(xrows())
    n1 = (standard * vec_row(0) + vec_row(1)).astype(bf16)
    R.n1[...] = n1
    R.xn[pl.ds(lo_row, 128), :] = n1[0:128]
    R.xn[pl.ds(hi_row, 128), :] = n1[128:256]
    R.xn[1024:1280, :] = n1[256:512]
    here = [R.xn.at[pl.ds(lo_row, 128), :], R.xn.at[pl.ds(hi_row, 128), :]]
    to_z = [send(s, s, zside) for s in here]
    to_core = [send(s, s, core) for s in here]
    w_z("d1")
    cot_sends, cot_wait = rows_in(R.cot, R.co, 1)
    w_3("up")
    w_1("d0")
    w_4("qkv")
    w_2("d0")
    qz = q + 2 - 4 * (q // 2)
    for cp in to_z:
        cp.wait_recv()
    there = [R.xn.at[pl.ds(pl.multiple_of(qz * 128, 128), 128), :],
             R.xn.at[pl.ds(pl.multiple_of((7 - qz) * 128, 128), 128), :]]
    to_core += [send(s, s, core) for s in there]
    for cp in to_core:
        cp.wait_recv()

    def qkv_pair(p):
        w = weight("qkv", p)
        R.qp[p] = (dot(R.n1[...], w[:, 0:128], 1, 0).astype(bf16).astype(f32) * 0.125).astype(bf16)
        R.kv[p] = dot(R.xn[...], w[:, 128:384], 1, 0).astype(bf16)
    loop(4, qkv_pair)
    w_1("d1")

    lane = lax.broadcasted_iota(jnp.int32, (T, 128), 1)
    key_at = lax.broadcasted_iota(jnp.int32, (512, 128), 0)
    col_at = lax.broadcasted_iota(jnp.int32, (512, 128), 1)
    lo_ok = key_at <= col_at + q * 128
    hi_ok = key_at + 512 <= col_at + (7 - q) * 128
    own_ok = (key_at <= col_at)[0:128]

    def attend_pair(p):
        for h in range(2):
            keys = R.kv[p, :, 0:128]
            vals = R.kv[p, :, 128:256]
            qm = jnp.where(lane // 64 == h, R.qp[p], jnp.zeros((), bf16))
            s1 = dot(keys[0:512], qm, 1, 1)
            s2 = dot(keys[512:1024], qm[128:512], 1, 1)
            sa = jnp.where(own_ok, dot(keys[1024:1152], qm[256:384], 1, 1), MASKED)
            sb = jnp.where(own_ok, dot(keys[1152:1280], qm[384:512], 1, 1), MASKED)
            s1 = cat([jnp.where(lo_ok, s1[:, 0:128], MASKED), s1[:, 128:512]])
            s2 = cat([jnp.where(hi_ok, s2[:, 0:128], MASKED), s2[:, 128:384]])
            top = lambda v: jnp.max(v, axis=0, keepdims=True)
            add = lambda v: jnp.sum(v, axis=0, keepdims=True)
            m1 = top(s1)
            m2 = jnp.maximum(m1[:, 128:512], top(s2))
            m = cat([m1[:, 0:128], m2[:, 0:128], jnp.maximum(m2[:, 128:384], cat([top(sa), top(sb)]))])
            e1 = jnp.exp(s1 - m)
            e2 = jnp.exp(s2 - m[:, 128:512])
            ea = jnp.exp(sa - m[:, 256:384])
            eb = jnp.exp(sb - m[:, 384:512])
            l1 = add(e1)
            l2 = l1[:, 128:512] + add(e2)
            total = cat([l1[:, 0:128], l2[:, 0:128], l2[:, 128:384] + cat([add(ea), add(eb)])])
            e1, e2, ea, eb = (v.astype(bf16) for v in (e1, e2, ea, eb))
            R.p1[2 * p + h] = e1
            R.p2[2 * p + h] = e2
            R.po[2 * p + h, :, 0:128] = ea
            R.po[2 * p + h, :, 128:256] = eb
            o1 = dot(vals[0:512], e1, 0, 0)
            o2 = dot(vals[512:1024], e2, 0, 0)
            oa = dot(vals[1024:1152], ea, 0, 0)
            ob = dot(vals[1152:1280], eb, 0, 0)
            o2 = o1[:, 128:512] + o2
            o = cat([o1[:, 0:128], o2[:, 0:128], o2[:, 128:384] + cat([oa, ob])])
            inv = 1.0 / total
            R.li[p, h:h + 1, :] = inv
            R.att[p, 64 * h:64 * h + 64, :] = (o[64 * h:64 * h + 64] * inv).astype(bf16)
    def attend_step(p):
        attend_pair(p)

        @pl.when(p == 0)
        def _():
            w_3("d0")

        @pl.when(p == 1)
        def _():
            w_2("d1")
    loop(4, attend_step)
    w_4("og")

    def lanes(cc):
        return pl.ds(pl.multiple_of(cc * 128, 128), 128)

    def wide(cc):
        return pl.ds(pl.multiple_of(cc * 256, 256), 256)

    def out_block(cc):
        w = R.w_og[:, :, cc].reshape(512, 256)
        br = dot(R.att[...].reshape(512, T), w, 0, 0)
        ao = br[:, 0:128]
        gate = sigmoid(br[:, 128:256] + R.vecs[cc, 2:3, :])
        R.ao[cc] = ao
        R.g1[cc] = gate
        R.mid[cc] = R.xo[cc].astype(f32) + gate * ao
    loop(4, out_block)

    def midrows():
        return cat([R.mid[cc] for cc in range(4)])

    standard, _ = norm_parts(midrows())
    R.n2[...] = (standard * vec_row(3) + vec_row(4)).astype(bf16)
    w_4("up")

    def up_block(rr):
        pre = dot(R.n2[...], weight("up", rr), 1, 0) + cat([R.vecr[rr, 8 + i:9 + i, :] for i in range(4)])
        s = sigmoid(pre)
        R.hid[rr] = (pre * s).astype(bf16)
        R.slp[rr] = (s * (1.0 + pre * (1.0 - s))).astype(bf16)
    loop(4, up_block)
    w_3("d1")
    w_4("d0")
    w_4("d1")
    cot_wait()

    def down_block(cc):
        br = 0.0
        for rr in range(4):
            for j in range(2):
                w = getattr(R, "w_d%d" % j)[rr // 2, rr % 2, cc].reshape(256, 256)
                br = br + dot(R.hid[rr, :, 256 * j:256 * j + 256], w, 1, 0)
        ffn = br[:, 0:128] + R.vecs[cc, 5:6, :]
        gate = sigmoid(br[:, 128:256] + R.vecs[cc, 6:7, :])
        R.out[cc] = (R.mid[cc] + gate * ffn).astype(bf16)
        g = R.co[cc].astype(f32)
        gf = (g * gate).astype(bf16)
        gg = (g * ffn * gate * (1.0 - gate)).astype(bf16)
        R.pair[:, wide(cc)] = cat([gf, gg])
        R.sv[5, pl.ds(cc, 1), :] = jnp.sum(gf.astype(f32), axis=0, keepdims=True)
        R.sv[6, pl.ds(cc, 1), :] = jnp.sum(gg.astype(f32), axis=0, keepdims=True)
    loop(4, down_block)
    out_sends, out_wait = rows_out(R.out, R.out_o, 2)

    def grad_down(j, kk):
        for yy in range(2):
            g = dot(R.hid[2 * yy + kk, :, 256 * j:256 * j + 256], R.pair[...], 0, 0).astype(bf16)
            for cc in range(4):
                getattr(R, "g_d%d" % j)[yy, kk, cc] = g[:, 256 * cc:256 * cc + 256].reshape(2, 2, 64, 256)
    for j in range(2):
        grad_down(j, 1 - k)
        g_0("d%d" % j)
        grad_down(j, k)
    g_1("d0")

    def back_up(rr):
        gh = 0.0
        for cc in range(4):
            w = [getattr(R, "w_d%d" % j)[rr // 2, rr % 2, cc].reshape(256, 256) for j in range(2)]
            gh = gh + dot(R.pair[:, 256 * cc:256 * cc + 256], cat(w, 0), 1, 1)
        gp = (gh * R.slp[rr].astype(f32)).astype(bf16)
        R.slp[rr] = gp
        tot = jnp.sum(gp.astype(f32), axis=0, keepdims=True)
        for i in range(4):
            R.sv[8 + rr, i:i + 1, :] = tot[:, 128 * i:128 * i + 128]
    loop(4, back_up)
    g_1("d1")

    def grad_up(yy, kk):
        g = dot(R.n2[...], R.slp[2 * yy + kk], 0, 0).astype(bf16)
        R.g_up[yy, kk] = g.reshape(4, 2, 2, 32, 512)
    grad_up(0, 1 - k)
    grad_up(1, 1 - k)
    g_0("up")
    grad_up(0, k)
    grad_up(1, k)

    gn = dot(R.slp[0], weight("up", 0), 1, 1)
    for rr in range(1, 4):
        gn = gn + dot(R.slp[rr], weight("up", rr), 1, 1)
    g_1("up")

    def norm_back(v, grad, gain_row, at):
        std, inv = norm_parts(v)
        gs = jnp.sum(grad * std, axis=0, keepdims=True)
        gb = jnp.sum(grad, axis=0, keepdims=True)
        for cc in range(4):
            R.sv[at, cc:cc + 1, :] = gs[:, 128 * cc:128 * cc + 128]
            R.sv[at + 1, cc:cc + 1, :] = gb[:, 128 * cc:128 * cc + 128]
        s = grad * vec_row(gain_row)
        f = jnp.sum(s, axis=1, keepdims=True) * (1.0 / D)
        e = jnp.sum(s * std, axis=1, keepdims=True) * (1.0 / D)
        return inv * (s - f - std * e)

    gm = norm_back(midrows(), gn, 3, 2)
    for cc in range(4):
        g_mid = R.co[cc].astype(f32) + gm[:, 128 * cc:128 * cc + 128]
        R.gm[cc] = g_mid
        gate = R.g1[cc]
        ga = (g_mid * gate).astype(bf16)
        gg = (g_mid * R.ao[cc] * gate * (1.0 - gate)).astype(bf16)
        R.pair[:, 256 * cc:256 * cc + 256] = cat([ga, gg])
        R.sv[4, cc:cc + 1, :] = jnp.sum(gg.astype(f32), axis=0, keepdims=True)
    def grad_out(cc):
        R.g_og[:, :, cc] = dot(R.att[...].reshape(512, T), R.pair[:, wide(cc)], 1, 0).astype(bf16).reshape(2, 2, 2, 2, 32, 256)
    loop(4, grad_out)
    g_0("og")
    g_2("d0")
    do = 0.0
    for cc in range(4):
        do = do + dot(R.w_og[:, :, cc].reshape(512, 256), R.pair[:, 256 * cc:256 * cc + 256], 1, 1)
    for cc in range(4):
        R.mid[cc] = do[:, 128 * cc:128 * cc + 128]
    for i in range(2):
        R.hid[i] = R.xn[512 * i:512 * i + 512, :].T
    R.hid[2, :, 0:256] = R.xn[1024:1280, :].T
    R.hid[3] = R.n1[...].T
    g_1("og")
    g_2("d1")

    row_of = lax.broadcasted_iota(jnp.int32, (128, T), 0)

    def back_pair(p):
        rows = pl.ds(pl.multiple_of(p * 128, 128), 128)
        dot_t = cat([R.mid[cc, rows, :] for cc in range(4)])
        dot_t = dot_t * jnp.where(row_of < 64, R.li[p, 0:1, :], R.li[p, 1:2, :])
        prod = dot_t * R.att[p].astype(f32)
        dot_t = dot_t.astype(bf16)
        dot_n = dot_t.T
        keys = R.kv[p, :, 0:128]
        vals = R.kv[p, :, 128:256]
        grads = []
        queries = []
        for h in range(2):
            delta = jnp.sum(prod[64 * h:64 * h + 64], axis=0, keepdims=True)
            qm = jnp.where(lane // 64 == h, R.qp[p], jnp.zeros((), bf16))
            om = jnp.where(lane // 64 == h, dot_n, jnp.zeros((), bf16))
            omt = jnp.where(row_of // 64 == h, dot_t, jnp.zeros((), bf16))
            e1, e2 = R.p1[2 * p + h], R.p2[2 * p + h]
            ea, eb = R.po[2 * p + h, :, 0:128], R.po[2 * p + h, :, 128:256]
            d1 = (e1.astype(f32) * (dot(vals[0:512], omt, 1, 0) - delta)).astype(bf16)
            d2 = (e2.astype(f32) * (dot(vals[512:1024], omt[:, 128:512], 1, 0) - delta[:, 128:512])).astype(bf16)
            da = (ea.astype(f32) * (dot(vals[1024:1152], omt[:, 256:384], 1, 0) - delta[:, 256:384])).astype(bf16)
            db = (eb.astype(f32) * (dot(vals[1152:1280], omt[:, 384:512], 1, 0) - delta[:, 384:512])).astype(bf16)
            dk = cat([dot(d1, qm, 1, 0), dot(d2, qm[128:512], 1, 0), dot(da, qm[256:384], 1, 0), dot(db, qm[384:512], 1, 0)], 0)
            dv = cat([dot(e1, om, 1, 0), dot(e2, om[128:512], 1, 0), dot(ea, om[256:384], 1, 0), dot(eb, om[384:512], 1, 0)], 0)
            grads.append((dk, dv))
            x1 = dot(keys[0:512], d1, 0, 0)
            x2 = x1[:, 128:512] + dot(keys[512:1024], d2, 0, 0)
            xab = cat([dot(keys[1024:1152], da, 0, 0), dot(keys[1152:1280], db, 0, 0)])
            dq = cat([x1[:, 0:128], x2[:, 0:128], x2[:, 128:384] + xab])
            queries.append(dq[64 * h:64 * h + 64])
        R.kv[p, :, 0:128] = (grads[0][0] + grads[1][0]).astype(bf16)
        R.kv[p, :, 128:256] = (grads[0][1] + grads[1][1]).astype(bf16)
        R.qp[p] = (cat(queries, 0) * 0.125).astype(bf16).T
        gk = dot(R.hid[0], R.kv[p, 0:512, :], 1, 0) + dot(R.hid[1], R.kv[p, 512:1024, :], 1, 0)
        gk = gk + dot(R.hid[2, :, 0:256], R.kv[p, 1024:1280, :], 1, 0)
        g = cat([dot(R.hid[3], R.qp[p], 1, 0), gk]).astype(bf16)
        R.g_qkv[p // 2, p % 2] = g.reshape(4, 2, 2, 32, 384)

    def qkv_copy(yy):
        return pltpu.make_async_remote_copy(
            src_ref=R.g_qkv.at[yy, 1 - k], dst_ref=R.b0_qkv.at[yy], send_sem=R.qsem.at[0, yy], recv_sem=R.qsem.at[1, yy],
            device_id=core, device_id_type=MESH)

    def back_step(p):
        back_pair(p)

        @pl.when(p % 2 != k)
        def _():
            qkv_copy(p // 2).start()

        @pl.when(p == 0)
        def _():
            g_3("d0")

        @pl.when(p == 1)
        def _():
            g_2("up")
            g_3("d1")

        @pl.when(p == 2)
        def _():
            g_4("d0")
            g_2("og")
            g_3("up")
    loop(4, back_step)

    def back_rows(first, count):
        rows = pl.ds(first, count)
        total = dot(R.kv[0, rows, :], weight("qkv", 0)[:, 128:384], 1, 1)
        for p in range(1, 4):
            total = total + dot(R.kv[p, rows, :], weight("qkv", p)[:, 128:384], 1, 1)
        return total

    def chunk_rows(qq):
        return (pl.multiple_of(qq * 128, 128), pl.multiple_of((7 - qq) * 128, 128))

    q1 = q + 1 - 2 * k
    q2 = qz
    q3 = q2 + 1 - 2 * k
    for i, row in enumerate(chunk_rows(q1)):
        R.ex[0, 128 * i:128 * i + 128, :] = back_rows(row, 128).astype(bf16)
    for i, row in enumerate(chunk_rows(q3)):
        R.ex[1, 128 * i:128 * i + 128, :] = back_rows(row, 128).astype(bf16)
    part_core = send(R.ex, R.exr, core)
    for yy in range(2):
        qkv_copy(yy).wait_recv()
    g_1("qkv")
    mine2 = [back_rows(row, 128) for row in chunk_rows(q2)]
    part_core.wait_recv()
    for i in range(2):
        R.ez[128 * i:128 * i + 128, :] = (mine2[i] + R.exr[1, 128 * i:128 * i + 128, :].astype(f32)).astype(bf16)
    part_z = send(R.ez, R.ezr, zside)
    g_3("og")
    g_4("d1")
    for row, n, at in ((lo_row, 128, 0), (hi_row, 128, 128), (1024, 256, 256)):
        own = back_rows(row, n)
        for cc in range(4):
            R.mid[cc, at:at + n, :] = own[:, 128 * cc:128 * cc + 128]

    def add_queries(p):
        more = dot(R.qp[p], weight("qkv", p)[:, 0:128], 1, 1)
        for cc in range(4):
            R.mid[cc] = R.mid[cc] + more[:, 128 * cc:128 * cc + 128]
    loop(4, add_queries)
    g_4("up")
    part_z.wait_recv()
    for cc in range(4):
        here = slice(128 * cc, 128 * cc + 128)
        R.mid[cc, 0:256, :] = R.mid[cc, 0:256, :] + (R.exr[0, :, here].astype(f32) + R.ezr[:, here].astype(f32))
    gx = norm_back(xrows(), midrows(), 0, 0)
    R.sva[c] = R.sv[...]
    sv_z = [send(R.sv, R.sva.at[c], (a, r, (c + i) % 4)) for i in range(1, 4)]
    for cc in range(4):
        R.ing[cc] = (R.gm[cc] + gx[:, 128 * cc:128 * cc + 128]).astype(bf16)
    g_2("qkv")
    g_4("og")
    ing_sends, ing_wait = rows_out(R.ing, R.ing_o, 3)

    for cp in sv_z:
        cp.wait_recv()
    R.sv2[...] = (R.sva[0] + R.sva[1]) + (R.sva[2] + R.sva[3])
    slot = 4 * ah + r if use_x else r
    R.svr[slot] = R.sv2[...]
    sv_all = [send(R.sv2, R.svr.at[slot], dev) for dev in corners]
    g_3("qkv")
    for name in ("d0", "d1", "up", "og"):
        g_5(name)
    for cp in sv_all:
        cp.wait_recv()
    total = R.svr[0]
    for i in range(1, 8 if use_x else 4):
        total = total + R.svr[i]
    R.sv2t[...] = total
    R.small_o[...] = jnp.zeros((16, 128), f32)
    for i in range(7):
        R.small_o[i:i + 1, :] = R.sv2t[i, pl.ds(c, 1), :]
    for i in range(4):
        R.small_o[8 + i:9 + i, :] = R.sv2t[8 + r, i:i + 1, :]
    g_4("qkv")
    g_5("qkv")

    out_wait()
    ing_wait()
    for yy in range(2):
        qkv_copy(yy).wait_send()
    for cp in pending:
        cp.wait_send()
    for sends in (tok_sends, cot_sends, out_sends, ing_sends):
        finish_sends(sends)


def body(use_x, tokens, cotangent, norm1_gain, norm1_bias, qkv_weight, out_weight, gate1_weight,
         gate1_bias, norm2_gain, norm2_bias, up_weight, up_bias, down_weight, down_bias,
         gate2_weight, gate2_bias):
    hbm = pl.BlockSpec(memory_space=pl.ANY)
    vmem = pl.BlockSpec(memory_space=pltpu.VMEM)
    ins = {"tok": tokens, "cot": cotangent, "i_qkv": qkv_weight, "i_out": out_weight, "i_gate1": gate1_weight,
           "i_up": up_weight, "i_down": down_weight, "i_gate2": gate2_weight,
           "norm1_gain": norm1_gain, "norm1_bias": norm1_bias, "gate1_bias": gate1_bias, "norm2_gain": norm2_gain,
           "norm2_bias": norm2_bias, "down_bias": down_bias, "gate2_bias": gate2_bias, "up_bias": up_bias}
    outs = {"out_o": ((2048, 128), bf16, hbm), "ing_o": ((2048, 128), bf16, hbm)}
    for name in NAMES:
        outs[name + "_o"] = (BLOCK[name], bf16, vmem)
    outs["small_o"] = ((16, 128), f32, vmem)
    scr = {}
    for name in NAMES:
        rows, cols = BLOCK[name]
        rq = rows // 4
        scr["w_" + name] = ((2, 2, 4, 2, 2, rq, cols), bf16)
        scr["g_" + name] = ((2, 2, 4, 2, 2, rq, cols), bf16)
        scr["b0_" + name] = ((2, 4, 2, 2, rq, cols), bf16)
        if use_x:
            scr["b1_" + name] = ((4, 2, rq, cols), bf16)
            scr["b2_" + name] = ((2, 4, rq, cols), bf16)
            scr["b3_" + name] = ((4, rq, cols), bf16)
            scr["b4_" + name] = ((4, rq, cols), bf16)
            scr["z_" + name] = ((4, 2, rq, cols), bf16)
            scr["b5_" + name] = ((3, 2, rq, cols), bf16)
        else:
            scr["b1_" + name] = ((4, 2, 2, rq, cols), bf16)
            scr["b5_" + name] = ((3, 2, 2, rq, cols), bf16)
        scr["fin_" + name] = ((2, 2, rq, cols), bf16)
    scr.update({
        "qstage": ((128, 384), bf16), "vec": ((16, 128), f32), "vecs": ((4, 16, 128), f32), "vecr": ((4, 16, 128), f32),
        "xo": ((4, T, 128), bf16), "co": ((4, T, 128), bf16), "n1": ((T, D), bf16),
        "xn": ((1280, D), bf16), "qp": ((4, T, 128), bf16), "kv": ((4, 1280, 256), bf16),
        "p1": ((8, 512, 512), bf16), "p2": ((8, 512, 384), bf16), "po": ((8, 128, 256), bf16),
        "li": ((4, 8, T), f32), "att": ((4, 128, T), bf16), "ao": ((4, T, 128), f32),
        "g1": ((4, T, 128), f32), "mid": ((4, T, 128), f32), "n2": ((T, D), bf16),
        "hid": ((4, T, 512), bf16), "slp": ((4, T, 512), bf16), "out": ((4, T, 128), bf16),
        "pair": ((T, 1024), bf16), "gm": ((4, T, 128), f32), "ing": ((4, T, 128), bf16),
        "ex": ((2, 256, D), bf16), "exr": ((2, 256, D), bf16), "ez": ((256, D), bf16), "ezr": ((256, D), bf16),
        "sv": ((12, 8, 128), f32), "sva": ((4, 12, 8, 128), f32), "sv2": ((12, 8, 128), f32),
        "sv2t": ((12, 8, 128), f32), "svr": ((8, 12, 8, 128), f32),
    })
    shapes = [pltpu.VMEM(s, d) for s, d in scr.values()]
    names_scr = tuple(scr) + ("ssem", "rsem", "issem", "irsem", "lsem", "qsem")
    n_sem = 160
    dma = pltpu.SemaphoreType.DMA
    shapes += [dma((n_sem,)), dma((n_sem,)), dma((4, 4, 3)), dma((4, 4, 3)), dma((20,)), dma((2, 2))]
    res = pl.pallas_call(
        partial(kernel, use_x, tuple(ins), tuple(outs), names_scr),
        out_shape=[jax.ShapeDtypeStruct(s, d) for s, d, _ in outs.values()],
        in_specs=[hbm] * 8 + [vmem] * 8,
        out_specs=[sp for _, _, sp in outs.values()],
        scratch_shapes=shapes,
        compiler_params=pltpu.CompilerParams(collective_id=0, has_side_effects=True, vmem_limit_bytes=60 * 1024 * 1024),
    )(*ins.values())
    if not use_x:
        summed = lax.psum(tuple(v.astype(f32) for v in res[2:]), "grp")
        res = list(res[:2]) + list(summed)
    flat = {"out": (2048, 128), "ing": (2048, 128), "n1g": (128,), "n1b": (128,), "qkv": (128, 384),
            "w_out": (128, 128), "w_gate1": (128, 128), "g1b": (128,), "n2g": (128,), "n2b": (128,),
            "up": (128, 512), "upb": (512,), "w_down": (512, 128), "db": (128,), "w_gate2": (512, 128), "g2b": (128,)}
    kinds = {name: bf16 if name in ("out", "ing") else f32 for name in flat}
    return pl.pallas_call(
        finish,
        out_shape=[jax.ShapeDtypeStruct(shape, kinds[name]) for name, shape in flat.items()],
        in_specs=[vmem] * 8,
        out_specs=[vmem] * 16,
    )(*res)


def finish(out_i, ing_i, qkv_i, og_i, up_i, d0_i, d1_i, small_i, out, ing, n1g, n1b, qkv, w_out, w_gate1, g1b, n2g, n2b,
           up, upb, w_down, db, w_gate2, g2b):
    out[...] = out_i[...]
    ing[...] = ing_i[...]
    g = qkv_i[...].astype(f32)
    qkv[...] = cat([g[:, (2 * j + h) * 64:(2 * j + h + 1) * 64] for h in range(2) for j in range(3)])
    w_out[...] = og_i[:, 0:128].astype(f32)
    w_gate1[...] = og_i[:, 128:256].astype(f32)
    up[...] = up_i[...].astype(f32)
    w_down[0:256, :] = d0_i[:, 0:128].astype(f32)
    w_down[256:512, :] = d1_i[:, 0:128].astype(f32)
    w_gate2[0:256, :] = d0_i[:, 128:256].astype(f32)
    w_gate2[256:512, :] = d1_i[:, 128:256].astype(f32)
    for i, ref in enumerate((n1g, n1b, n2g, n2b, g1b, db, g2b)):
        ref[...] = small_i[i:i + 1, :].reshape(128)
    for i in range(4):
        upb[128 * i:128 * i + 128] = small_i[8 + i:9 + i, :].reshape(128)


def solution(mesh):
    act = P(("grp", "row"), "col")
    col, row = P("col"), P("row")
    cr, rc = P("col", "row"), P("row", "col")
    return jax.shard_map(
        partial(body, mesh.shape["grp"] == 2),
        mesh=mesh,
        in_specs=(act, act, col, col, cr, rc, rc, col, col, col, cr, row, rc, col, rc, col),
        out_specs=(act, act, col, col, cr, rc, rc, col, col, col, cr, row, rc, col, rc, col),
        check_vma=False,
    )
```

```python
from functools import partial

import jax
import jax.numpy as jnp
from jax import lax
from jax.experimental import pallas as pl
from jax.experimental.pallas import tpu as pltpu
from jax.sharding import PartitionSpec as P

bf16 = jnp.bfloat16
f32 = jnp.float32
EPS = 1e-05
MASKED = -1e30
MESH = pl.DeviceIdType.MESH

T = 512
D = 512
BLOCK = {"qkv": (128, 384), "og": (128, 256), "up": (128, 512), "d0": (256, 256), "d1": (256, 256)}
NAMES = ("qkv", "og", "up", "d0", "d1")
VECTORS = ("norm1_gain", "norm1_bias", "gate1_bias", "norm2_gain", "norm2_bias", "down_bias", "gate2_bias")


def dot(a, b, ca, cb):
    return lax.dot_general(a, b, (((ca,), (cb,)), ((), ())), preferred_element_type=f32)


def loop(count, step):
    lax.fori_loop(0, count, lambda i, z: (step(i), z)[1], 0)


def cat(parts, axis=1):
    return jnp.concatenate(parts, axis=axis)


class Waiter:
    def __init__(self, make):
        self.make = make

    def wait_recv(self):
        self.make().wait_recv()

    def wait_send(self):
        self.make().wait_send()


def sigmoid(v):
    return 1.0 / (1.0 + jnp.exp(-v))


def kernel(use_x, names_in, names_out, names_scr, *refs):
    ref = dict(zip(names_in + names_out + names_scr, refs))
    R = type("R", (), ref)
    a = lax.axis_index("grp")
    r = lax.axis_index("row")
    c = lax.axis_index("col")
    y, k = r // 2, r % 2
    ah = a % 2
    q = 2 * (c % 2) + k
    y_, k_, a_ = 1 - y, 1 - k, 1 - ah
    c_far = lax.rem(c + 2, 4)
    c_near = c + 1 - 2 * (c % 2)
    c_across = lax.rem(c_near + 2, 4)
    others = [lax.rem(c + i, 4) for i in range(1, 4)]
    core = (a, 2 * y + 1 - k, c)
    yside = (a, 2 * (1 - y) + k, c)
    xside = (a + 1 - 2 * ah, r, c)
    zside = (a, r, c + 1 - 2 * (c % 2))
    owner_row = 2 * y + c // 2
    lo_row = pl.multiple_of(q * 128, 128)
    hi_row = pl.multiple_of((7 - q) * 128, 128)

    counter = [0]
    pending = []

    def send(src, dst, dev):
        i = counter[0]
        counter[0] += 1

        def make():
            return pltpu.make_async_remote_copy(
                src_ref=src() if callable(src) else src, dst_ref=dst() if callable(dst) else dst,
                send_sem=R.ssem.at[i], recv_sem=R.rsem.at[i], device_id=dev, device_id_type=MESH)
        make().start()
        pending.append(Waiter(make))
        return pending[-1]

    local = []

    def fetch(src, dst):
        cp = pltpu.make_async_copy(src, dst, R.lsem.at[len(local)])
        cp.start()
        local.append(cp)

    fetch(R.i_qkv, R.qstage)
    for t in range(2):
        for name, sources, skip in (("og", ("out", "gate1"), 0), ("up", ("up",), 0),
                                    ("d0", ("down", "gate2"), 0), ("d1", ("down", "gate2"), 256)):
            rows, cols = BLOCK[name]
            rq = rows // 4
            w = getattr(R, "w_" + name)
            width = cols // len(sources)
            for j, s in enumerate(sources):
                at = pl.multiple_of((2 * t + ah) * rq + skip, 32)
                fetch(getattr(R, "i_" + s).at[pl.ds(at, rq), :],
                      w.at[y, k, c, t, ah, :, pl.ds(j * width, width)])

    barrier = pltpu.get_barrier_semaphore()
    for kk in range(2):
        for cc in range(4):
            me = (k == kk) & (c == cc)

            @pl.when(jnp.logical_not(me))
            def _():
                pl.semaphore_signal(barrier, inc=1, device_id=(a, 2 * y + kk, cc), device_id_type=MESH)
    diag = (a, 2 * (1 - y) + 1 - k, c)
    corners = [(g, rr, c) for g in ((a, a + 1 - 2 * ah) if use_x else (a,))
               for rr in (r, 2 * y + 1 - k, 2 * (1 - y) + k, 2 * (1 - y) + 1 - k)][1:]
    for dev in (corners[1:] if use_x else corners[1:] + [xside]):
        pl.semaphore_signal(barrier, inc=1, device_id=dev, device_id_type=MESH)

    local[0].wait()
    for t in range(2):
        blk = R.qstage[pl.ds(pl.multiple_of((2 * t + ah) * 32, 32), 32), :].astype(f32)
        parts = [blk[:, (3 * h + j) * 64:(3 * h + j + 1) * 64] for j in range(3) for h in range(2)]
        R.w_qkv[y, k, c, t, ah] = cat(parts).astype(bf16)
    R.vec[...] = jnp.zeros((16, 128), f32)
    for i, name in enumerate(VECTORS):
        R.vec[i:i + 1, :] = getattr(R, name)[...].astype(f32).reshape(1, 128)
    for i in range(4):
        R.vec[8 + i:9 + i, :] = R.up_bias[128 * i:128 * i + 128].astype(f32).reshape(1, 128)
    pl.semaphore_wait(barrier, 13 if use_x else 10)

    def rows_in(src, dst, which):
        sends = []
        for qq in range(4):
            kq, cq = qq % 2, 2 * k + qq // 2
            me = (k == kq) & (c == cq)
            for j, (s0, d0, n) in enumerate(((qq * 128, 0, 128), ((7 - qq) * 128, 128, 128), ((8 + 2 * qq) * 128, 256, 256))):
                s = src.at[pl.ds(s0, n), :]
                d = dst.at[c, pl.ds(d0, n), :]
                rs = R.irsem.at[which, c, j]
                cp = pltpu.make_async_remote_copy(
                    src_ref=s, dst_ref=d, send_sem=R.issem.at[which, qq, j], recv_sem=rs,
                    device_id=(a, 2 * y + kq, cq), device_id_type=MESH)
                sends.append((me, cp))

                @pl.when(jnp.logical_not(me))
                def _():
                    cp.start()

                @pl.when(me)
                def _():
                    pltpu.make_async_copy(s, d, rs).start()

        def wait():
            for cc in range(4):
                for j, (d0, n) in enumerate(((0, 128), (128, 128), (256, 256))):
                    d = dst.at[cc, pl.ds(d0, n), :]
                    pltpu.make_async_copy(d, d, R.irsem.at[which, cc, j]).wait()
        return sends, wait

    def rows_out(src, dst, which, only=(0, 1, 2)):
        sends = []
        for cc in range(4):
            me = (c // 2 == k) & (c == cc)
            for j, (s0, d0, n) in enumerate(((0, lo_row, 128), (128, hi_row, 128), (256, 1024 + pl.multiple_of(q * 256, 256), 256))):
                if j not in only:
                    continue
                s = src.at[cc, pl.ds(s0, n), :]
                d = dst.at[pl.ds(d0, n), :]
                rs = R.irsem.at[which, q, j]
                cp = pltpu.make_async_remote_copy(
                    src_ref=s, dst_ref=d, send_sem=R.issem.at[which, cc, j], recv_sem=rs,
                    device_id=(a, owner_row, cc), device_id_type=MESH)
                sends.append((me, cp))

                @pl.when(jnp.logical_not(me))
                def _():
                    cp.start()

                @pl.when(me)
                def _():
                    pltpu.make_async_copy(s, d, rs).start()

        def wait():
            for qq in range(4):
                for j, (d0, n) in enumerate(((qq * 128, 128), ((7 - qq) * 128, 128), ((8 + 2 * qq) * 128, 256))):
                    d = dst.at[pl.ds(d0, n), :]
                    pltpu.make_async_copy(d, d, R.irsem.at[which, qq, j]).wait()
        return sends, wait

    def finish_sends(sends):
        for me, cp in sends:
            @pl.when(jnp.logical_not(me))
            def _():
                cp.wait_send()

    wst = {}

    def w_z(name):
        w = getattr(R, "w_" + name)
        here = lambda: w.at[y, k, c, :, ah]
        wst[name, "far"] = send(here, here, (a, r, c_far))
        wst[name, "near"] = send(here, here, zside)

    def w_f(name):
        w = getattr(R, "w_" + name)
        wst[name, "far"].wait_recv()
        here = lambda: w.at[y, k, c_far, :, ah]
        wst[name, "on"] = send(here, here, zside)

    def to_sibling(name, s):
        wst.setdefault((name, "core"), []).append(send(s, s, core))

    def w_1(name):
        w = getattr(R, "w_" + name)
        wst[name, "near"].wait_recv()
        wst[name, "on"].wait_recv()
        s = lambda: w.at[y, k, :, 0, ah]
        wst[name, "x1"] = send(s, s, xside)
        s = lambda: w.at[y, k, :, 1, ah]
        wst[name, "y1"] = send(s, s, yside)
        to_sibling(name, lambda: w.at[y, k, :, :, ah])

    def w_2(name):
        w = getattr(R, "w_" + name)
        wst[name, "x1"].wait_recv()
        s = lambda: w.at[y, k, :, 0]
        wst[name, "y2"] = send(s, s, yside)
        to_sibling(name, lambda: w.at[y, k, :, 0, a_])
        wst[name, "y1"].wait_recv()
        s = lambda: w.at[:, k, :, 1, ah]
        wst[name, "x2"] = send(s, s, xside)
        to_sibling(name, lambda: w.at[y_, k, :, 1, ah])

    def w_3(name):
        w = getattr(R, "w_" + name)
        wst[name, "y2"].wait_recv()
        to_sibling(name, lambda: w.at[y_, k, :, 0])
        wst[name, "x2"].wait_recv()
        to_sibling(name, lambda: w.at[:, k, :, 1, a_])

    def w_4(name):
        for cp in wst[name, "core"]:
            cp.wait_recv()

    gst = {}

    def g_0(name):
        g, b0 = getattr(R, "g_" + name), getattr(R, "b0_" + name)
        gst[name, "core"] = send(lambda: g.at[:, k_], b0, core)

    def g_1(name):
        g, b0, b1 = getattr(R, "g_" + name), getattr(R, "b0_" + name), getattr(R, "b1_" + name)
        if name != "qkv":
            gst[name, "core"].wait_recv()

        def one(i):
            yy, cc = i // 4, i % 4
            b0[yy, cc] = (b0[yy, cc].astype(f32) + g[yy, k, cc].astype(f32)).astype(bf16)
        loop(8, one)
        if use_x:
            b2 = getattr(R, "b2_" + name)
            gst[name, "y1"] = send(lambda: b0.at[y_, :, 0], b1, yside)
            gst[name, "x1"] = send(lambda: b0.at[:, :, 1, a_], b2, xside)
        else:
            gst[name, "y1"] = send(lambda: b0.at[y_], b1, yside)

    def g_2(name):
        b0, b1 = getattr(R, "b0_" + name), getattr(R, "b1_" + name)
        gst[name, "y1"].wait_recv()
        if not use_x:
            def one(cc):
                b1[cc] = (b1[cc].astype(f32) + b0[y, cc].astype(f32)).astype(bf16)
            loop(4, one)
            return
        b2, b3, b4 = (getattr(R, "b%d_%s" % (i, name)) for i in (2, 3, 4))

        def one(cc):
            b1[cc] = (b1[cc].astype(f32) + b0[y, cc, 0].astype(f32)).astype(bf16)
        loop(4, one)
        gst[name, "x2"] = send(lambda: b1.at[:, a_], b3, xside)
        gst[name, "x1"].wait_recv()

        def two(i):
            yy, cc = i // 4, i % 4
            b2[yy, cc] = (b2[yy, cc].astype(f32) + b0[yy, cc, 1, ah].astype(f32)).astype(bf16)
        loop(8, two)
        gst[name, "y2"] = send(lambda: b2.at[y_], b4, yside)

    def g_3(name):
        b1, z, b5 = (getattr(R, "%s_%s" % (i, name)) for i in ("b1", "z" if use_x else "b1", "b5"))
        if use_x:
            b2, b3, b4 = (getattr(R, "b%d_%s" % (i, name)) for i in (2, 3, 4))
            gst[name, "x2"].wait_recv()
            gst[name, "y2"].wait_recv()

            def one(cc):
                z[cc, 0] = (b1[cc, ah].astype(f32) + b3[cc].astype(f32)).astype(bf16)
                z[cc, 1] = (b2[y, cc].astype(f32) + b4[cc].astype(f32)).astype(bf16)
            loop(4, one)
        gst[name, "near"] = [send(lambda cc=cc: z.at[cc], lambda i=i: b5.at[i], zside) for i, cc in enumerate((c_near, c_across))]

    def g_4(name):
        z, b5, b6 = (getattr(R, "%s_%s" % (i, name)) for i in ("z" if use_x else "b1", "b5", "b6"))
        for cp in gst[name, "near"]:
            cp.wait_recv()
        b5[1] = (b5[1].astype(f32) + z[c_far].astype(f32)).astype(bf16)
        gst[name, "far"] = send(lambda: b5.at[1], b6, (a, r, c_far))

    def g_5(name):
        z, b5, b6, fin = (getattr(R, "%s_%s" % (i, name)) for i in ("z" if use_x else "b1", "b5", "b6", "fin"))
        gst[name, "far"].wait_recv()
        total = z[c].astype(f32) + b5[0].astype(f32) + b6[...].astype(f32)
        if use_x:
            for t in range(2):
                fin[t, ah] = total[t].astype(bf16)
            s = lambda: fin.at[:, ah]
            gst[name, "x3"] = send(s, s, xside)
        else:
            fin[...] = total.astype(bf16)

    def g_6(name):
        if use_x:
            gst[name, "x3"].wait_recv()
        rows, cols = BLOCK[name]
        getattr(R, name + "_o")[...] = getattr(R, "fin_" + name)[...].reshape(rows, cols)

    def weight(name, rr):
        w = getattr(R, "w_" + name)
        return w[rr // 2, rr % 2].reshape(4 * BLOCK[name][0], BLOCK[name][1])

    R.vecs[c] = R.vec[...]
    R.vecr[r] = R.vec[...]
    vec_cp = [send(R.vec, R.vecs.at[c], (a, r, (c + i) % 4)) for i in range(1, 4)]
    vec_cp += [send(R.vec, R.vecr.at[r], dev) for dev in (core, yside, diag)]
    w_z("qkv")
    for cp in local[1:]:
        cp.wait()
    w_z("og")
    w_f("qkv")
    w_z("up")
    w_f("og")
    w_1("qkv")
    w_z("d0")
    w_1("og")
    w_f("up")
    w_2("qkv")
    w_1("up")
    w_f("d0")
    tok_sends, tok_wait = rows_in(R.tok, R.xo, 0)
    w_2("og")
    w_1("d0")
    w_3("qkv")
    w_2("up")
    for cp in vec_cp:
        cp.wait_recv()

    def vec_row(i):
        return cat([R.vecs[cc, i:i + 1, :] for cc in range(4)])

    tok_wait()

    def xrows():
        return cat([R.xo[cc] for cc in range(4)]).astype(f32)

    def norm_parts(v):
        mean = jnp.sum(v, axis=1, keepdims=True) * (1.0 / D)
        cen = v - mean
        var = jnp.sum(cen * cen, axis=1, keepdims=True) * (1.0 / D)
        inv = lax.rsqrt(var + EPS)
        return cen * inv, inv

    standard, _ = norm_parts(xrows())
    n1 = (standard * vec_row(0) + vec_row(1)).astype(bf16)
    R.n1[...] = n1
    R.xn[pl.ds(lo_row, 128), :] = n1[0:128]
    R.xn[pl.ds(hi_row, 128), :] = n1[128:256]
    R.xn[1024:1280, :] = n1[256:512]
    here = [R.xn.at[pl.ds(lo_row, 128), :], R.xn.at[pl.ds(hi_row, 128), :]]
    to_z = [send(s, s, zside) for s in here]
    to_core = [send(s, s, core) for s in here]
    w_z("d1")
    w_3("og")
    w_2("d0")
    w_4("qkv")
    w_3("up")
    qz = q + 2 - 4 * (q // 2)
    for cp in to_z:
        cp.wait_recv()
    there = [R.xn.at[pl.ds(pl.multiple_of(qz * 128, 128), 128), :],
             R.xn.at[pl.ds(pl.multiple_of((7 - qz) * 128, 128), 128), :]]
    to_core += [send(s, s, core) for s in there]
    for cp in to_core:
        cp.wait_recv()

    def qkv_pair(p):
        w = weight("qkv", p)
        R.qp[p] = (dot(R.n1[...], w[:, 0:128], 1, 0).astype(bf16).astype(f32) * 0.125).astype(bf16)
        R.kv[p] = dot(R.xn[...], w[:, 128:384], 1, 0).astype(bf16)
    loop(4, qkv_pair)
    w_f("d1")
    cot_sends, cot_wait = rows_in(R.cot, R.co, 1)

    lane = lax.broadcasted_iota(jnp.int32, (T, 128), 1)
    key_at = lax.broadcasted_iota(jnp.int32, (512, 128), 0)
    col_at = lax.broadcasted_iota(jnp.int32, (512, 128), 1)
    lo_ok = key_at <= col_at + q * 128
    hi_ok = key_at + 512 <= col_at + (7 - q) * 128
    own_ok = (key_at <= col_at)[0:128]

    def attend_pair(p):
        for h in range(2):
            keys = R.kv[p, :, 0:128]
            vals = R.kv[p, :, 128:256]
            qm = jnp.where(lane // 64 == h, R.qp[p], jnp.zeros((), bf16))
            s1 = dot(keys[0:512], qm, 1, 1)
            s2 = dot(keys[512:1024], qm[128:512], 1, 1)
            sa = jnp.where(own_ok, dot(keys[1024:1152], qm[256:384], 1, 1), MASKED)
            sb = jnp.where(own_ok, dot(keys[1152:1280], qm[384:512], 1, 1), MASKED)
            s1 = cat([jnp.where(lo_ok, s1[:, 0:128], MASKED), s1[:, 128:512]])
            s2 = cat([jnp.where(hi_ok, s2[:, 0:128], MASKED), s2[:, 128:384]])
            top = lambda v: jnp.max(v, axis=0, keepdims=True)
            add = lambda v: jnp.sum(v, axis=0, keepdims=True)
            m1 = top(s1)
            m2 = jnp.maximum(m1[:, 128:512], top(s2))
            m = cat([m1[:, 0:128], m2[:, 0:128], jnp.maximum(m2[:, 128:384], cat([top(sa), top(sb)]))])
            e1 = jnp.exp(s1 - m)
            e2 = jnp.exp(s2 - m[:, 128:512])
            ea = jnp.exp(sa - m[:, 256:384])
            eb = jnp.exp(sb - m[:, 384:512])
            l1 = add(e1)
            l2 = l1[:, 128:512] + add(e2)
            total = cat([l1[:, 0:128], l2[:, 0:128], l2[:, 128:384] + cat([add(ea), add(eb)])])
            e1, e2, ea, eb = (v.astype(bf16) for v in (e1, e2, ea, eb))
            R.p1[2 * p + h] = e1
            R.p2[2 * p + h] = e2
            R.po[2 * p + h, :, 0:128] = ea
            R.po[2 * p + h, :, 128:256] = eb
            o1 = dot(vals[0:512], e1, 0, 0)
            o2 = dot(vals[512:1024], e2, 0, 0)
            oa = dot(vals[1024:1152], ea, 0, 0)
            ob = dot(vals[1152:1280], eb, 0, 0)
            o2 = o1[:, 128:512] + o2
            o = cat([o1[:, 0:128], o2[:, 0:128], o2[:, 128:384] + cat([oa, ob])])
            inv = 1.0 / total
            R.li[p, h:h + 1, :] = inv
            R.att[p, 64 * h:64 * h + 64, :] = (o[64 * h:64 * h + 64] * inv).astype(bf16)
    def attend_step(p):
        attend_pair(p)

        @pl.when(p == 0)
        def _():
            w_1("d1")
            w_3("d0")

        @pl.when(p == 2)
        def _():
            w_2("d1")
    loop(4, attend_step)
    w_4("og")

    def lanes(cc):
        return pl.ds(pl.multiple_of(cc * 128, 128), 128)

    def wide(cc):
        return pl.ds(pl.multiple_of(cc * 256, 256), 256)

    def out_block(cc):
        w = R.w_og[:, :, cc].reshape(512, 256)
        br = dot(R.att[...].reshape(512, T), w, 0, 0)
        ao = br[:, 0:128]
        gate = sigmoid(br[:, 128:256] + R.vecs[cc, 2:3, :])
        R.ao[cc] = ao
        R.g1[cc] = gate
        R.mid[cc] = R.xo[cc].astype(f32) + gate * ao
    loop(4, out_block)

    def midrows():
        return cat([R.mid[cc] for cc in range(4)])

    standard, _ = norm_parts(midrows())
    R.n2[...] = (standard * vec_row(3) + vec_row(4)).astype(bf16)
    w_4("up")

    def up_block(rr):
        pre = dot(R.n2[...], weight("up", rr), 1, 0) + cat([R.vecr[rr, 8 + i:9 + i, :] for i in range(4)])
        s = sigmoid(pre)
        R.hid[rr] = (pre * s).astype(bf16)
        R.slp[rr] = (s * (1.0 + pre * (1.0 - s))).astype(bf16)
    loop(4, up_block)
    w_3("d1")
    w_4("d0")
    w_4("d1")
    cot_wait()

    def down_block(cc):
        br = 0.0
        for rr in range(4):
            for j in range(2):
                w = getattr(R, "w_d%d" % j)[rr // 2, rr % 2, cc].reshape(256, 256)
                br = br + dot(R.hid[rr, :, 256 * j:256 * j + 256], w, 1, 0)
        ffn = br[:, 0:128] + R.vecs[cc, 5:6, :]
        gate = sigmoid(br[:, 128:256] + R.vecs[cc, 6:7, :])
        R.out[cc] = (R.mid[cc] + gate * ffn).astype(bf16)
        g = R.co[cc].astype(f32)
        gf = (g * gate).astype(bf16)
        gg = (g * ffn * gate * (1.0 - gate)).astype(bf16)
        R.pair[:, wide(cc)] = cat([gf, gg])
        R.sv[5, pl.ds(cc, 1), :] = jnp.sum(gf.astype(f32), axis=0, keepdims=True)
        R.sv[6, pl.ds(cc, 1), :] = jnp.sum(gg.astype(f32), axis=0, keepdims=True)
    loop(4, down_block)
    out_sends, out_wait = rows_out(R.out, R.out_o, 2)

    def grad_down(j, kk):
        for yy in range(2):
            g = dot(R.hid[2 * yy + kk, :, 256 * j:256 * j + 256], R.pair[...], 0, 0).astype(bf16)
            for cc in range(4):
                getattr(R, "g_d%d" % j)[yy, kk, cc] = g[:, 256 * cc:256 * cc + 256].reshape(2, 2, 64, 256)
    for j in range(2):
        grad_down(j, 1 - k)
        g_0("d%d" % j)
        grad_down(j, k)
    g_1("d0")

    def back_up(rr):
        gh = 0.0
        for cc in range(4):
            w = [getattr(R, "w_d%d" % j)[rr // 2, rr % 2, cc].reshape(256, 256) for j in range(2)]
            gh = gh + dot(R.pair[:, 256 * cc:256 * cc + 256], cat(w, 0), 1, 1)
        gp = (gh * R.slp[rr].astype(f32)).astype(bf16)
        R.slp[rr] = gp
        tot = jnp.sum(gp.astype(f32), axis=0, keepdims=True)
        for i in range(4):
            R.sv[8 + rr, i:i + 1, :] = tot[:, 128 * i:128 * i + 128]
    loop(4, back_up)
    g_1("d1")

    def grad_up(yy, kk):
        g = dot(R.n2[...], R.slp[2 * yy + kk], 0, 0).astype(bf16)
        R.g_up[yy, kk] = g.reshape(4, 2, 2, 32, 512)
    grad_up(0, 1 - k)
    grad_up(1, 1 - k)
    g_0("up")
    grad_up(0, k)
    grad_up(1, k)

    gn = dot(R.slp[0], weight("up", 0), 1, 1)
    for rr in range(1, 4):
        gn = gn + dot(R.slp[rr], weight("up", rr), 1, 1)

    def norm_back(v, grad, gain_row):
        std, inv = norm_parts(v)
        gs = jnp.sum(grad * std, axis=0, keepdims=True)
        gb = jnp.sum(grad, axis=0, keepdims=True)
        s = grad * vec_row(gain_row)
        f = jnp.sum(s, axis=1, keepdims=True) * (1.0 / D)
        e = jnp.sum(s * std, axis=1, keepdims=True) * (1.0 / D)
        return inv * (s - f - std * e), gs, gb

    def put_sums(at, gs, gb):
        for cc in range(4):
            R.sv[at, cc:cc + 1, :] = gs[:, 128 * cc:128 * cc + 128]
            R.sv[at + 1, cc:cc + 1, :] = gb[:, 128 * cc:128 * cc + 128]

    gm, gs, gb = norm_back(midrows(), gn, 3)
    put_sums(2, gs, gb)
    for cc in range(4):
        g_mid = R.co[cc].astype(f32) + gm[:, 128 * cc:128 * cc + 128]
        R.gm[cc] = g_mid
        gate = R.g1[cc]
        ga = (g_mid * gate).astype(bf16)
        gg = (g_mid * R.ao[cc] * gate * (1.0 - gate)).astype(bf16)
        R.pair[:, 256 * cc:256 * cc + 256] = cat([ga, gg])
        R.sv[4, cc:cc + 1, :] = jnp.sum(gg.astype(f32), axis=0, keepdims=True)
    g_2("d0")
    g_1("up")

    def grad_out(cc):
        R.g_og[:, :, cc] = dot(R.att[...].reshape(512, T), R.pair[:, wide(cc)], 1, 0).astype(bf16).reshape(2, 2, 2, 2, 32, 256)
    loop(4, grad_out)
    g_0("og")
    do = 0.0
    for cc in range(4):
        do = do + dot(R.w_og[:, :, cc].reshape(512, 256), R.pair[:, 256 * cc:256 * cc + 256], 1, 1)
    for cc in range(4):
        R.mid[cc] = do[:, 128 * cc:128 * cc + 128]
    for i in range(2):
        R.hid[i] = R.xn[512 * i:512 * i + 512, :].T
    R.hid[2, :, 0:256] = R.xn[1024:1280, :].T
    R.hid[3] = R.n1[...].T
    g_1("og")

    row_of = lax.broadcasted_iota(jnp.int32, (128, T), 0)

    def back_pair(p):
        rows = pl.ds(pl.multiple_of(p * 128, 128), 128)
        dot_t = cat([R.mid[cc, rows, :] for cc in range(4)])
        dot_t = dot_t * jnp.where(row_of < 64, R.li[p, 0:1, :], R.li[p, 1:2, :])
        prod = dot_t * R.att[p].astype(f32)
        dot_t = dot_t.astype(bf16)
        dot_n = dot_t.T
        keys = R.kv[p, :, 0:128]
        vals = R.kv[p, :, 128:256]
        grads = []
        queries = []
        for h in range(2):
            delta = jnp.sum(prod[64 * h:64 * h + 64], axis=0, keepdims=True)
            qm = jnp.where(lane // 64 == h, R.qp[p], jnp.zeros((), bf16))
            om = jnp.where(lane // 64 == h, dot_n, jnp.zeros((), bf16))
            omt = jnp.where(row_of // 64 == h, dot_t, jnp.zeros((), bf16))
            e1, e2 = R.p1[2 * p + h], R.p2[2 * p + h]
            ea, eb = R.po[2 * p + h, :, 0:128], R.po[2 * p + h, :, 128:256]
            d1 = (e1.astype(f32) * (dot(vals[0:512], omt, 1, 0) - delta)).astype(bf16)
            d2 = (e2.astype(f32) * (dot(vals[512:1024], omt[:, 128:512], 1, 0) - delta[:, 128:512])).astype(bf16)
            da = (ea.astype(f32) * (dot(vals[1024:1152], omt[:, 256:384], 1, 0) - delta[:, 256:384])).astype(bf16)
            db = (eb.astype(f32) * (dot(vals[1152:1280], omt[:, 384:512], 1, 0) - delta[:, 384:512])).astype(bf16)
            dk = cat([dot(d1, qm, 1, 0), dot(d2, qm[128:512], 1, 0), dot(da, qm[256:384], 1, 0), dot(db, qm[384:512], 1, 0)], 0)
            dv = cat([dot(e1, om, 1, 0), dot(e2, om[128:512], 1, 0), dot(ea, om[256:384], 1, 0), dot(eb, om[384:512], 1, 0)], 0)
            grads.append((dk, dv))
            x1 = dot(keys[0:512], d1, 0, 0)
            x2 = x1[:, 128:512] + dot(keys[512:1024], d2, 0, 0)
            xab = cat([dot(keys[1024:1152], da, 0, 0), dot(keys[1152:1280], db, 0, 0)])
            dq = cat([x1[:, 0:128], x2[:, 0:128], x2[:, 128:384] + xab])
            queries.append(dq[64 * h:64 * h + 64])
        R.kv[p, :, 0:128] = (grads[0][0] + grads[1][0]).astype(bf16)
        R.kv[p, :, 128:256] = (grads[0][1] + grads[1][1]).astype(bf16)
        R.qp[p] = (cat(queries, 0) * 0.125).astype(bf16).T
        gk = dot(R.hid[0], R.kv[p, 0:512, :], 1, 0) + dot(R.hid[1], R.kv[p, 512:1024, :], 1, 0)
        gk = gk + dot(R.hid[2, :, 0:256], R.kv[p, 1024:1280, :], 1, 0)
        g = cat([dot(R.hid[3], R.qp[p], 1, 0), gk]).astype(bf16)
        R.g_qkv[p // 2, p % 2] = g.reshape(4, 2, 2, 32, 384)

    def qkv_copy(yy):
        return pltpu.make_async_remote_copy(
            src_ref=R.g_qkv.at[yy, 1 - k], dst_ref=R.b0_qkv.at[yy], send_sem=R.qsem.at[0, yy], recv_sem=R.qsem.at[1, yy],
            device_id=core, device_id_type=MESH)

    def back_step(p):
        back_pair(p)

        @pl.when(p % 2 != k)
        def _():
            qkv_copy(p // 2).start()

        @pl.when(p == 0)
        def _():
            g_2("d1")

        @pl.when(p == 1)
        def _():
            g_3("d0")
    loop(4, back_step)
    g_2("up")
    g_4("d0")

    def back_rows(first, count):
        rows = pl.ds(first, count)
        total = dot(R.kv[0, rows, :], weight("qkv", 0)[:, 128:384], 1, 1)
        for p in range(1, 4):
            total = total + dot(R.kv[p, rows, :], weight("qkv", p)[:, 128:384], 1, 1)
        return total

    def chunk_rows(qq):
        return (pl.multiple_of(qq * 128, 128), pl.multiple_of((7 - qq) * 128, 128))

    q1 = q + 1 - 2 * k
    q2 = qz
    q3 = q2 + 1 - 2 * k
    for i, row in enumerate(chunk_rows(q1)):
        R.ex[0, 128 * i:128 * i + 128, :] = back_rows(row, 128).astype(bf16)
    for i, row in enumerate(chunk_rows(q3)):
        R.ex[1, 128 * i:128 * i + 128, :] = back_rows(row, 128).astype(bf16)
    part_core = send(R.ex, R.exr, core)
    for yy in range(2):
        qkv_copy(yy).wait_recv()
    g_2("og")
    g_1("qkv")
    mine2 = [back_rows(row, 128) for row in chunk_rows(q2)]
    part_core.wait_recv()
    for i in range(2):
        R.ez[128 * i:128 * i + 128, :] = (mine2[i] + R.exr[1, 128 * i:128 * i + 128, :].astype(f32)).astype(bf16)
    part_z = send(R.ez, R.ezr, zside)

    def x_rows(at, n):
        return cat([R.xo[cc, at:at + n, :] for cc in range(4)]).astype(f32)

    def own_rows(row, n, at):
        own = back_rows(row, n)
        for cc in range(4):
            R.mid[cc, at:at + n, :] = own[:, 128 * cc:128 * cc + 128]

    def add_queries(p):
        more = dot(R.qp[p], weight("qkv", p)[:, 0:128], 1, 1)
        for cc in range(4):
            R.mid[cc] = R.mid[cc] + more[:, 128 * cc:128 * cc + 128]

    def to_input(at, n):
        gx, gs, gb = norm_back(x_rows(at, n), cat([R.mid[cc, at:at + n, :] for cc in range(4)]), 0)
        for cc in range(4):
            R.ing[cc, at:at + n, :] = (R.gm[cc, at:at + n, :] + gx[:, 128 * cc:128 * cc + 128]).astype(bf16)
        return gs, gb

    own_rows(lo_row, 128, 0)
    own_rows(hi_row, 128, 128)
    own_rows(1024, 256, 256)
    loop(4, add_queries)
    g_3("d1")
    gs2, gb2 = to_input(256, 256)
    g_3("up")
    ing_sends2, _ = rows_out(R.ing, R.ing_o, 3, (2,))
    g_5("d0")
    g_3("og")
    g_4("d1")
    part_z.wait_recv()
    for cc in range(4):
        here = slice(128 * cc, 128 * cc + 128)
        R.mid[cc, 0:256, :] = R.mid[cc, 0:256, :] + (R.exr[0, :, here].astype(f32) + R.ezr[:, here].astype(f32))
    gs, gb = to_input(0, 256)
    put_sums(0, gs + gs2, gb + gb2)
    R.sva[c] = R.sv[...]
    sv_z = [send(R.sv, R.sva.at[c], (a, r, (c + i) % 4)) for i in range(1, 4)]
    ing_sends, ing_wait = rows_out(R.ing, R.ing_o, 3, (0, 1))
    g_2("qkv")
    g_4("up")

    for cp in sv_z:
        cp.wait_recv()
    R.sv2[...] = (R.sva[0] + R.sva[1]) + (R.sva[2] + R.sva[3])
    slot = 4 * ah + r if use_x else r
    R.svr[slot] = R.sv2[...]
    sv_all = [send(R.sv2, R.svr.at[slot], dev) for dev in corners]
    g_5("d1")
    g_4("og")
    g_3("qkv")
    g_5("up")
    g_5("og")
    g_4("qkv")
    for cp in sv_all:
        cp.wait_recv()
    total = R.svr[0]
    for i in range(1, 8 if use_x else 4):
        total = total + R.svr[i]
    R.sv2t[...] = total
    R.small_o[...] = jnp.zeros((16, 128), f32)
    for i in range(7):
        R.small_o[i:i + 1, :] = R.sv2t[i, pl.ds(c, 1), :]
    for i in range(4):
        R.small_o[8 + i:9 + i, :] = R.sv2t[8 + r, i:i + 1, :]
    g_5("qkv")
    for name in NAMES:
        g_6(name)

    out_wait()
    ing_wait()
    for yy in range(2):
        qkv_copy(yy).wait_send()
    for cp in pending:
        cp.wait_send()
    for sends in (tok_sends, cot_sends, out_sends, ing_sends2, ing_sends):
        finish_sends(sends)


def body(use_x, tokens, cotangent, norm1_gain, norm1_bias, qkv_weight, out_weight, gate1_weight,
         gate1_bias, norm2_gain, norm2_bias, up_weight, up_bias, down_weight, down_bias,
         gate2_weight, gate2_bias):
    hbm = pl.BlockSpec(memory_space=pl.ANY)
    vmem = pl.BlockSpec(memory_space=pltpu.VMEM)
    ins = {"tok": tokens, "cot": cotangent, "i_qkv": qkv_weight, "i_out": out_weight, "i_gate1": gate1_weight,
           "i_up": up_weight, "i_down": down_weight, "i_gate2": gate2_weight,
           "norm1_gain": norm1_gain, "norm1_bias": norm1_bias, "gate1_bias": gate1_bias, "norm2_gain": norm2_gain,
           "norm2_bias": norm2_bias, "down_bias": down_bias, "gate2_bias": gate2_bias, "up_bias": up_bias}
    outs = {"out_o": ((2048, 128), bf16, hbm), "ing_o": ((2048, 128), bf16, hbm)}
    for name in NAMES:
        outs[name + "_o"] = (BLOCK[name], bf16, vmem)
    outs["small_o"] = ((16, 128), f32, vmem)
    scr = {}
    for name in NAMES:
        rows, cols = BLOCK[name]
        rq = rows // 4
        scr["w_" + name] = ((2, 2, 4, 2, 2, rq, cols), bf16)
        scr["g_" + name] = ((2, 2, 4, 2, 2, rq, cols), bf16)
        scr["b0_" + name] = ((2, 4, 2, 2, rq, cols), bf16)
        if use_x:
            scr["b1_" + name] = ((4, 2, rq, cols), bf16)
            scr["b2_" + name] = ((2, 4, rq, cols), bf16)
            scr["b3_" + name] = ((4, rq, cols), bf16)
            scr["b4_" + name] = ((4, rq, cols), bf16)
            scr["z_" + name] = ((4, 2, rq, cols), bf16)
            scr["b5_" + name] = ((2, 2, rq, cols), bf16)
            scr["b6_" + name] = ((2, rq, cols), bf16)
        else:
            scr["b1_" + name] = ((4, 2, 2, rq, cols), bf16)
            scr["b5_" + name] = ((2, 2, 2, rq, cols), bf16)
            scr["b6_" + name] = ((2, 2, rq, cols), bf16)
        scr["fin_" + name] = ((2, 2, rq, cols), bf16)
    scr.update({
        "qstage": ((128, 384), bf16), "vec": ((16, 128), f32), "vecs": ((4, 16, 128), f32), "vecr": ((4, 16, 128), f32),
        "xo": ((4, T, 128), bf16), "co": ((4, T, 128), bf16), "n1": ((T, D), bf16),
        "xn": ((1280, D), bf16), "qp": ((4, T, 128), bf16), "kv": ((4, 1280, 256), bf16),
        "p1": ((8, 512, 512), bf16), "p2": ((8, 512, 384), bf16), "po": ((8, 128, 256), bf16),
        "li": ((4, 8, T), f32), "att": ((4, 128, T), bf16), "ao": ((4, T, 128), f32),
        "g1": ((4, T, 128), f32), "mid": ((4, T, 128), f32), "n2": ((T, D), bf16),
        "hid": ((4, T, 512), bf16), "slp": ((4, T, 512), bf16), "out": ((4, T, 128), bf16),
        "pair": ((T, 1024), bf16), "gm": ((4, T, 128), f32), "ing": ((4, T, 128), bf16),
        "ex": ((2, 256, D), bf16), "exr": ((2, 256, D), bf16), "ez": ((256, D), bf16), "ezr": ((256, D), bf16),
        "sv": ((12, 8, 128), f32), "sva": ((4, 12, 8, 128), f32), "sv2": ((12, 8, 128), f32),
        "sv2t": ((12, 8, 128), f32), "svr": ((8, 12, 8, 128), f32),
    })
    shapes = [pltpu.VMEM(s, d) for s, d in scr.values()]
    names_scr = tuple(scr) + ("ssem", "rsem", "issem", "irsem", "lsem", "qsem")
    n_sem = 160
    dma = pltpu.SemaphoreType.DMA
    shapes += [dma((n_sem,)), dma((n_sem,)), dma((4, 4, 3)), dma((4, 4, 3)), dma((20,)), dma((2, 2))]
    res = pl.pallas_call(
        partial(kernel, use_x, tuple(ins), tuple(outs), names_scr),
        out_shape=[jax.ShapeDtypeStruct(s, d) for s, d, _ in outs.values()],
        in_specs=[hbm] * 8 + [vmem] * 8,
        out_specs=[sp for _, _, sp in outs.values()],
        scratch_shapes=shapes,
        compiler_params=pltpu.CompilerParams(collective_id=0, has_side_effects=True, vmem_limit_bytes=60 * 1024 * 1024),
    )(*ins.values())
    if not use_x:
        summed = lax.psum(tuple(v.astype(f32) for v in res[2:]), "grp")
        res = list(res[:2]) + list(summed)
    flat = {"out": (2048, 128), "ing": (2048, 128), "n1g": (128,), "n1b": (128,), "qkv": (128, 384),
            "w_out": (128, 128), "w_gate1": (128, 128), "g1b": (128,), "n2g": (128,), "n2b": (128,),
            "up": (128, 512), "upb": (512,), "w_down": (512, 128), "db": (128,), "w_gate2": (512, 128), "g2b": (128,)}
    kinds = {name: bf16 if name in ("out", "ing") else f32 for name in flat}
    return pl.pallas_call(
        finish,
        out_shape=[jax.ShapeDtypeStruct(shape, kinds[name]) for name, shape in flat.items()],
        in_specs=[vmem] * 8,
        out_specs=[vmem] * 16,
    )(*res)


def finish(out_i, ing_i, qkv_i, og_i, up_i, d0_i, d1_i, small_i, out, ing, n1g, n1b, qkv, w_out, w_gate1, g1b, n2g, n2b,
           up, upb, w_down, db, w_gate2, g2b):
    out[...] = out_i[...]
    ing[...] = ing_i[...]
    g = qkv_i[...].astype(f32)
    qkv[...] = cat([g[:, (2 * j + h) * 64:(2 * j + h + 1) * 64] for h in range(2) for j in range(3)])
    w_out[...] = og_i[:, 0:128].astype(f32)
    w_gate1[...] = og_i[:, 128:256].astype(f32)
    up[...] = up_i[...].astype(f32)
    w_down[0:256, :] = d0_i[:, 0:128].astype(f32)
    w_down[256:512, :] = d1_i[:, 0:128].astype(f32)
    w_gate2[0:256, :] = d0_i[:, 128:256].astype(f32)
    w_gate2[256:512, :] = d1_i[:, 128:256].astype(f32)
    for i, ref in enumerate((n1g, n1b, n2g, n2b, g1b, db, g2b)):
        ref[...] = small_i[i:i + 1, :].reshape(128)
    for i in range(4):
        upb[128 * i:128 * i + 128] = small_i[8 + i:9 + i, :].reshape(128)


def solution(mesh):
    act = P(("grp", "row"), "col")
    col, row = P("col"), P("row")
    cr, rc = P("col", "row"), P("row", "col")
    return jax.shard_map(
        partial(body, mesh.shape["grp"] == 2),
        mesh=mesh,
        in_specs=(act, act, col, col, cr, rc, rc, col, col, col, cr, row, rc, col, rc, col),
        out_specs=(act, act, col, col, cr, rc, rc, col, col, col, cr, row, rc, col, rc, col),
        check_vma=False,
    )
```

```python
from functools import partial

import jax
import jax.numpy as jnp
from jax import lax
from jax.experimental import pallas as pl
from jax.experimental.pallas import tpu as pltpu
from jax.sharding import PartitionSpec as P

bf16 = jnp.bfloat16
f32 = jnp.float32
EPS = 1e-05
MASKED = -1e30
MESH = pl.DeviceIdType.MESH

T = 512
D = 512
BLOCK = {"qkv": (128, 384), "og": (128, 256), "up": (128, 512), "d0": (256, 256), "d1": (256, 256)}
NAMES = ("qkv", "og", "up", "d0", "d1")
VECTORS = ("norm1_gain", "norm1_bias", "gate1_bias", "norm2_gain", "norm2_bias", "down_bias", "gate2_bias")


def dot(a, b, ca, cb):
    return lax.dot_general(a, b, (((ca,), (cb,)), ((), ())), preferred_element_type=f32)


def loop(count, step):
    lax.fori_loop(0, count, lambda i, z: (step(i), z)[1], 0)


def cat(parts, axis=1):
    return jnp.concatenate(parts, axis=axis)


class Waiter:
    def __init__(self, make):
        self.make = make

    def wait_recv(self):
        self.make().wait_recv()

    def wait_send(self):
        self.make().wait_send()


def sigmoid(v):
    return 1.0 / (1.0 + jnp.exp(-v))


def kernel(use_x, names_in, names_out, names_scr, *refs):
    ref = dict(zip(names_in + names_out + names_scr, refs))
    R = type("R", (), ref)
    a = lax.axis_index("grp")
    r = lax.axis_index("row")
    c = lax.axis_index("col")
    y, k = r // 2, r % 2
    ah = a % 2
    q = 2 * (c % 2) + k
    y_, k_, a_ = 1 - y, 1 - k, 1 - ah
    c_far = lax.rem(c + 2, 4)
    c_near = c + 1 - 2 * (c % 2)
    c_across = lax.rem(c_near + 2, 4)
    slot = 4 * ah + r if use_x else r
    others = [lax.rem(c + i, 4) for i in range(1, 4)]
    core = (a, 2 * y + 1 - k, c)
    yside = (a, 2 * (1 - y) + k, c)
    xside = (a + 1 - 2 * ah, r, c)
    zside = (a, r, c + 1 - 2 * (c % 2))
    owner_row = 2 * y + c // 2
    lo_row = pl.multiple_of(q * 128, 128)
    hi_row = pl.multiple_of((7 - q) * 128, 128)

    counter = [0]
    pending = []

    def send(src, dst, dev):
        i = counter[0]
        counter[0] += 1

        def make():
            return pltpu.make_async_remote_copy(
                src_ref=src() if callable(src) else src, dst_ref=dst() if callable(dst) else dst,
                send_sem=R.ssem.at[i], recv_sem=R.rsem.at[i], device_id=dev, device_id_type=MESH)
        make().start()
        pending.append(Waiter(make))
        return pending[-1]

    local = []

    def fetch(src, dst):
        cp = pltpu.make_async_copy(src, dst, R.lsem.at[len(local)])
        cp.start()
        local.append(cp)

    fetch(R.i_qkv, R.qstage)
    for t in range(2):
        for name, sources, skip in (("og", ("out", "gate1"), 0), ("up", ("up",), 0),
                                    ("d0", ("down", "gate2"), 0), ("d1", ("down", "gate2"), 256)):
            rows, cols = BLOCK[name]
            rq = rows // 4
            w = getattr(R, "w_" + name)
            width = cols // len(sources)
            for j, s in enumerate(sources):
                at = pl.multiple_of((2 * t + ah) * rq + skip, 32)
                fetch(getattr(R, "i_" + s).at[pl.ds(at, rq), :],
                      w.at[y, k, c, t, ah, :, pl.ds(j * width, width)])

    barrier = pltpu.get_barrier_semaphore()
    for kk in range(2):
        for cc in range(4):
            me = (k == kk) & (c == cc)

            @pl.when(jnp.logical_not(me))
            def _():
                pl.semaphore_signal(barrier, inc=1, device_id=(a, 2 * y + kk, cc), device_id_type=MESH)
    diag = (a, 2 * (1 - y) + 1 - k, c)
    corners = [(g, rr, c) for g in ((a, a + 1 - 2 * ah) if use_x else (a,))
               for rr in (r, 2 * y + 1 - k, 2 * (1 - y) + k, 2 * (1 - y) + 1 - k)][1:]
    for dev in (corners[1:] if use_x else corners[1:] + [xside]):
        pl.semaphore_signal(barrier, inc=1, device_id=dev, device_id_type=MESH)

    local[0].wait()
    for t in range(2):
        blk = R.qstage[pl.ds(pl.multiple_of((2 * t + ah) * 32, 32), 32), :].astype(f32)
        parts = [blk[:, (3 * h + j) * 64:(3 * h + j + 1) * 64] for j in range(3) for h in range(2)]
        R.w_qkv[y, k, c, t, ah] = cat(parts).astype(bf16)
    R.vec[...] = jnp.zeros((16, 128), f32)
    R.svb[32:40, :] = jnp.zeros((8, 128), f32)
    for i, name in enumerate(VECTORS):
        R.vec[i:i + 1, :] = getattr(R, name)[...].astype(f32).reshape(1, 128)
    for i in range(4):
        R.vec[8 + i:9 + i, :] = R.up_bias[128 * i:128 * i + 128].astype(f32).reshape(1, 128)
    pl.semaphore_wait(barrier, 13 if use_x else 10)

    def rows_in(src, dst, which):
        sends = []
        for qq in range(4):
            kq, cq = qq % 2, 2 * k + qq // 2
            me = (k == kq) & (c == cq)
            for j, (s0, d0, n) in enumerate(((qq * 128, 0, 128), ((7 - qq) * 128, 128, 128), ((8 + 2 * qq) * 128, 256, 256))):
                s = src.at[pl.ds(s0, n), :]
                d = dst.at[c, pl.ds(d0, n), :]
                rs = R.irsem.at[which, c, j]
                cp = pltpu.make_async_remote_copy(
                    src_ref=s, dst_ref=d, send_sem=R.issem.at[which, qq, j], recv_sem=rs,
                    device_id=(a, 2 * y + kq, cq), device_id_type=MESH)
                sends.append((me, cp))

                @pl.when(jnp.logical_not(me))
                def _():
                    cp.start()

                @pl.when(me)
                def _():
                    pltpu.make_async_copy(s, d, rs).start()

        def wait():
            for cc in range(4):
                for j, (d0, n) in enumerate(((0, 128), (128, 128), (256, 256))):
                    d = dst.at[cc, pl.ds(d0, n), :]
                    pltpu.make_async_copy(d, d, R.irsem.at[which, cc, j]).wait()
        return sends, wait

    def rows_out(src, dst, which, only=(0, 1, 2)):
        sends = []
        for cc in range(4):
            me = (c // 2 == k) & (c == cc)
            for j, (s0, d0, n) in enumerate(((0, lo_row, 128), (128, hi_row, 128), (256, 1024 + pl.multiple_of(q * 256, 256), 256))):
                if j not in only:
                    continue
                s = src.at[cc, pl.ds(s0, n), :]
                d = dst.at[pl.ds(d0, n), :]
                rs = R.irsem.at[which, q, j]
                cp = pltpu.make_async_remote_copy(
                    src_ref=s, dst_ref=d, send_sem=R.issem.at[which, cc, j], recv_sem=rs,
                    device_id=(a, owner_row, cc), device_id_type=MESH)
                sends.append((me, cp))

                @pl.when(jnp.logical_not(me))
                def _():
                    cp.start()

                @pl.when(me)
                def _():
                    pltpu.make_async_copy(s, d, rs).start()

        def wait():
            for qq in range(4):
                for j, (d0, n) in enumerate(((qq * 128, 128), ((7 - qq) * 128, 128), ((8 + 2 * qq) * 128, 256))):
                    d = dst.at[pl.ds(d0, n), :]
                    pltpu.make_async_copy(d, d, R.irsem.at[which, qq, j]).wait()
        return sends, wait

    def finish_sends(sends):
        for me, cp in sends:
            @pl.when(jnp.logical_not(me))
            def _():
                cp.wait_send()

    wst = {}

    def w_z(name):
        w = getattr(R, "w_" + name)
        here = lambda: w.at[y, k, c, :, ah]
        wst[name, "far"] = send(here, here, (a, r, c_far))
        wst[name, "near"] = send(here, here, zside)

    def w_f(name):
        w = getattr(R, "w_" + name)
        wst[name, "far"].wait_recv()
        here = lambda: w.at[y, k, c_far, :, ah]
        wst[name, "on"] = send(here, here, zside)

    def to_sibling(name, s):
        wst.setdefault((name, "core"), []).append(send(s, s, core))

    def w_1(name):
        w = getattr(R, "w_" + name)
        wst[name, "near"].wait_recv()
        wst[name, "on"].wait_recv()
        s = lambda: w.at[y, k, :, 0, ah]
        wst[name, "x1"] = send(s, s, xside)
        s = lambda: w.at[y, k, :, 1, ah]
        wst[name, "y1"] = send(s, s, yside)
        to_sibling(name, lambda: w.at[y, k, :, :, ah])

    def w_2(name):
        w = getattr(R, "w_" + name)
        wst[name, "x1"].wait_recv()
        s = lambda: w.at[y, k, :, 0]
        wst[name, "y2"] = send(s, s, yside)
        to_sibling(name, lambda: w.at[y, k, :, 0, a_])
        wst[name, "y1"].wait_recv()
        s = lambda: w.at[:, k, :, 1, ah]
        wst[name, "x2"] = send(s, s, xside)
        to_sibling(name, lambda: w.at[y_, k, :, 1, ah])

    def w_3(name):
        w = getattr(R, "w_" + name)
        wst[name, "y2"].wait_recv()
        to_sibling(name, lambda: w.at[y_, k, :, 0])
        wst[name, "x2"].wait_recv()
        to_sibling(name, lambda: w.at[:, k, :, 1, a_])

    def w_4(name):
        for cp in wst[name, "core"]:
            cp.wait_recv()

    gst = {}

    def g_0(name):
        g, b0 = getattr(R, "g_" + name), getattr(R, "b0_" + name)
        gst[name, "core"] = send(lambda: g.at[:, k_], b0, core)

    def g_1(name):
        g, b0, b1 = getattr(R, "g_" + name), getattr(R, "b0_" + name), getattr(R, "b1_" + name)
        if name != "qkv":
            gst[name, "core"].wait_recv()

        def one(i):
            yy, cc = i // 4, i % 4
            b0[yy, cc] = (b0[yy, cc].astype(f32) + g[yy, k, cc].astype(f32)).astype(bf16)
        loop(8, one)
        if use_x:
            b2 = getattr(R, "b2_" + name)
            gst[name, "y1"] = send(lambda: b0.at[y_, :, 0], b1, yside)
            gst[name, "x1"] = send(lambda: b0.at[:, :, 1, a_], b2, xside)
        else:
            gst[name, "y1"] = send(lambda: b0.at[y_], b1, yside)

    def g_2(name):
        b0, b1 = getattr(R, "b0_" + name), getattr(R, "b1_" + name)
        gst[name, "y1"].wait_recv()
        if not use_x:
            def one(cc):
                b1[cc] = (b1[cc].astype(f32) + b0[y, cc].astype(f32)).astype(bf16)
            loop(4, one)
            return
        b2, b3, b4 = (getattr(R, "b%d_%s" % (i, name)) for i in (2, 3, 4))

        def one(cc):
            b1[cc] = (b1[cc].astype(f32) + b0[y, cc, 0].astype(f32)).astype(bf16)
        loop(4, one)
        gst[name, "x2"] = send(lambda: b1.at[:, a_], b3, xside)
        gst[name, "x1"].wait_recv()

        def two(i):
            yy, cc = i // 4, i % 4
            b2[yy, cc] = (b2[yy, cc].astype(f32) + b0[yy, cc, 1, ah].astype(f32)).astype(bf16)
        loop(8, two)
        gst[name, "y2"] = send(lambda: b2.at[y_], b4, yside)

    def g_3(name):
        b1, z, b5 = (getattr(R, "%s_%s" % (i, name)) for i in ("b1", "z" if use_x else "b1", "b5"))
        if use_x:
            b2, b3, b4 = (getattr(R, "b%d_%s" % (i, name)) for i in (2, 3, 4))
            gst[name, "x2"].wait_recv()
            gst[name, "y2"].wait_recv()

            def one(cc):
                z[cc, 0] = (b1[cc, ah].astype(f32) + b3[cc].astype(f32)).astype(bf16)
                z[cc, 1] = (b2[y, cc].astype(f32) + b4[cc].astype(f32)).astype(bf16)
            loop(4, one)
        gst[name, "near"] = [send(lambda cc=cc: z.at[cc], lambda i=i: b5.at[i], zside) for i, cc in enumerate((c_near, c_across))]

    def g_4(name):
        z, b5, b6 = (getattr(R, "%s_%s" % (i, name)) for i in ("z" if use_x else "b1", "b5", "b6"))
        for cp in gst[name, "near"]:
            cp.wait_recv()
        b5[1] = (b5[1].astype(f32) + z[c_far].astype(f32)).astype(bf16)
        gst[name, "far"] = send(lambda: b5.at[1], b6, (a, r, c_far))

    def g_5(name):
        z, b5, b6, fin = (getattr(R, "%s_%s" % (i, name)) for i in ("z" if use_x else "b1", "b5", "b6", "fin"))
        gst[name, "far"].wait_recv()
        total = z[c].astype(f32) + b5[0].astype(f32) + b6[...].astype(f32)
        if use_x:
            for t in range(2):
                fin[t, ah] = total[t].astype(bf16)
            s = lambda: fin.at[:, ah]
            gst[name, "x3"] = send(s, s, xside)
        else:
            fin[...] = total.astype(bf16)

    def g_6(name):
        if use_x:
            gst[name, "x3"].wait_recv()
        rows, cols = BLOCK[name]
        getattr(R, name + "_o")[...] = getattr(R, "fin_" + name)[...].reshape(rows, cols)

    def weight(name, rr):
        w = getattr(R, "w_" + name)
        return w[rr // 2, rr % 2].reshape(4 * BLOCK[name][0], BLOCK[name][1])

    R.vecs[c] = R.vec[...]
    R.vecr[r] = R.vec[...]
    vec_cp = [send(R.vec, R.vecs.at[c], (a, r, (c + i) % 4)) for i in range(1, 4)]
    vec_cp += [send(R.vec, R.vecr.at[r], dev) for dev in (core, yside, diag)]
    w_z("qkv")
    for cp in local[1:]:
        cp.wait()
    w_z("og")
    w_f("qkv")
    w_z("up")
    w_f("og")
    w_1("qkv")
    w_z("d0")
    w_1("og")
    w_f("up")
    w_2("qkv")
    w_1("up")
    w_f("d0")
    tok_sends, tok_wait = rows_in(R.tok, R.xo, 0)
    w_2("og")
    w_1("d0")
    w_3("qkv")
    w_2("up")
    for cp in vec_cp:
        cp.wait_recv()

    def vec_row(i):
        return cat([R.vecs[cc, i:i + 1, :] for cc in range(4)])

    tok_wait()

    def xrows():
        return cat([R.xo[cc] for cc in range(4)]).astype(f32)

    def norm_parts(v):
        mean = jnp.sum(v, axis=1, keepdims=True) * (1.0 / D)
        cen = v - mean
        var = jnp.sum(cen * cen, axis=1, keepdims=True) * (1.0 / D)
        inv = lax.rsqrt(var + EPS)
        return cen * inv, inv

    standard, _ = norm_parts(xrows())
    n1 = (standard * vec_row(0) + vec_row(1)).astype(bf16)
    R.n1[...] = n1
    R.xn[pl.ds(lo_row, 128), :] = n1[0:128]
    R.xn[pl.ds(hi_row, 128), :] = n1[128:256]
    R.xn[1024:1280, :] = n1[256:512]
    here = [R.xn.at[pl.ds(lo_row, 128), :], R.xn.at[pl.ds(hi_row, 128), :]]
    to_z = [send(s, s, zside) for s in here]
    to_core = [send(s, s, core) for s in here]
    w_z("d1")
    w_3("og")
    w_2("d0")
    w_4("qkv")
    w_3("up")
    qz = q + 2 - 4 * (q // 2)
    for cp in to_z:
        cp.wait_recv()
    there = [R.xn.at[pl.ds(pl.multiple_of(qz * 128, 128), 128), :],
             R.xn.at[pl.ds(pl.multiple_of((7 - qz) * 128, 128), 128), :]]
    to_core += [send(s, s, core) for s in there]
    w_f("d1")
    for cp in to_core:
        cp.wait_recv()

    def qkv_pair(p):
        w = weight("qkv", p)
        R.qp[p] = (dot(R.n1[...], w[:, 0:128], 1, 0).astype(bf16).astype(f32) * 0.125).astype(bf16)
        R.kv[p] = dot(R.xn[...], w[:, 128:384], 1, 0).astype(bf16)
    loop(4, qkv_pair)
    cot_sends, cot_wait = rows_in(R.cot, R.co, 1)
    w_1("d1")

    lane = lax.broadcasted_iota(jnp.int32, (T, 128), 1)
    key_at = lax.broadcasted_iota(jnp.int32, (512, 128), 0)
    col_at = lax.broadcasted_iota(jnp.int32, (512, 128), 1)
    lo_ok = key_at <= col_at + q * 128
    hi_ok = key_at + 512 <= col_at + (7 - q) * 128
    own_ok = (key_at <= col_at)[0:128]

    def attend_pair(p):
        for h in range(2):
            keys = R.kv[p, :, 0:128]
            vals = R.kv[p, :, 128:256]
            qm = jnp.where(lane // 64 == h, R.qp[p], jnp.zeros((), bf16))
            s1 = dot(keys[0:512], qm, 1, 1)
            s2 = dot(keys[512:1024], qm[128:512], 1, 1)
            sa = jnp.where(own_ok, dot(keys[1024:1152], qm[256:384], 1, 1), MASKED)
            sb = jnp.where(own_ok, dot(keys[1152:1280], qm[384:512], 1, 1), MASKED)
            s1 = cat([jnp.where(lo_ok, s1[:, 0:128], MASKED), s1[:, 128:512]])
            s2 = cat([jnp.where(hi_ok, s2[:, 0:128], MASKED), s2[:, 128:384]])
            top = lambda v: jnp.max(v, axis=0, keepdims=True)
            add = lambda v: jnp.sum(v, axis=0, keepdims=True)
            m1 = top(s1)
            m2 = jnp.maximum(m1[:, 128:512], top(s2))
            m = cat([m1[:, 0:128], m2[:, 0:128], jnp.maximum(m2[:, 128:384], cat([top(sa), top(sb)]))])
            e1 = jnp.exp(s1 - m)
            e2 = jnp.exp(s2 - m[:, 128:512])
            ea = jnp.exp(sa - m[:, 256:384])
            eb = jnp.exp(sb - m[:, 384:512])
            l1 = add(e1)
            l2 = l1[:, 128:512] + add(e2)
            total = cat([l1[:, 0:128], l2[:, 0:128], l2[:, 128:384] + cat([add(ea), add(eb)])])
            e1, e2, ea, eb = (v.astype(bf16) for v in (e1, e2, ea, eb))
            R.p1[2 * p + h] = e1
            R.p2[2 * p + h] = e2
            R.po[2 * p + h, :, 0:128] = ea
            R.po[2 * p + h, :, 128:256] = eb
            o1 = dot(vals[0:512], e1, 0, 0)
            o2 = dot(vals[512:1024], e2, 0, 0)
            oa = dot(vals[1024:1152], ea, 0, 0)
            ob = dot(vals[1152:1280], eb, 0, 0)
            o2 = o1[:, 128:512] + o2
            o = cat([o1[:, 0:128], o2[:, 0:128], o2[:, 128:384] + cat([oa, ob])])
            inv = 1.0 / total
            R.li[p, h:h + 1, :] = inv
            R.att[p, 64 * h:64 * h + 64, :] = (o[64 * h:64 * h + 64] * inv).astype(bf16)
    def attend_step(p):
        attend_pair(p)

        @pl.when(p == 0)
        def _():
            w_3("d0")

        @pl.when(p == 1)
        def _():
            w_2("d1")
    loop(4, attend_step)
    w_4("og")

    def lanes(cc):
        return pl.ds(pl.multiple_of(cc * 128, 128), 128)

    def wide(cc):
        return pl.ds(pl.multiple_of(cc * 256, 256), 256)

    def out_block(cc):
        w = R.w_og[:, :, cc].reshape(512, 256)
        br = dot(R.att[...].reshape(512, T), w, 0, 0)
        ao = br[:, 0:128]
        gate = sigmoid(br[:, 128:256] + R.vecs[cc, 2:3, :])
        R.ao[cc] = ao
        R.g1[cc] = gate
        R.mid[cc] = R.xo[cc].astype(f32) + gate * ao
    loop(4, out_block)

    def midrows():
        return cat([R.mid[cc] for cc in range(4)])

    standard, _ = norm_parts(midrows())
    R.n2[...] = (standard * vec_row(3) + vec_row(4)).astype(bf16)
    w_4("up")

    def up_block(rr):
        pre = dot(R.n2[...], weight("up", rr), 1, 0) + cat([R.vecr[rr, 8 + i:9 + i, :] for i in range(4)])
        s = sigmoid(pre)
        R.hid[rr] = (pre * s).astype(bf16)
        R.slp[rr] = (s * (1.0 + pre * (1.0 - s))).astype(bf16)
    loop(4, up_block)
    w_3("d1")
    w_4("d0")
    w_4("d1")
    cot_wait()

    def down_block(cc):
        br = 0.0
        for rr in range(4):
            for j in range(2):
                w = getattr(R, "w_d%d" % j)[rr // 2, rr % 2, cc].reshape(256, 256)
                br = br + dot(R.hid[rr, :, 256 * j:256 * j + 256], w, 1, 0)
        ffn = br[:, 0:128] + R.vecs[cc, 5:6, :]
        gate = sigmoid(br[:, 128:256] + R.vecs[cc, 6:7, :])
        R.out[cc] = (R.mid[cc] + gate * ffn).astype(bf16)
        g = R.co[cc].astype(f32)
        gf = (g * gate).astype(bf16)
        gg = (g * ffn * gate * (1.0 - gate)).astype(bf16)
        R.pair[:, wide(cc)] = cat([gf, gg])
        R.svb[pl.ds(12 + cc, 1), :] = jnp.sum(gf.astype(f32), axis=0, keepdims=True)
        R.svb[pl.ds(16 + cc, 1), :] = jnp.sum(gg.astype(f32), axis=0, keepdims=True)
    loop(4, down_block)
    out_sends, out_wait = rows_out(R.out, R.out_o, 2)

    def grad_down(j, kk):
        for yy in range(2):
            g = dot(R.hid[2 * yy + kk, :, 256 * j:256 * j + 256], R.pair[...], 0, 0).astype(bf16)
            for cc in range(4):
                getattr(R, "g_d%d" % j)[yy, kk, cc] = g[:, 256 * cc:256 * cc + 256].reshape(2, 2, 64, 256)
    for j in range(2):
        grad_down(j, 1 - k)
        g_0("d%d" % j)
        grad_down(j, k)
    g_1("d0")

    def back_up(rr):
        gh = 0.0
        for cc in range(4):
            w = [getattr(R, "w_d%d" % j)[rr // 2, rr % 2, cc].reshape(256, 256) for j in range(2)]
            gh = gh + dot(R.pair[:, 256 * cc:256 * cc + 256], cat(w, 0), 1, 1)
        gp = (gh * R.slp[rr].astype(f32)).astype(bf16)
        R.slp[rr] = gp
        tot = jnp.sum(gp.astype(f32), axis=0, keepdims=True)
        for i in range(4):
            R.svb[pl.ds(20 + 4 * rr + i, 1), :] = tot[:, 128 * i:128 * i + 128]
    loop(4, back_up)
    g_1("d1")

    def grad_up(yy, kk):
        g = dot(R.n2[...], R.slp[2 * yy + kk], 0, 0).astype(bf16)
        R.g_up[yy, kk] = g.reshape(4, 2, 2, 32, 512)
    grad_up(0, 1 - k)
    grad_up(1, 1 - k)
    g_0("up")
    grad_up(0, k)
    grad_up(1, k)

    gn = dot(R.slp[0], weight("up", 0), 1, 1)
    for rr in range(1, 4):
        gn = gn + dot(R.slp[rr], weight("up", rr), 1, 1)

    def norm_back(v, grad, gain_row):
        std, inv = norm_parts(v)
        gs = jnp.sum(grad * std, axis=0, keepdims=True)
        gb = jnp.sum(grad, axis=0, keepdims=True)
        s = grad * vec_row(gain_row)
        f = jnp.sum(s, axis=1, keepdims=True) * (1.0 / D)
        e = jnp.sum(s * std, axis=1, keepdims=True) * (1.0 / D)
        return inv * (s - f - std * e), gs, gb

    def put_sums(to, gs, gb):
        for cc in range(4):
            to[cc:cc + 1, :] = gs[:, 128 * cc:128 * cc + 128]
            to[4 + cc:5 + cc, :] = gb[:, 128 * cc:128 * cc + 128]

    def small_1(v, parts):
        parts[c] = v[...]
        return [send(v, lambda: parts.at[c], (a, r, cc)) for cc in others]

    def small_2(sent, parts, mine, alls):
        for cp in sent:
            cp.wait_recv()
        mine[...] = (parts[0] + parts[1]) + (parts[2] + parts[3])
        alls[slot] = mine[...]
        return [send(mine, lambda: alls.at[slot], dev) for dev in corners]

    def small_3(sent, alls, total):
        for cp in sent:
            cp.wait_recv()
        v = alls[0]
        for i in range(1, 8 if use_x else 4):
            v = v + alls[i]
        total[...] = v

    gm, gs, gb = norm_back(midrows(), gn, 3)
    put_sums(R.svb, gs, gb)
    for cc in range(4):
        g_mid = R.co[cc].astype(f32) + gm[:, 128 * cc:128 * cc + 128]
        R.gm[cc] = g_mid
        gate = R.g1[cc]
        ga = (g_mid * gate).astype(bf16)
        gg = (g_mid * R.ao[cc] * gate * (1.0 - gate)).astype(bf16)
        R.pair[:, 256 * cc:256 * cc + 256] = cat([ga, gg])
        R.svb[8 + cc:9 + cc, :] = jnp.sum(gg.astype(f32), axis=0, keepdims=True)
    g_2("d0")
    g_1("up")

    def grad_out(cc):
        R.g_og[:, :, cc] = dot(R.att[...].reshape(512, T), R.pair[:, wide(cc)], 1, 0).astype(bf16).reshape(2, 2, 2, 2, 32, 256)
    loop(4, grad_out)
    g_0("og")
    do = 0.0
    for cc in range(4):
        do = do + dot(R.w_og[:, :, cc].reshape(512, 256), R.pair[:, 256 * cc:256 * cc + 256], 1, 1)
    for cc in range(4):
        R.mid[cc] = do[:, 128 * cc:128 * cc + 128]
    for i in range(2):
        R.hid[i] = R.xn[512 * i:512 * i + 512, :].T
    R.hid[2, :, 0:256] = R.xn[1024:1280, :].T
    R.hid[3] = R.n1[...].T
    g_1("og")
    svb_1 = small_1(R.svb, R.svb_parts)

    row_of = lax.broadcasted_iota(jnp.int32, (128, T), 0)

    def back_pair(p):
        rows = pl.ds(pl.multiple_of(p * 128, 128), 128)
        dot_t = cat([R.mid[cc, rows, :] for cc in range(4)])
        dot_t = dot_t * jnp.where(row_of < 64, R.li[p, 0:1, :], R.li[p, 1:2, :])
        prod = dot_t * R.att[p].astype(f32)
        dot_t = dot_t.astype(bf16)
        dot_n = dot_t.T
        keys = R.kv[p, :, 0:128]
        vals = R.kv[p, :, 128:256]
        grads = []
        queries = []
        for h in range(2):
            delta = jnp.sum(prod[64 * h:64 * h + 64], axis=0, keepdims=True)
            qm = jnp.where(lane // 64 == h, R.qp[p], jnp.zeros((), bf16))
            om = jnp.where(lane // 64 == h, dot_n, jnp.zeros((), bf16))
            omt = jnp.where(row_of // 64 == h, dot_t, jnp.zeros((), bf16))
            e1, e2 = R.p1[2 * p + h], R.p2[2 * p + h]
            ea, eb = R.po[2 * p + h, :, 0:128], R.po[2 * p + h, :, 128:256]
            d1 = (e1.astype(f32) * (dot(vals[0:512], omt, 1, 0) - delta)).astype(bf16)
            d2 = (e2.astype(f32) * (dot(vals[512:1024], omt[:, 128:512], 1, 0) - delta[:, 128:512])).astype(bf16)
            da = (ea.astype(f32) * (dot(vals[1024:1152], omt[:, 256:384], 1, 0) - delta[:, 256:384])).astype(bf16)
            db = (eb.astype(f32) * (dot(vals[1152:1280], omt[:, 384:512], 1, 0) - delta[:, 384:512])).astype(bf16)
            dk = cat([dot(d1, qm, 1, 0), dot(d2, qm[128:512], 1, 0), dot(da, qm[256:384], 1, 0), dot(db, qm[384:512], 1, 0)], 0)
            dv = cat([dot(e1, om, 1, 0), dot(e2, om[128:512], 1, 0), dot(ea, om[256:384], 1, 0), dot(eb, om[384:512], 1, 0)], 0)
            grads.append((dk, dv))
            x1 = dot(keys[0:512], d1, 0, 0)
            x2 = x1[:, 128:512] + dot(keys[512:1024], d2, 0, 0)
            xab = cat([dot(keys[1024:1152], da, 0, 0), dot(keys[1152:1280], db, 0, 0)])
            dq = cat([x1[:, 0:128], x2[:, 0:128], x2[:, 128:384] + xab])
            queries.append(dq[64 * h:64 * h + 64])
        R.kv[p, :, 0:128] = (grads[0][0] + grads[1][0]).astype(bf16)
        R.kv[p, :, 128:256] = (grads[0][1] + grads[1][1]).astype(bf16)
        R.qp[p] = (cat(queries, 0) * 0.125).astype(bf16).T
        gk = dot(R.hid[0], R.kv[p, 0:512, :], 1, 0) + dot(R.hid[1], R.kv[p, 512:1024, :], 1, 0)
        gk = gk + dot(R.hid[2, :, 0:256], R.kv[p, 1024:1280, :], 1, 0)
        g = cat([dot(R.hid[3], R.qp[p], 1, 0), gk]).astype(bf16)
        R.g_qkv[p // 2, p % 2] = g.reshape(4, 2, 2, 32, 384)

    def qkv_copy(yy):
        return pltpu.make_async_remote_copy(
            src_ref=R.g_qkv.at[yy, 1 - k], dst_ref=R.b0_qkv.at[yy], send_sem=R.qsem.at[0, yy], recv_sem=R.qsem.at[1, yy],
            device_id=core, device_id_type=MESH)

    def back_step(p):
        back_pair(p)

        @pl.when(p % 2 != k)
        def _():
            qkv_copy(p // 2).start()

        @pl.when(p == 0)
        def _():
            g_2("d1")

        @pl.when(p == 1)
        def _():
            g_3("d0")
    loop(4, back_step)
    g_2("up")
    g_4("d0")

    def back_rows(first, count):
        rows = pl.ds(first, count)
        total = dot(R.kv[0, rows, :], weight("qkv", 0)[:, 128:384], 1, 1)
        for p in range(1, 4):
            total = total + dot(R.kv[p, rows, :], weight("qkv", p)[:, 128:384], 1, 1)
        return total

    def chunk_rows(qq):
        return (pl.multiple_of(qq * 128, 128), pl.multiple_of((7 - qq) * 128, 128))

    q1 = q + 1 - 2 * k
    q2 = qz
    q3 = q2 + 1 - 2 * k
    for i, row in enumerate(chunk_rows(q1)):
        R.ex[0, 128 * i:128 * i + 128, :] = back_rows(row, 128).astype(bf16)
    for i, row in enumerate(chunk_rows(q3)):
        R.ex[1, 128 * i:128 * i + 128, :] = back_rows(row, 128).astype(bf16)
    part_core = send(R.ex, R.exr, core)
    for yy in range(2):
        qkv_copy(yy).wait_recv()
    g_2("og")
    g_1("qkv")
    svb_2 = small_2(svb_1, R.svb_parts, R.svb_mine, R.svb_all)
    mine2 = [back_rows(row, 128) for row in chunk_rows(q2)]
    part_core.wait_recv()
    for i in range(2):
        R.ez[128 * i:128 * i + 128, :] = (mine2[i] + R.exr[1, 128 * i:128 * i + 128, :].astype(f32)).astype(bf16)
    part_z = send(R.ez, R.ezr, zside)

    def x_rows(at, n):
        return cat([R.xo[cc, at:at + n, :] for cc in range(4)]).astype(f32)

    def own_rows(row, n, at):
        own = back_rows(row, n)
        for cc in range(4):
            R.mid[cc, at:at + n, :] = own[:, 128 * cc:128 * cc + 128]

    def add_queries(p):
        more = dot(R.qp[p], weight("qkv", p)[:, 0:128], 1, 1)
        for cc in range(4):
            R.mid[cc] = R.mid[cc] + more[:, 128 * cc:128 * cc + 128]

    def to_input(at, n):
        gx, gs, gb = norm_back(x_rows(at, n), cat([R.mid[cc, at:at + n, :] for cc in range(4)]), 0)
        for cc in range(4):
            R.ing[cc, at:at + n, :] = (R.gm[cc, at:at + n, :] + gx[:, 128 * cc:128 * cc + 128]).astype(bf16)
        return gs, gb

    own_rows(lo_row, 128, 0)
    own_rows(hi_row, 128, 128)
    own_rows(1024, 256, 256)
    loop(4, add_queries)
    g_3("d1")
    gs2, gb2 = to_input(256, 256)
    g_3("up")
    ing_sends2, _ = rows_out(R.ing, R.ing_o, 3, (2,))
    g_5("d0")
    g_3("og")
    g_4("d1")
    part_z.wait_recv()
    for cc in range(4):
        here = slice(128 * cc, 128 * cc + 128)
        R.mid[cc, 0:256, :] = R.mid[cc, 0:256, :] + (R.exr[0, :, here].astype(f32) + R.ezr[:, here].astype(f32))
    gs, gb = to_input(0, 256)
    put_sums(R.sva, gs + gs2, gb + gb2)
    sva_1 = small_1(R.sva, R.sva_parts)
    ing_sends, ing_wait = rows_out(R.ing, R.ing_o, 3, (0, 1))
    g_2("qkv")
    g_4("up")

    sva_2 = small_2(sva_1, R.sva_parts, R.sva_mine, R.sva_all)
    g_5("d1")
    g_4("og")
    g_3("qkv")
    g_5("up")
    g_5("og")
    g_4("qkv")
    small_3(svb_2, R.svb_all, R.svb_total)
    small_3(sva_2, R.sva_all, R.sva_total)
    R.small_o[...] = jnp.zeros((16, 128), f32)
    for i in range(2):
        R.small_o[i:i + 1, :] = R.sva_total[pl.ds(4 * i + c, 1), :]
    for i in range(5):
        R.small_o[2 + i:3 + i, :] = R.svb_total[pl.ds(4 * i + c, 1), :]
    for i in range(4):
        R.small_o[8 + i:9 + i, :] = R.svb_total[pl.ds(20 + 4 * r + i, 1), :]
    g_5("qkv")
    for name in NAMES:
        g_6(name)

    out_wait()
    ing_wait()
    for yy in range(2):
        qkv_copy(yy).wait_send()
    for cp in pending:
        cp.wait_send()
    for sends in (tok_sends, cot_sends, out_sends, ing_sends2, ing_sends):
        finish_sends(sends)


def body(use_x, tokens, cotangent, norm1_gain, norm1_bias, qkv_weight, out_weight, gate1_weight,
         gate1_bias, norm2_gain, norm2_bias, up_weight, up_bias, down_weight, down_bias,
         gate2_weight, gate2_bias):
    hbm = pl.BlockSpec(memory_space=pl.ANY)
    vmem = pl.BlockSpec(memory_space=pltpu.VMEM)
    ins = {"tok": tokens, "cot": cotangent, "i_qkv": qkv_weight, "i_out": out_weight, "i_gate1": gate1_weight,
           "i_up": up_weight, "i_down": down_weight, "i_gate2": gate2_weight,
           "norm1_gain": norm1_gain, "norm1_bias": norm1_bias, "gate1_bias": gate1_bias, "norm2_gain": norm2_gain,
           "norm2_bias": norm2_bias, "down_bias": down_bias, "gate2_bias": gate2_bias, "up_bias": up_bias}
    outs = {"out_o": ((2048, 128), bf16, hbm), "ing_o": ((2048, 128), bf16, hbm)}
    for name in NAMES:
        outs[name + "_o"] = (BLOCK[name], bf16, vmem)
    outs["small_o"] = ((16, 128), f32, vmem)
    scr = {}
    for name in NAMES:
        rows, cols = BLOCK[name]
        rq = rows // 4
        scr["w_" + name] = ((2, 2, 4, 2, 2, rq, cols), bf16)
        scr["g_" + name] = ((2, 2, 4, 2, 2, rq, cols), bf16)
        scr["b0_" + name] = ((2, 4, 2, 2, rq, cols), bf16)
        if use_x:
            scr["b1_" + name] = ((4, 2, rq, cols), bf16)
            scr["b2_" + name] = ((2, 4, rq, cols), bf16)
            scr["b3_" + name] = ((4, rq, cols), bf16)
            scr["b4_" + name] = ((4, rq, cols), bf16)
            scr["z_" + name] = ((4, 2, rq, cols), bf16)
            scr["b5_" + name] = ((2, 2, rq, cols), bf16)
            scr["b6_" + name] = ((2, rq, cols), bf16)
        else:
            scr["b1_" + name] = ((4, 2, 2, rq, cols), bf16)
            scr["b5_" + name] = ((2, 2, 2, rq, cols), bf16)
            scr["b6_" + name] = ((2, 2, rq, cols), bf16)
        scr["fin_" + name] = ((2, 2, rq, cols), bf16)
    scr.update({
        "qstage": ((128, 384), bf16), "vec": ((16, 128), f32), "vecs": ((4, 16, 128), f32), "vecr": ((4, 16, 128), f32),
        "xo": ((4, T, 128), bf16), "co": ((4, T, 128), bf16), "n1": ((T, D), bf16),
        "xn": ((1280, D), bf16), "qp": ((4, T, 128), bf16), "kv": ((4, 1280, 256), bf16),
        "p1": ((8, 512, 512), bf16), "p2": ((8, 512, 384), bf16), "po": ((8, 128, 256), bf16),
        "li": ((4, 8, T), f32), "att": ((4, 128, T), bf16), "ao": ((4, T, 128), f32),
        "g1": ((4, T, 128), f32), "mid": ((4, T, 128), f32), "n2": ((T, D), bf16),
        "hid": ((4, T, 512), bf16), "slp": ((4, T, 512), bf16), "out": ((4, T, 128), bf16),
        "pair": ((T, 1024), bf16), "gm": ((4, T, 128), f32), "ing": ((4, T, 128), bf16),
        "ex": ((2, 256, D), bf16), "exr": ((2, 256, D), bf16), "ez": ((256, D), bf16), "ezr": ((256, D), bf16),
        "sva": ((8, 128), f32), "sva_parts": ((4, 8, 128), f32), "sva_mine": ((8, 128), f32), "sva_total": ((8, 128), f32), "sva_all": ((8, 8, 128), f32),
        "svb": ((40, 128), f32), "svb_parts": ((4, 40, 128), f32), "svb_mine": ((40, 128), f32), "svb_total": ((40, 128), f32), "svb_all": ((8, 40, 128), f32),
    })
    shapes = [pltpu.VMEM(s, d) for s, d in scr.values()]
    names_scr = tuple(scr) + ("ssem", "rsem", "issem", "irsem", "lsem", "qsem")
    n_sem = 160
    dma = pltpu.SemaphoreType.DMA
    shapes += [dma((n_sem,)), dma((n_sem,)), dma((4, 4, 3)), dma((4, 4, 3)), dma((20,)), dma((2, 2))]
    res = pl.pallas_call(
        partial(kernel, use_x, tuple(ins), tuple(outs), names_scr),
        out_shape=[jax.ShapeDtypeStruct(s, d) for s, d, _ in outs.values()],
        in_specs=[hbm] * 8 + [vmem] * 8,
        out_specs=[sp for _, _, sp in outs.values()],
        scratch_shapes=shapes,
        compiler_params=pltpu.CompilerParams(collective_id=0, has_side_effects=True, vmem_limit_bytes=60 * 1024 * 1024),
    )(*ins.values())
    if not use_x:
        summed = lax.psum(tuple(v.astype(f32) for v in res[2:]), "grp")
        res = list(res[:2]) + list(summed)
    flat = {"out": (2048, 128), "ing": (2048, 128), "n1g": (128,), "n1b": (128,), "qkv": (128, 384),
            "w_out": (128, 128), "w_gate1": (128, 128), "g1b": (128,), "n2g": (128,), "n2b": (128,),
            "up": (128, 512), "upb": (512,), "w_down": (512, 128), "db": (128,), "w_gate2": (512, 128), "g2b": (128,)}
    kinds = {name: bf16 if name in ("out", "ing") else f32 for name in flat}
    return pl.pallas_call(
        finish,
        out_shape=[jax.ShapeDtypeStruct(shape, kinds[name]) for name, shape in flat.items()],
        in_specs=[vmem] * 8,
        out_specs=[vmem] * 16,
    )(*res)


def finish(out_i, ing_i, qkv_i, og_i, up_i, d0_i, d1_i, small_i, out, ing, n1g, n1b, qkv, w_out, w_gate1, g1b, n2g, n2b,
           up, upb, w_down, db, w_gate2, g2b):
    out[...] = out_i[...]
    ing[...] = ing_i[...]
    g = qkv_i[...].astype(f32)
    qkv[...] = cat([g[:, (2 * j + h) * 64:(2 * j + h + 1) * 64] for h in range(2) for j in range(3)])
    w_out[...] = og_i[:, 0:128].astype(f32)
    w_gate1[...] = og_i[:, 128:256].astype(f32)
    up[...] = up_i[...].astype(f32)
    w_down[0:256, :] = d0_i[:, 0:128].astype(f32)
    w_down[256:512, :] = d1_i[:, 0:128].astype(f32)
    w_gate2[0:256, :] = d0_i[:, 128:256].astype(f32)
    w_gate2[256:512, :] = d1_i[:, 128:256].astype(f32)
    for i, ref in enumerate((n1g, n1b, n2g, n2b, g1b, db, g2b)):
        ref[...] = small_i[i:i + 1, :].reshape(128)
    for i in range(4):
        upb[128 * i:128 * i + 128] = small_i[8 + i:9 + i, :].reshape(128)


def solution(mesh):
    act = P(("grp", "row"), "col")
    col, row = P("col"), P("row")
    cr, rc = P("col", "row"), P("row", "col")
    return jax.shard_map(
        partial(body, mesh.shape["grp"] == 2),
        mesh=mesh,
        in_specs=(act, act, col, col, cr, rc, rc, col, col, col, cr, row, rc, col, rc, col),
        out_specs=(act, act, col, col, cr, rc, rc, col, col, col, cr, row, rc, col, rc, col),
        check_vma=False,
    )
```

```python
from functools import partial

import jax
import jax.numpy as jnp
from jax import lax
from jax.experimental import pallas as pl
from jax.experimental.pallas import tpu as pltpu
from jax.sharding import PartitionSpec as P

bf16 = jnp.bfloat16
f32 = jnp.float32
EPS = 1e-05
MASKED = -1e30
MESH = pl.DeviceIdType.MESH

T = 512
D = 512
BLOCK = {"qkv": (128, 384), "og": (128, 256), "up": (128, 512), "d0": (256, 256), "d1": (256, 256)}
NAMES = ("qkv", "og", "up", "d0", "d1")
VECTORS = ("norm1_gain", "norm1_bias", "gate1_bias", "norm2_gain", "norm2_bias", "down_bias", "gate2_bias")


def dot(a, b, ca, cb):
    return lax.dot_general(a, b, (((ca,), (cb,)), ((), ())), preferred_element_type=f32)


def loop(count, step):
    lax.fori_loop(0, count, lambda i, z: (step(i), z)[1], 0)


def cat(parts, axis=1):
    return jnp.concatenate(parts, axis=axis)


class Waiter:
    def __init__(self, make):
        self.make = make

    def wait_recv(self):
        self.make().wait_recv()

    def wait_send(self):
        self.make().wait_send()


def sigmoid(v):
    return 1.0 / (1.0 + jnp.exp(-v))


def kernel(use_x, names_in, names_out, names_scr, *refs):
    ref = dict(zip(names_in + names_out + names_scr, refs))
    R = type("R", (), ref)
    a = lax.axis_index("grp")
    r = lax.axis_index("row")
    c = lax.axis_index("col")
    y, k = r // 2, r % 2
    ah = a % 2
    q = 2 * (c % 2) + k
    y_, k_, a_ = 1 - y, 1 - k, 1 - ah
    c_far = lax.rem(c + 2, 4)
    c_near = c + 1 - 2 * (c % 2)
    c_across = lax.rem(c_near + 2, 4)
    slot = 4 * ah + r if use_x else r
    others = [lax.rem(c + i, 4) for i in range(1, 4)]
    core = (a, 2 * y + 1 - k, c)
    yside = (a, 2 * (1 - y) + k, c)
    xside = (a + 1 - 2 * ah, r, c)
    zside = (a, r, c + 1 - 2 * (c % 2))
    owner_row = 2 * y + c // 2
    lo_row = pl.multiple_of(q * 128, 128)
    hi_row = pl.multiple_of((7 - q) * 128, 128)

    counter = [0]
    pending = []

    def send(src, dst, dev):
        i = counter[0]
        counter[0] += 1

        def make():
            return pltpu.make_async_remote_copy(
                src_ref=src() if callable(src) else src, dst_ref=dst() if callable(dst) else dst,
                send_sem=R.ssem.at[i], recv_sem=R.rsem.at[i], device_id=dev, device_id_type=MESH)
        make().start()
        pending.append(Waiter(make))
        return pending[-1]

    local = []

    def fetch(src, dst):
        cp = pltpu.make_async_copy(src, dst, R.lsem.at[len(local)])
        cp.start()
        local.append(cp)

    fetch(R.i_qkv, R.qstage)
    for t in range(2):
        for name, sources, skip in (("og", ("out", "gate1"), 0), ("up", ("up",), 0),
                                    ("d0", ("down", "gate2"), 0), ("d1", ("down", "gate2"), 256)):
            rows, cols = BLOCK[name]
            rq = rows // 4
            w = getattr(R, "w_" + name)
            width = cols // len(sources)
            for j, s in enumerate(sources):
                at = pl.multiple_of((2 * t + ah) * rq + skip, 32)
                fetch(getattr(R, "i_" + s).at[pl.ds(at, rq), :],
                      w.at[y, k, c, t, ah, :, pl.ds(j * width, width)])

    barrier = pltpu.get_barrier_semaphore()
    for kk in range(2):
        for cc in range(4):
            me = (k == kk) & (c == cc)

            @pl.when(jnp.logical_not(me))
            def _():
                pl.semaphore_signal(barrier, inc=1, device_id=(a, 2 * y + kk, cc), device_id_type=MESH)
    diag = (a, 2 * (1 - y) + 1 - k, c)
    corners = [(g, rr, c) for g in ((a, a + 1 - 2 * ah) if use_x else (a,))
               for rr in (r, 2 * y + 1 - k, 2 * (1 - y) + k, 2 * (1 - y) + 1 - k)][1:]
    for dev in (corners[1:] if use_x else corners[1:] + [xside]):
        pl.semaphore_signal(barrier, inc=1, device_id=dev, device_id_type=MESH)

    local[0].wait()
    for t in range(2):
        blk = R.qstage[pl.ds(pl.multiple_of((2 * t + ah) * 32, 32), 32), :].astype(f32)
        parts = [blk[:, (3 * h + j) * 64:(3 * h + j + 1) * 64] for j in range(3) for h in range(2)]
        R.w_qkv[y, k, c, t, ah] = cat(parts).astype(bf16)
    R.vec[...] = jnp.zeros((16, 128), f32)
    R.svb[32:40, :] = jnp.zeros((8, 128), f32)
    for i, name in enumerate(VECTORS):
        R.vec[i:i + 1, :] = getattr(R, name)[...].astype(f32).reshape(1, 128)
    for i in range(4):
        R.vec[8 + i:9 + i, :] = R.up_bias[128 * i:128 * i + 128].astype(f32).reshape(1, 128)
    pl.semaphore_wait(barrier, 13 if use_x else 10)

    def rows_in(src, dst, which):
        sends = []
        for qq in range(4):
            kq, cq = qq % 2, 2 * k + qq // 2
            me = (k == kq) & (c == cq)
            for j, (s0, d0, n) in enumerate(((qq * 128, 0, 128), ((7 - qq) * 128, 128, 128), ((8 + 2 * qq) * 128, 256, 256))):
                s = src.at[pl.ds(s0, n), :]
                d = dst.at[c, pl.ds(d0, n), :]
                rs = R.irsem.at[which, c, j]
                cp = pltpu.make_async_remote_copy(
                    src_ref=s, dst_ref=d, send_sem=R.issem.at[which, qq, j], recv_sem=rs,
                    device_id=(a, 2 * y + kq, cq), device_id_type=MESH)
                sends.append((me, cp))

                @pl.when(jnp.logical_not(me))
                def _():
                    cp.start()

                @pl.when(me)
                def _():
                    pltpu.make_async_copy(s, d, rs).start()

        def wait():
            for cc in range(4):
                for j, (d0, n) in enumerate(((0, 128), (128, 128), (256, 256))):
                    d = dst.at[cc, pl.ds(d0, n), :]
                    pltpu.make_async_copy(d, d, R.irsem.at[which, cc, j]).wait()
        return sends, wait

    def rows_out(src, dst, which, only=(0, 1, 2)):
        sends = []
        for cc in range(4):
            me = (c // 2 == k) & (c == cc)
            for j, (s0, d0, n) in enumerate(((0, lo_row, 128), (128, hi_row, 128), (256, 1024 + pl.multiple_of(q * 256, 256), 256))):
                if j not in only:
                    continue
                s = src.at[cc, pl.ds(s0, n), :]
                d = dst.at[pl.ds(d0, n), :]
                rs = R.irsem.at[which, q, j]
                cp = pltpu.make_async_remote_copy(
                    src_ref=s, dst_ref=d, send_sem=R.issem.at[which, cc, j], recv_sem=rs,
                    device_id=(a, owner_row, cc), device_id_type=MESH)
                sends.append((me, cp))

                @pl.when(jnp.logical_not(me))
                def _():
                    cp.start()

                @pl.when(me)
                def _():
                    pltpu.make_async_copy(s, d, rs).start()

        def wait():
            for qq in range(4):
                for j, (d0, n) in enumerate(((qq * 128, 128), ((7 - qq) * 128, 128), ((8 + 2 * qq) * 128, 256))):
                    d = dst.at[pl.ds(d0, n), :]
                    pltpu.make_async_copy(d, d, R.irsem.at[which, qq, j]).wait()
        return sends, wait

    def finish_sends(sends):
        for me, cp in sends:
            @pl.when(jnp.logical_not(me))
            def _():
                cp.wait_send()

    wst = {}

    def w_z(name):
        w = getattr(R, "w_" + name)
        here = lambda: w.at[y, k, c, :, ah]
        wst[name, "far"] = send(here, here, (a, r, c_far))
        wst[name, "near"] = send(here, here, zside)

    def w_f(name):
        w = getattr(R, "w_" + name)
        wst[name, "far"].wait_recv()
        here = lambda: w.at[y, k, c_far, :, ah]
        wst[name, "on"] = send(here, here, zside)

    def to_sibling(name, s):
        wst.setdefault((name, "core"), []).append(send(s, s, core))

    def w_1(name):
        w = getattr(R, "w_" + name)
        wst[name, "near"].wait_recv()
        wst[name, "on"].wait_recv()
        s = lambda: w.at[y, k, :, 0, ah]
        wst[name, "x1"] = send(s, s, xside)
        s = lambda: w.at[y, k, :, 1, ah]
        wst[name, "y1"] = send(s, s, yside)
        to_sibling(name, lambda: w.at[y, k, :, :, ah])

    def w_2(name):
        w = getattr(R, "w_" + name)
        wst[name, "x1"].wait_recv()
        s = lambda: w.at[y, k, :, 0]
        wst[name, "y2"] = send(s, s, yside)
        to_sibling(name, lambda: w.at[y, k, :, 0, a_])
        wst[name, "y1"].wait_recv()
        s = lambda: w.at[:, k, :, 1, ah]
        wst[name, "x2"] = send(s, s, xside)
        to_sibling(name, lambda: w.at[y_, k, :, 1, ah])

    def w_3(name):
        w = getattr(R, "w_" + name)
        wst[name, "y2"].wait_recv()
        to_sibling(name, lambda: w.at[y_, k, :, 0])
        wst[name, "x2"].wait_recv()
        to_sibling(name, lambda: w.at[:, k, :, 1, a_])

    def w_4(name):
        for cp in wst[name, "core"]:
            cp.wait_recv()

    gst = {}

    def g_0(name):
        g, b0 = getattr(R, "g_" + name), getattr(R, "b0_" + name)
        gst[name, "core"] = send(lambda: g.at[:, k_], b0, core)

    def g_1(name):
        g, b0, b1 = getattr(R, "g_" + name), getattr(R, "b0_" + name), getattr(R, "b1_" + name)
        if name != "qkv":
            gst[name, "core"].wait_recv()

        def one(i):
            yy, cc = i // 4, i % 4
            b0[yy, cc] = (b0[yy, cc].astype(f32) + g[yy, k, cc].astype(f32)).astype(bf16)
        loop(8, one)
        if use_x:
            b2 = getattr(R, "b2_" + name)
            gst[name, "y1"] = send(lambda: b0.at[y_, :, 0], b1, yside)
            gst[name, "x1"] = send(lambda: b0.at[:, :, 1, a_], b2, xside)
        else:
            gst[name, "y1"] = send(lambda: b0.at[y_], b1, yside)

    def g_2(name):
        b0, b1 = getattr(R, "b0_" + name), getattr(R, "b1_" + name)
        gst[name, "y1"].wait_recv()
        if not use_x:
            def one(cc):
                b1[cc] = (b1[cc].astype(f32) + b0[y, cc].astype(f32)).astype(bf16)
            loop(4, one)
            return
        b2, b3, b4 = (getattr(R, "b%d_%s" % (i, name)) for i in (2, 3, 4))

        def one(cc):
            b1[cc] = (b1[cc].astype(f32) + b0[y, cc, 0].astype(f32)).astype(bf16)
        loop(4, one)
        gst[name, "x2"] = send(lambda: b1.at[:, a_], b3, xside)
        gst[name, "x1"].wait_recv()

        def two(i):
            yy, cc = i // 4, i % 4
            b2[yy, cc] = (b2[yy, cc].astype(f32) + b0[yy, cc, 1, ah].astype(f32)).astype(bf16)
        loop(8, two)
        gst[name, "y2"] = send(lambda: b2.at[y_], b4, yside)

    def g_3(name):
        b1, z, b5 = (getattr(R, "%s_%s" % (i, name)) for i in ("b1", "z" if use_x else "b1", "b5"))
        if use_x:
            b2, b3, b4 = (getattr(R, "b%d_%s" % (i, name)) for i in (2, 3, 4))
            gst[name, "x2"].wait_recv()
            gst[name, "y2"].wait_recv()

            def one(cc):
                z[cc, 0] = (b1[cc, ah].astype(f32) + b3[cc].astype(f32)).astype(bf16)
                z[cc, 1] = (b2[y, cc].astype(f32) + b4[cc].astype(f32)).astype(bf16)
            loop(4, one)
        gst[name, "near"] = [send(lambda cc=cc: z.at[cc], lambda i=i: b5.at[i], zside) for i, cc in enumerate((c_near, c_across))]

    def g_4(name):
        z, b5, b6 = (getattr(R, "%s_%s" % (i, name)) for i in ("z" if use_x else "b1", "b5", "b6"))
        for cp in gst[name, "near"]:
            cp.wait_recv()
        b5[1] = (b5[1].astype(f32) + z[c_far].astype(f32)).astype(bf16)
        gst[name, "far"] = send(lambda: b5.at[1], b6, (a, r, c_far))

    def g_5(name):
        z, b5, b6, fin = (getattr(R, "%s_%s" % (i, name)) for i in ("z" if use_x else "b1", "b5", "b6", "fin"))
        gst[name, "far"].wait_recv()
        total = z[c].astype(f32) + b5[0].astype(f32) + b6[...].astype(f32)
        if use_x:
            for t in range(2):
                fin[t, ah] = total[t].astype(bf16)
            s = lambda: fin.at[:, ah]
            gst[name, "x3"] = send(s, s, xside)
        else:
            fin[...] = total.astype(bf16)

    def g_6(name):
        if use_x:
            gst[name, "x3"].wait_recv()
        rows, cols = BLOCK[name]
        getattr(R, name + "_o")[...] = getattr(R, "fin_" + name)[...].reshape(rows, cols)

    def weight(name, rr):
        w = getattr(R, "w_" + name)
        return w[rr // 2, rr % 2].reshape(4 * BLOCK[name][0], BLOCK[name][1])

    R.vecs[c] = R.vec[...]
    R.vecr[r] = R.vec[...]
    vec_cp = [send(R.vec, R.vecs.at[c], (a, r, (c + i) % 4)) for i in range(1, 4)]
    vec_cp += [send(R.vec, R.vecr.at[r], dev) for dev in (core, yside, diag)]
    w_z("qkv")
    for cp in local[1:]:
        cp.wait()
    w_z("og")
    w_f("qkv")
    w_z("up")
    w_f("og")
    w_1("qkv")
    w_z("d0")
    w_1("og")
    w_f("up")
    w_2("qkv")
    w_1("up")
    w_f("d0")
    tok_sends, tok_wait = rows_in(R.tok, R.xo, 0)
    w_2("og")
    w_1("d0")
    w_3("qkv")
    w_2("up")
    for cp in vec_cp:
        cp.wait_recv()

    def vec_row(i):
        return cat([R.vecs[cc, i:i + 1, :] for cc in range(4)])

    tok_wait()

    def xrows():
        return cat([R.xo[cc] for cc in range(4)]).astype(f32)

    def norm_parts(v):
        mean = jnp.sum(v, axis=1, keepdims=True) * (1.0 / D)
        cen = v - mean
        var = jnp.sum(cen * cen, axis=1, keepdims=True) * (1.0 / D)
        inv = lax.rsqrt(var + EPS)
        return cen * inv, inv

    standard, _ = norm_parts(xrows())
    n1 = (standard * vec_row(0) + vec_row(1)).astype(bf16)
    R.n1[...] = n1
    R.xn[pl.ds(lo_row, 128), :] = n1[0:128]
    R.xn[pl.ds(hi_row, 128), :] = n1[128:256]
    R.xn[1024:1280, :] = n1[256:512]
    here = [R.xn.at[pl.ds(lo_row, 128), :], R.xn.at[pl.ds(hi_row, 128), :]]
    to_z = [send(s, s, zside) for s in here]
    to_core = [send(s, s, core) for s in here]
    w_z("d1")
    w_3("og")
    w_2("d0")
    w_4("qkv")
    w_3("up")
    qz = q + 2 - 4 * (q // 2)
    for cp in to_z:
        cp.wait_recv()
    there = [R.xn.at[pl.ds(pl.multiple_of(qz * 128, 128), 128), :],
             R.xn.at[pl.ds(pl.multiple_of((7 - qz) * 128, 128), 128), :]]
    to_core += [send(s, s, core) for s in there]
    w_f("d1")
    for cp in to_core:
        cp.wait_recv()

    def qkv_pair(p):
        w = weight("qkv", p)
        R.qp[p] = (dot(R.n1[...], w[:, 0:128], 1, 0).astype(bf16).astype(f32) * 0.125).astype(bf16)
        R.kv[p] = dot(R.xn[...], w[:, 128:384], 1, 0).astype(bf16)
    loop(4, qkv_pair)
    cot_sends, cot_wait = rows_in(R.cot, R.co, 1)
    w_1("d1")

    lane = lax.broadcasted_iota(jnp.int32, (T, 128), 1)
    key_at = lax.broadcasted_iota(jnp.int32, (512, 128), 0)
    col_at = lax.broadcasted_iota(jnp.int32, (512, 128), 1)
    lo_ok = key_at <= col_at + q * 128
    hi_ok = key_at + 512 <= col_at + (7 - q) * 128
    own_ok = (key_at <= col_at)[0:128]

    def attend_pair(p):
        for h in range(2):
            keys = R.kv[p, :, 0:128]
            vals = R.kv[p, :, 128:256]
            qm = jnp.where(lane // 64 == h, R.qp[p], jnp.zeros((), bf16))
            s1 = dot(keys[0:512], qm, 1, 1)
            s2 = dot(keys[512:1024], qm[128:512], 1, 1)
            sa = jnp.where(own_ok, dot(keys[1024:1152], qm[256:384], 1, 1), MASKED)
            sb = jnp.where(own_ok, dot(keys[1152:1280], qm[384:512], 1, 1), MASKED)
            s1 = cat([jnp.where(lo_ok, s1[:, 0:128], MASKED), s1[:, 128:512]])
            s2 = cat([jnp.where(hi_ok, s2[:, 0:128], MASKED), s2[:, 128:384]])
            top = lambda v: jnp.max(v, axis=0, keepdims=True)
            add = lambda v: jnp.sum(v, axis=0, keepdims=True)
            m1 = top(s1)
            m2 = jnp.maximum(m1[:, 128:512], top(s2))
            m = cat([m1[:, 0:128], m2[:, 0:128], jnp.maximum(m2[:, 128:384], cat([top(sa), top(sb)]))])
            e1 = jnp.exp(s1 - m)
            e2 = jnp.exp(s2 - m[:, 128:512])
            ea = jnp.exp(sa - m[:, 256:384])
            eb = jnp.exp(sb - m[:, 384:512])
            l1 = add(e1)
            l2 = l1[:, 128:512] + add(e2)
            total = cat([l1[:, 0:128], l2[:, 0:128], l2[:, 128:384] + cat([add(ea), add(eb)])])
            e1, e2, ea, eb = (v.astype(bf16) for v in (e1, e2, ea, eb))
            R.p1[2 * p + h] = e1
            R.p2[2 * p + h] = e2
            R.po[2 * p + h, :, 0:128] = ea
            R.po[2 * p + h, :, 128:256] = eb
            o1 = dot(vals[0:512], e1, 0, 0)
            o2 = dot(vals[512:1024], e2, 0, 0)
            oa = dot(vals[1024:1152], ea, 0, 0)
            ob = dot(vals[1152:1280], eb, 0, 0)
            o2 = o1[:, 128:512] + o2
            o = cat([o1[:, 0:128], o2[:, 0:128], o2[:, 128:384] + cat([oa, ob])])
            inv = 1.0 / total
            R.li[p, h:h + 1, :] = inv
            R.att[p, 64 * h:64 * h + 64, :] = (o[64 * h:64 * h + 64] * inv).astype(bf16)
    def attend_step(p):
        attend_pair(p)

        @pl.when(p == 0)
        def _():
            w_3("d0")

        @pl.when(p == 1)
        def _():
            w_2("d1")
    loop(4, attend_step)
    w_4("og")

    def lanes(cc):
        return pl.ds(pl.multiple_of(cc * 128, 128), 128)

    def wide(cc):
        return pl.ds(pl.multiple_of(cc * 256, 256), 256)

    def out_block(cc):
        w = R.w_og[:, :, cc].reshape(512, 256)
        br = dot(R.att[...].reshape(512, T), w, 0, 0)
        ao = br[:, 0:128]
        gate = sigmoid(br[:, 128:256] + R.vecs[cc, 2:3, :])
        R.ao[cc] = ao
        R.g1[cc] = gate
        R.mid[cc] = R.xo[cc].astype(f32) + gate * ao
    loop(4, out_block)

    def midrows():
        return cat([R.mid[cc] for cc in range(4)])

    standard, _ = norm_parts(midrows())
    R.n2[...] = (standard * vec_row(3) + vec_row(4)).astype(bf16)
    w_4("up")

    def up_block(rr):
        pre = dot(R.n2[...], weight("up", rr), 1, 0) + cat([R.vecr[rr, 8 + i:9 + i, :] for i in range(4)])
        s = sigmoid(pre)
        R.hid[rr] = (pre * s).astype(bf16)
        R.slp[rr] = (s * (1.0 + pre * (1.0 - s))).astype(bf16)
    loop(4, up_block)
    w_3("d1")
    w_4("d0")
    w_4("d1")
    cot_wait()

    def down_block(cc):
        br = 0.0
        for rr in range(4):
            for j in range(2):
                w = getattr(R, "w_d%d" % j)[rr // 2, rr % 2, cc].reshape(256, 256)
                br = br + dot(R.hid[rr, :, 256 * j:256 * j + 256], w, 1, 0)
        ffn = br[:, 0:128] + R.vecs[cc, 5:6, :]
        gate = sigmoid(br[:, 128:256] + R.vecs[cc, 6:7, :])
        R.out[cc] = (R.mid[cc] + gate * ffn).astype(bf16)
        g = R.co[cc].astype(f32)
        gf = (g * gate).astype(bf16)
        gg = (g * ffn * gate * (1.0 - gate)).astype(bf16)
        R.pair[:, wide(cc)] = cat([gf, gg])
        R.svb[pl.ds(12 + cc, 1), :] = jnp.sum(gf.astype(f32), axis=0, keepdims=True)
        R.svb[pl.ds(16 + cc, 1), :] = jnp.sum(gg.astype(f32), axis=0, keepdims=True)
    loop(4, down_block)
    out_sends, out_wait = rows_out(R.out, R.out_o, 2)

    def grad_down(j, kk):
        for yy in range(2):
            g = dot(R.hid[2 * yy + kk, :, 256 * j:256 * j + 256], R.pair[...], 0, 0).astype(bf16)
            for cc in range(4):
                getattr(R, "g_d%d" % j)[yy, kk, cc] = g[:, 256 * cc:256 * cc + 256].reshape(2, 2, 64, 256)
    for j in range(2):
        grad_down(j, 1 - k)
        g_0("d%d" % j)
        grad_down(j, k)
    g_1("d0")

    def back_up(rr):
        gh = 0.0
        for cc in range(4):
            w = [getattr(R, "w_d%d" % j)[rr // 2, rr % 2, cc].reshape(256, 256) for j in range(2)]
            gh = gh + dot(R.pair[:, 256 * cc:256 * cc + 256], cat(w, 0), 1, 1)
        gp = (gh * R.slp[rr].astype(f32)).astype(bf16)
        R.slp[rr] = gp
        tot = jnp.sum(gp.astype(f32), axis=0, keepdims=True)
        for i in range(4):
            R.svb[pl.ds(20 + 4 * rr + i, 1), :] = tot[:, 128 * i:128 * i + 128]
    loop(4, back_up)
    g_1("d1")

    def grad_up(yy, kk):
        g = dot(R.n2[...], R.slp[2 * yy + kk], 0, 0).astype(bf16)
        R.g_up[yy, kk] = g.reshape(4, 2, 2, 32, 512)
    grad_up(0, 1 - k)
    grad_up(1, 1 - k)
    g_0("up")
    grad_up(0, k)
    grad_up(1, k)

    gn = dot(R.slp[0], weight("up", 0), 1, 1)
    for rr in range(1, 4):
        gn = gn + dot(R.slp[rr], weight("up", rr), 1, 1)

    def norm_back(v, grad, gain_row):
        std, inv = norm_parts(v)
        gs = jnp.sum(grad * std, axis=0, keepdims=True)
        gb = jnp.sum(grad, axis=0, keepdims=True)
        s = grad * vec_row(gain_row)
        f = jnp.sum(s, axis=1, keepdims=True) * (1.0 / D)
        e = jnp.sum(s * std, axis=1, keepdims=True) * (1.0 / D)
        return inv * (s - f - std * e), gs, gb

    def put_sums(to, gs, gb):
        for cc in range(4):
            to[cc:cc + 1, :] = gs[:, 128 * cc:128 * cc + 128]
            to[4 + cc:5 + cc, :] = gb[:, 128 * cc:128 * cc + 128]

    def small_1(v, parts):
        parts[c] = v[...]
        return [send(v, lambda: parts.at[c], (a, r, cc)) for cc in others]

    def small_2(sent, parts, mine, alls):
        for cp in sent:
            cp.wait_recv()
        mine[...] = (parts[0] + parts[1]) + (parts[2] + parts[3])
        alls[slot] = mine[...]
        return [send(mine, lambda: alls.at[slot], dev) for dev in corners]

    def small_3(sent, alls, total):
        for cp in sent:
            cp.wait_recv()
        v = alls[0]
        for i in range(1, 8 if use_x else 4):
            v = v + alls[i]
        total[...] = v

    gm, gs, gb = norm_back(midrows(), gn, 3)
    put_sums(R.svb, gs, gb)
    for cc in range(4):
        g_mid = R.co[cc].astype(f32) + gm[:, 128 * cc:128 * cc + 128]
        R.gm[cc] = g_mid
        gate = R.g1[cc]
        ga = (g_mid * gate).astype(bf16)
        gg = (g_mid * R.ao[cc] * gate * (1.0 - gate)).astype(bf16)
        R.pair[:, 256 * cc:256 * cc + 256] = cat([ga, gg])
        R.svb[8 + cc:9 + cc, :] = jnp.sum(gg.astype(f32), axis=0, keepdims=True)
    g_2("d0")
    g_1("up")

    def grad_out(cc):
        R.g_og[:, :, cc] = dot(R.att[...].reshape(512, T), R.pair[:, wide(cc)], 1, 0).astype(bf16).reshape(2, 2, 2, 2, 32, 256)
    loop(4, grad_out)
    g_0("og")
    do = 0.0
    for cc in range(4):
        do = do + dot(R.w_og[:, :, cc].reshape(512, 256), R.pair[:, 256 * cc:256 * cc + 256], 1, 1)
    for cc in range(4):
        R.mid[cc] = do[:, 128 * cc:128 * cc + 128]
    for i in range(2):
        R.hid[i] = R.xn[512 * i:512 * i + 512, :].T
    R.hid[2, :, 0:256] = R.xn[1024:1280, :].T
    R.hid[3] = R.n1[...].T
    g_1("og")
    svb_1 = small_1(R.svb, R.svb_parts)

    row_of = lax.broadcasted_iota(jnp.int32, (128, T), 0)

    def back_pair(p):
        rows = pl.ds(pl.multiple_of(p * 128, 128), 128)
        dot_t = cat([R.mid[cc, rows, :] for cc in range(4)])
        dot_t = dot_t * jnp.where(row_of < 64, R.li[p, 0:1, :], R.li[p, 1:2, :])
        prod = dot_t * R.att[p].astype(f32)
        dot_t = dot_t.astype(bf16)
        dot_n = dot_t.T
        keys = R.kv[p, :, 0:128]
        vals = R.kv[p, :, 128:256]
        grads = []
        queries = []
        for h in range(2):
            delta = jnp.sum(prod[64 * h:64 * h + 64], axis=0, keepdims=True)
            qm = jnp.where(lane // 64 == h, R.qp[p], jnp.zeros((), bf16))
            om = jnp.where(lane // 64 == h, dot_n, jnp.zeros((), bf16))
            omt = jnp.where(row_of // 64 == h, dot_t, jnp.zeros((), bf16))
            e1, e2 = R.p1[2 * p + h], R.p2[2 * p + h]
            ea, eb = R.po[2 * p + h, :, 0:128], R.po[2 * p + h, :, 128:256]
            d1 = (e1.astype(f32) * (dot(vals[0:512], omt, 1, 0) - delta)).astype(bf16)
            d2 = (e2.astype(f32) * (dot(vals[512:1024], omt[:, 128:512], 1, 0) - delta[:, 128:512])).astype(bf16)
            da = (ea.astype(f32) * (dot(vals[1024:1152], omt[:, 256:384], 1, 0) - delta[:, 256:384])).astype(bf16)
            db = (eb.astype(f32) * (dot(vals[1152:1280], omt[:, 384:512], 1, 0) - delta[:, 384:512])).astype(bf16)
            dk = cat([dot(d1, qm, 1, 0), dot(d2, qm[128:512], 1, 0), dot(da, qm[256:384], 1, 0), dot(db, qm[384:512], 1, 0)], 0)
            dv = cat([dot(e1, om, 1, 0), dot(e2, om[128:512], 1, 0), dot(ea, om[256:384], 1, 0), dot(eb, om[384:512], 1, 0)], 0)
            grads.append((dk, dv))
            x1 = dot(keys[0:512], d1, 0, 0)
            x2 = x1[:, 128:512] + dot(keys[512:1024], d2, 0, 0)
            xab = cat([dot(keys[1024:1152], da, 0, 0), dot(keys[1152:1280], db, 0, 0)])
            dq = cat([x1[:, 0:128], x2[:, 0:128], x2[:, 128:384] + xab])
            queries.append(dq[64 * h:64 * h + 64])
        R.kv[p, :, 0:128] = (grads[0][0] + grads[1][0]).astype(bf16)
        R.kv[p, :, 128:256] = (grads[0][1] + grads[1][1]).astype(bf16)
        R.qp[p] = (cat(queries, 0) * 0.125).astype(bf16).T
        gk = dot(R.hid[0], R.kv[p, 0:512, :], 1, 0) + dot(R.hid[1], R.kv[p, 512:1024, :], 1, 0)
        gk = gk + dot(R.hid[2, :, 0:256], R.kv[p, 1024:1280, :], 1, 0)
        g = cat([dot(R.hid[3], R.qp[p], 1, 0), gk]).astype(bf16)
        R.g_qkv[p // 2, p % 2] = g.reshape(4, 2, 2, 32, 384)

    def qkv_copy(yy):
        return pltpu.make_async_remote_copy(
            src_ref=R.g_qkv.at[yy, 1 - k], dst_ref=R.b0_qkv.at[yy], send_sem=R.qsem.at[0, yy], recv_sem=R.qsem.at[1, yy],
            device_id=core, device_id_type=MESH)

    def back_step(p):
        back_pair(p)

        @pl.when(p % 2 != k)
        def _():
            qkv_copy(p // 2).start()

        @pl.when(p == 0)
        def _():
            g_2("d1")

        @pl.when(p == 1)
        def _():
            g_3("d0")
    loop(4, back_step)
    g_2("up")
    g_4("d0")

    def back_rows(first, count):
        rows = pl.ds(first, count)
        total = dot(R.kv[0, rows, :], weight("qkv", 0)[:, 128:384], 1, 1)
        for p in range(1, 4):
            total = total + dot(R.kv[p, rows, :], weight("qkv", p)[:, 128:384], 1, 1)
        return total

    def chunk_rows(qq):
        return (pl.multiple_of(qq * 128, 128), pl.multiple_of((7 - qq) * 128, 128))

    q1 = q + 1 - 2 * k
    q2 = qz
    q3 = q2 + 1 - 2 * k
    for i, row in enumerate(chunk_rows(q1)):
        R.ex[0, 128 * i:128 * i + 128, :] = back_rows(row, 128).astype(bf16)
    for i, row in enumerate(chunk_rows(q3)):
        R.ex[1, 128 * i:128 * i + 128, :] = back_rows(row, 128).astype(bf16)
    part_core = send(R.ex, R.exr, core)
    for yy in range(2):
        qkv_copy(yy).wait_recv()
    mine2 = [back_rows(row, 128) for row in chunk_rows(q2)]
    part_core.wait_recv()
    for i in range(2):
        R.ez[128 * i:128 * i + 128, :] = (mine2[i] + R.exr[1, 128 * i:128 * i + 128, :].astype(f32)).astype(bf16)
    part_z = send(R.ez, R.ezr, zside)
    g_2("og")
    g_1("qkv")
    svb_2 = small_2(svb_1, R.svb_parts, R.svb_mine, R.svb_all)

    def x_rows(at, n):
        return cat([R.xo[cc, at:at + n, :] for cc in range(4)]).astype(f32)

    def own_rows(row, n, at):
        own = back_rows(row, n)
        for cc in range(4):
            R.mid[cc, at:at + n, :] = own[:, 128 * cc:128 * cc + 128]

    def add_queries(p):
        more = dot(R.qp[p], weight("qkv", p)[:, 0:128], 1, 1)
        for cc in range(4):
            R.mid[cc] = R.mid[cc] + more[:, 128 * cc:128 * cc + 128]

    def to_input(at, n):
        gx, gs, gb = norm_back(x_rows(at, n), cat([R.mid[cc, at:at + n, :] for cc in range(4)]), 0)
        for cc in range(4):
            R.ing[cc, at:at + n, :] = (R.gm[cc, at:at + n, :] + gx[:, 128 * cc:128 * cc + 128]).astype(bf16)
        return gs, gb

    own_rows(lo_row, 128, 0)
    own_rows(hi_row, 128, 128)
    own_rows(1024, 256, 256)
    loop(4, add_queries)
    g_3("d1")
    gs2, gb2 = to_input(256, 256)
    g_3("up")
    ing_sends2, _ = rows_out(R.ing, R.ing_o, 3, (2,))
    g_5("d0")
    g_3("og")
    g_4("d1")
    part_z.wait_recv()
    for cc in range(4):
        here = slice(128 * cc, 128 * cc + 128)
        R.mid[cc, 0:256, :] = R.mid[cc, 0:256, :] + (R.exr[0, :, here].astype(f32) + R.ezr[:, here].astype(f32))
    gs, gb = to_input(0, 256)
    put_sums(R.sva, gs + gs2, gb + gb2)
    sva_1 = small_1(R.sva, R.sva_parts)
    ing_sends, ing_wait = rows_out(R.ing, R.ing_o, 3, (0, 1))
    g_2("qkv")
    g_4("up")

    sva_2 = small_2(sva_1, R.sva_parts, R.sva_mine, R.sva_all)
    g_5("d1")
    g_4("og")
    g_3("qkv")
    g_5("up")
    g_5("og")
    g_4("qkv")
    small_3(svb_2, R.svb_all, R.svb_total)
    small_3(sva_2, R.sva_all, R.sva_total)
    R.small_o[...] = jnp.zeros((16, 128), f32)
    for i in range(2):
        R.small_o[i:i + 1, :] = R.sva_total[pl.ds(4 * i + c, 1), :]
    for i in range(5):
        R.small_o[2 + i:3 + i, :] = R.svb_total[pl.ds(4 * i + c, 1), :]
    for i in range(4):
        R.small_o[8 + i:9 + i, :] = R.svb_total[pl.ds(20 + 4 * r + i, 1), :]
    g_5("qkv")
    for name in NAMES:
        g_6(name)

    out_wait()
    ing_wait()
    for yy in range(2):
        qkv_copy(yy).wait_send()
    for cp in pending:
        cp.wait_send()
    for sends in (tok_sends, cot_sends, out_sends, ing_sends2, ing_sends):
        finish_sends(sends)


def body(use_x, tokens, cotangent, norm1_gain, norm1_bias, qkv_weight, out_weight, gate1_weight,
         gate1_bias, norm2_gain, norm2_bias, up_weight, up_bias, down_weight, down_bias,
         gate2_weight, gate2_bias):
    hbm = pl.BlockSpec(memory_space=pl.ANY)
    vmem = pl.BlockSpec(memory_space=pltpu.VMEM)
    ins = {"tok": tokens, "cot": cotangent, "i_qkv": qkv_weight, "i_out": out_weight, "i_gate1": gate1_weight,
           "i_up": up_weight, "i_down": down_weight, "i_gate2": gate2_weight,
           "norm1_gain": norm1_gain, "norm1_bias": norm1_bias, "gate1_bias": gate1_bias, "norm2_gain": norm2_gain,
           "norm2_bias": norm2_bias, "down_bias": down_bias, "gate2_bias": gate2_bias, "up_bias": up_bias}
    outs = {"out_o": ((2048, 128), bf16, hbm), "ing_o": ((2048, 128), bf16, hbm)}
    for name in NAMES:
        outs[name + "_o"] = (BLOCK[name], bf16, vmem)
    outs["small_o"] = ((16, 128), f32, vmem)
    scr = {}
    for name in NAMES:
        rows, cols = BLOCK[name]
        rq = rows // 4
        scr["w_" + name] = ((2, 2, 4, 2, 2, rq, cols), bf16)
        scr["g_" + name] = ((2, 2, 4, 2, 2, rq, cols), bf16)
        scr["b0_" + name] = ((2, 4, 2, 2, rq, cols), bf16)
        if use_x:
            scr["b1_" + name] = ((4, 2, rq, cols), bf16)
            scr["b2_" + name] = ((2, 4, rq, cols), bf16)
            scr["b3_" + name] = ((4, rq, cols), bf16)
            scr["b4_" + name] = ((4, rq, cols), bf16)
            scr["z_" + name] = ((4, 2, rq, cols), bf16)
            scr["b5_" + name] = ((2, 2, rq, cols), bf16)
            scr["b6_" + name] = ((2, rq, cols), bf16)
        else:
            scr["b1_" + name] = ((4, 2, 2, rq, cols), bf16)
            scr["b5_" + name] = ((2, 2, 2, rq, cols), bf16)
            scr["b6_" + name] = ((2, 2, rq, cols), bf16)
        scr["fin_" + name] = ((2, 2, rq, cols), bf16)
    scr.update({
        "qstage": ((128, 384), bf16), "vec": ((16, 128), f32), "vecs": ((4, 16, 128), f32), "vecr": ((4, 16, 128), f32),
        "xo": ((4, T, 128), bf16), "co": ((4, T, 128), bf16), "n1": ((T, D), bf16),
        "xn": ((1280, D), bf16), "qp": ((4, T, 128), bf16), "kv": ((4, 1280, 256), bf16),
        "p1": ((8, 512, 512), bf16), "p2": ((8, 512, 384), bf16), "po": ((8, 128, 256), bf16),
        "li": ((4, 8, T), f32), "att": ((4, 128, T), bf16), "ao": ((4, T, 128), f32),
        "g1": ((4, T, 128), f32), "mid": ((4, T, 128), f32), "n2": ((T, D), bf16),
        "hid": ((4, T, 512), bf16), "slp": ((4, T, 512), bf16), "out": ((4, T, 128), bf16),
        "pair": ((T, 1024), bf16), "gm": ((4, T, 128), f32), "ing": ((4, T, 128), bf16),
        "ex": ((2, 256, D), bf16), "exr": ((2, 256, D), bf16), "ez": ((256, D), bf16), "ezr": ((256, D), bf16),
        "sva": ((8, 128), f32), "sva_parts": ((4, 8, 128), f32), "sva_mine": ((8, 128), f32), "sva_total": ((8, 128), f32), "sva_all": ((8, 8, 128), f32),
        "svb": ((40, 128), f32), "svb_parts": ((4, 40, 128), f32), "svb_mine": ((40, 128), f32), "svb_total": ((40, 128), f32), "svb_all": ((8, 40, 128), f32),
    })
    shapes = [pltpu.VMEM(s, d) for s, d in scr.values()]
    names_scr = tuple(scr) + ("ssem", "rsem", "issem", "irsem", "lsem", "qsem")
    n_sem = 160
    dma = pltpu.SemaphoreType.DMA
    shapes += [dma((n_sem,)), dma((n_sem,)), dma((4, 4, 3)), dma((4, 4, 3)), dma((20,)), dma((2, 2))]
    res = pl.pallas_call(
        partial(kernel, use_x, tuple(ins), tuple(outs), names_scr),
        out_shape=[jax.ShapeDtypeStruct(s, d) for s, d, _ in outs.values()],
        in_specs=[hbm] * 8 + [vmem] * 8,
        out_specs=[sp for _, _, sp in outs.values()],
        scratch_shapes=shapes,
        compiler_params=pltpu.CompilerParams(collective_id=0, has_side_effects=True, vmem_limit_bytes=60 * 1024 * 1024),
    )(*ins.values())
    if not use_x:
        summed = lax.psum(tuple(v.astype(f32) for v in res[2:]), "grp")
        res = list(res[:2]) + list(summed)
    flat = {"out": (2048, 128), "ing": (2048, 128), "n1g": (128,), "n1b": (128,), "qkv": (128, 384),
            "w_out": (128, 128), "w_gate1": (128, 128), "g1b": (128,), "n2g": (128,), "n2b": (128,),
            "up": (128, 512), "upb": (512,), "w_down": (512, 128), "db": (128,), "w_gate2": (512, 128), "g2b": (128,)}
    kinds = {name: bf16 if name in ("out", "ing") else f32 for name in flat}
    return pl.pallas_call(
        finish,
        out_shape=[jax.ShapeDtypeStruct(shape, kinds[name]) for name, shape in flat.items()],
        in_specs=[vmem] * 8,
        out_specs=[vmem] * 16,
    )(*res)


def finish(out_i, ing_i, qkv_i, og_i, up_i, d0_i, d1_i, small_i, out, ing, n1g, n1b, qkv, w_out, w_gate1, g1b, n2g, n2b,
           up, upb, w_down, db, w_gate2, g2b):
    out[...] = out_i[...]
    ing[...] = ing_i[...]
    g = qkv_i[...].astype(f32)
    qkv[...] = cat([g[:, (2 * j + h) * 64:(2 * j + h + 1) * 64] for h in range(2) for j in range(3)])
    w_out[...] = og_i[:, 0:128].astype(f32)
    w_gate1[...] = og_i[:, 128:256].astype(f32)
    up[...] = up_i[...].astype(f32)
    w_down[0:256, :] = d0_i[:, 0:128].astype(f32)
    w_down[256:512, :] = d1_i[:, 0:128].astype(f32)
    w_gate2[0:256, :] = d0_i[:, 128:256].astype(f32)
    w_gate2[256:512, :] = d1_i[:, 128:256].astype(f32)
    for i, ref in enumerate((n1g, n1b, n2g, n2b, g1b, db, g2b)):
        ref[...] = small_i[i:i + 1, :].reshape(128)
    for i in range(4):
        upb[128 * i:128 * i + 128] = small_i[8 + i:9 + i, :].reshape(128)


def solution(mesh):
    act = P(("grp", "row"), "col")
    col, row = P("col"), P("row")
    cr, rc = P("col", "row"), P("row", "col")
    return jax.shard_map(
        partial(body, mesh.shape["grp"] == 2),
        mesh=mesh,
        in_specs=(act, act, col, col, cr, rc, rc, col, col, col, cr, row, rc, col, rc, col),
        out_specs=(act, act, col, col, cr, rc, rc, col, col, col, cr, row, rc, col, rc, col),
        check_vma=False,
    )
```

```python
from functools import partial

import jax
import jax.numpy as jnp
from jax import lax
from jax.experimental import pallas as pl
from jax.experimental.pallas import tpu as pltpu
from jax.sharding import PartitionSpec as P

bf16 = jnp.bfloat16
f32 = jnp.float32
EPS = 1e-05
MASKED = -1e30
MESH = pl.DeviceIdType.MESH

T = 512
D = 512
BLOCK = {"qkv": (128, 384), "og": (128, 256), "up": (128, 512), "d0": (256, 256), "d1": (256, 256)}
NAMES = ("qkv", "og", "up", "d0", "d1")
VECTORS = ("norm1_gain", "norm1_bias", "gate1_bias", "norm2_gain", "norm2_bias", "down_bias", "gate2_bias")


def dot(a, b, ca, cb):
    return lax.dot_general(a, b, (((ca,), (cb,)), ((), ())), preferred_element_type=f32)


def loop(count, step):
    lax.fori_loop(0, count, lambda i, z: (step(i), z)[1], 0)


def cat(parts, axis=1):
    return jnp.concatenate(parts, axis=axis)


class Waiter:
    def __init__(self, make):
        self.make = make

    def wait_recv(self):
        self.make().wait_recv()

    def wait_send(self):
        self.make().wait_send()


def sigmoid(v):
    return 1.0 / (1.0 + jnp.exp(-v))


def kernel(use_x, names_in, names_out, names_scr, *refs):
    ref = dict(zip(names_in + names_out + names_scr, refs))
    R = type("R", (), ref)
    a = lax.axis_index("grp")
    r = lax.axis_index("row")
    c = lax.axis_index("col")
    y, k = r // 2, r % 2
    ah = a % 2
    q = 2 * (c % 2) + k
    y_, k_, a_ = 1 - y, 1 - k, 1 - ah
    c_far = lax.rem(c + 2, 4)
    c_near = c + 1 - 2 * (c % 2)
    c_across = lax.rem(c_near + 2, 4)
    slot = 4 * ah + r if use_x else r
    others = [lax.rem(c + i, 4) for i in range(1, 4)]
    core = (a, 2 * y + 1 - k, c)
    yside = (a, 2 * (1 - y) + k, c)
    xside = (a + 1 - 2 * ah, r, c)
    zside = (a, r, c + 1 - 2 * (c % 2))
    owner_row = 2 * y + c // 2
    lo_row = pl.multiple_of(q * 128, 128)
    hi_row = pl.multiple_of((7 - q) * 128, 128)

    counter = [0]
    pending = []

    def send(src, dst, dev):
        i = counter[0]
        counter[0] += 1

        def make():
            return pltpu.make_async_remote_copy(
                src_ref=src() if callable(src) else src, dst_ref=dst() if callable(dst) else dst,
                send_sem=R.ssem.at[i], recv_sem=R.rsem.at[i], device_id=dev, device_id_type=MESH)
        make().start()
        pending.append(Waiter(make))
        return pending[-1]

    local = []

    def fetch(src, dst):
        cp = pltpu.make_async_copy(src, dst, R.lsem.at[len(local)])
        cp.start()
        local.append(cp)

    fetch(R.i_qkv, R.qstage)
    for t in range(2):
        for name, sources, skip in (("og", ("out", "gate1"), 0), ("up", ("up",), 0),
                                    ("d0", ("down", "gate2"), 0), ("d1", ("down", "gate2"), 256)):
            rows, cols = BLOCK[name]
            rq = rows // 4
            w = getattr(R, "w_" + name)
            width = cols // len(sources)
            for j, s in enumerate(sources):
                at = pl.multiple_of((2 * t + ah) * rq + skip, 32)
                fetch(getattr(R, "i_" + s).at[pl.ds(at, rq), :],
                      w.at[y, k, c, t, ah, :, pl.ds(j * width, width)])

    barrier = pltpu.get_barrier_semaphore()
    for kk in range(2):
        for cc in range(4):
            me = (k == kk) & (c == cc)

            @pl.when(jnp.logical_not(me))
            def _():
                pl.semaphore_signal(barrier, inc=1, device_id=(a, 2 * y + kk, cc), device_id_type=MESH)
    diag = (a, 2 * (1 - y) + 1 - k, c)
    corners = [(g, rr, c) for g in ((a, a + 1 - 2 * ah) if use_x else (a,))
               for rr in (r, 2 * y + 1 - k, 2 * (1 - y) + k, 2 * (1 - y) + 1 - k)][1:]
    for dev in (corners[1:] if use_x else corners[1:] + [xside]):
        pl.semaphore_signal(barrier, inc=1, device_id=dev, device_id_type=MESH)

    local[0].wait()
    for t in range(2):
        blk = R.qstage[pl.ds(pl.multiple_of((2 * t + ah) * 32, 32), 32), :].astype(f32)
        parts = [blk[:, (3 * h + j) * 64:(3 * h + j + 1) * 64] for j in range(3) for h in range(2)]
        R.w_qkv[y, k, c, t, ah] = cat(parts).astype(bf16)
    R.vec[...] = jnp.zeros((16, 128), f32)
    R.svb[32:40, :] = jnp.zeros((8, 128), f32)
    for i, name in enumerate(VECTORS):
        R.vec[i:i + 1, :] = getattr(R, name)[...].astype(f32).reshape(1, 128)
    for i in range(4):
        R.vec[8 + i:9 + i, :] = R.up_bias[128 * i:128 * i + 128].astype(f32).reshape(1, 128)
    pl.semaphore_wait(barrier, 13 if use_x else 10)

    def rows_in(src, dst, which):
        sends = []
        for qq in range(4):
            kq, cq = qq % 2, 2 * k + qq // 2
            me = (k == kq) & (c == cq)
            for j, (s0, d0, n) in enumerate(((qq * 128, 0, 128), ((7 - qq) * 128, 128, 128), ((8 + 2 * qq) * 128, 256, 256))):
                s = src.at[pl.ds(s0, n), :]
                d = dst.at[c, pl.ds(d0, n), :]
                rs = R.irsem.at[which, c, j]
                cp = pltpu.make_async_remote_copy(
                    src_ref=s, dst_ref=d, send_sem=R.issem.at[which, qq, j], recv_sem=rs,
                    device_id=(a, 2 * y + kq, cq), device_id_type=MESH)
                sends.append((me, cp))

                @pl.when(jnp.logical_not(me))
                def _():
                    cp.start()

                @pl.when(me)
                def _():
                    pltpu.make_async_copy(s, d, rs).start()

        def wait():
            for cc in range(4):
                for j, (d0, n) in enumerate(((0, 128), (128, 128), (256, 256))):
                    d = dst.at[cc, pl.ds(d0, n), :]
                    pltpu.make_async_copy(d, d, R.irsem.at[which, cc, j]).wait()
        return sends, wait

    def rows_out(src, dst, which, only=(0, 1, 2)):
        sends = []
        for cc in range(4):
            me = (c // 2 == k) & (c == cc)
            for j, (s0, d0, n) in enumerate(((0, lo_row, 128), (128, hi_row, 128), (256, 1024 + pl.multiple_of(q * 256, 256), 256))):
                if j not in only:
                    continue
                s = src.at[cc, pl.ds(s0, n), :]
                d = dst.at[pl.ds(d0, n), :]
                rs = R.irsem.at[which, q, j]
                cp = pltpu.make_async_remote_copy(
                    src_ref=s, dst_ref=d, send_sem=R.issem.at[which, cc, j], recv_sem=rs,
                    device_id=(a, owner_row, cc), device_id_type=MESH)
                sends.append((me, cp))

                @pl.when(jnp.logical_not(me))
                def _():
                    cp.start()

                @pl.when(me)
                def _():
                    pltpu.make_async_copy(s, d, rs).start()

        def wait():
            for qq in range(4):
                for j, (d0, n) in enumerate(((qq * 128, 128), ((7 - qq) * 128, 128), ((8 + 2 * qq) * 128, 256))):
                    d = dst.at[pl.ds(d0, n), :]
                    pltpu.make_async_copy(d, d, R.irsem.at[which, qq, j]).wait()
        return sends, wait

    def finish_sends(sends):
        for me, cp in sends:
            @pl.when(jnp.logical_not(me))
            def _():
                cp.wait_send()

    wst = {}

    def w_z(name):
        w = getattr(R, "w_" + name)
        here = lambda: w.at[y, k, c, :, ah]
        wst[name, "far"] = send(here, here, (a, r, c_far))
        wst[name, "near"] = send(here, here, zside)

    def w_f(name):
        w = getattr(R, "w_" + name)
        wst[name, "far"].wait_recv()
        here = lambda: w.at[y, k, c_far, :, ah]
        wst[name, "on"] = send(here, here, zside)

    def to_sibling(name, s):
        wst.setdefault((name, "core"), []).append(send(s, s, core))

    def w_1(name):
        w = getattr(R, "w_" + name)
        wst[name, "near"].wait_recv()
        wst[name, "on"].wait_recv()
        s = lambda: w.at[y, k, :, 0, ah]
        wst[name, "x1"] = send(s, s, xside)
        s = lambda: w.at[y, k, :, 1, ah]
        wst[name, "y1"] = send(s, s, yside)
        to_sibling(name, lambda: w.at[y, k, :, :, ah])

    def w_2(name):
        w = getattr(R, "w_" + name)
        wst[name, "x1"].wait_recv()
        s = lambda: w.at[y, k, :, 0]
        wst[name, "y2"] = send(s, s, yside)
        to_sibling(name, lambda: w.at[y, k, :, 0, a_])
        wst[name, "y1"].wait_recv()
        s = lambda: w.at[:, k, :, 1, ah]
        wst[name, "x2"] = send(s, s, xside)
        to_sibling(name, lambda: w.at[y_, k, :, 1, ah])

    def w_3(name):
        w = getattr(R, "w_" + name)
        wst[name, "y2"].wait_recv()
        to_sibling(name, lambda: w.at[y_, k, :, 0])
        wst[name, "x2"].wait_recv()
        to_sibling(name, lambda: w.at[:, k, :, 1, a_])

    def w_4(name):
        for cp in wst[name, "core"]:
            cp.wait_recv()

    gst = {}

    def g_0(name):
        g, b0 = getattr(R, "g_" + name), getattr(R, "b0_" + name)
        gst[name, "core"] = send(lambda: g.at[:, k_], b0, core)

    def g_1(name):
        g, b0, b1 = getattr(R, "g_" + name), getattr(R, "b0_" + name), getattr(R, "b1_" + name)
        if name != "qkv":
            gst[name, "core"].wait_recv()

        def one(i):
            yy, cc = i // 4, i % 4
            b0[yy, cc] = (b0[yy, cc].astype(f32) + g[yy, k, cc].astype(f32)).astype(bf16)
        loop(8, one)
        if use_x:
            b2 = getattr(R, "b2_" + name)
            gst[name, "y1"] = send(lambda: b0.at[y_, :, 0], b1, yside)
            gst[name, "x1"] = send(lambda: b0.at[:, :, 1, a_], b2, xside)
        else:
            gst[name, "y1"] = send(lambda: b0.at[y_], b1, yside)

    def g_2(name):
        b0, b1 = getattr(R, "b0_" + name), getattr(R, "b1_" + name)
        gst[name, "y1"].wait_recv()
        if not use_x:
            def one(cc):
                b1[cc] = (b1[cc].astype(f32) + b0[y, cc].astype(f32)).astype(bf16)
            loop(4, one)
            return
        b2, b3, b4 = (getattr(R, "b%d_%s" % (i, name)) for i in (2, 3, 4))

        def one(cc):
            b1[cc] = (b1[cc].astype(f32) + b0[y, cc, 0].astype(f32)).astype(bf16)
        loop(4, one)
        gst[name, "x2"] = send(lambda: b1.at[:, a_], b3, xside)
        gst[name, "x1"].wait_recv()

        def two(i):
            yy, cc = i // 4, i % 4
            b2[yy, cc] = (b2[yy, cc].astype(f32) + b0[yy, cc, 1, ah].astype(f32)).astype(bf16)
        loop(8, two)
        gst[name, "y2"] = send(lambda: b2.at[y_], b4, yside)

    def g_3(name):
        b1, z, b5 = (getattr(R, "%s_%s" % (i, name)) for i in ("b1", "z" if use_x else "b1", "b5"))
        if use_x:
            b2, b3, b4 = (getattr(R, "b%d_%s" % (i, name)) for i in (2, 3, 4))
            gst[name, "x2"].wait_recv()
            gst[name, "y2"].wait_recv()

            def one(cc):
                z[cc, 0] = (b1[cc, ah].astype(f32) + b3[cc].astype(f32)).astype(bf16)
                z[cc, 1] = (b2[y, cc].astype(f32) + b4[cc].astype(f32)).astype(bf16)
            loop(4, one)
        gst[name, "near"] = [send(lambda cc=cc: z.at[cc], lambda i=i: b5.at[i], zside) for i, cc in enumerate((c_near, c_across))]

    def g_4(name):
        z, b5, b6 = (getattr(R, "%s_%s" % (i, name)) for i in ("z" if use_x else "b1", "b5", "b6"))
        for cp in gst[name, "near"]:
            cp.wait_recv()
        b5[1] = (b5[1].astype(f32) + z[c_far].astype(f32)).astype(bf16)
        gst[name, "far"] = send(lambda: b5.at[1], b6, (a, r, c_far))

    def g_5(name):
        z, b5, b6, fin = (getattr(R, "%s_%s" % (i, name)) for i in ("z" if use_x else "b1", "b5", "b6", "fin"))
        gst[name, "far"].wait_recv()
        total = z[c].astype(f32) + b5[0].astype(f32) + b6[...].astype(f32)
        if use_x:
            for t in range(2):
                fin[t, ah] = total[t].astype(bf16)
            s = lambda: fin.at[:, ah]
            gst[name, "x3"] = send(s, s, xside)
        else:
            fin[...] = total.astype(bf16)

    def g_6(name):
        if use_x:
            gst[name, "x3"].wait_recv()
        rows, cols = BLOCK[name]
        getattr(R, name + "_o")[...] = getattr(R, "fin_" + name)[...].reshape(rows, cols)

    def weight(name, rr):
        w = getattr(R, "w_" + name)
        return w[rr // 2, rr % 2].reshape(4 * BLOCK[name][0], BLOCK[name][1])

    R.vecs[c] = R.vec[...]
    R.vecr[r] = R.vec[...]
    vec_cp = [send(R.vec, R.vecs.at[c], (a, r, (c + i) % 4)) for i in range(1, 4)]
    vec_cp += [send(R.vec, R.vecr.at[r], dev) for dev in (core, yside, diag)]
    w_z("qkv")
    for cp in local[1:]:
        cp.wait()
    w_z("og")
    w_f("qkv")
    w_z("up")
    w_f("og")
    w_1("qkv")
    w_z("d0")
    w_1("og")
    w_f("up")
    w_2("qkv")
    w_1("up")
    w_f("d0")
    tok_sends, tok_wait = rows_in(R.tok, R.xo, 0)
    w_2("og")
    w_1("d0")
    w_3("qkv")
    w_2("up")
    for cp in vec_cp:
        cp.wait_recv()

    def vec_row(i):
        return cat([R.vecs[cc, i:i + 1, :] for cc in range(4)])

    tok_wait()

    def xrows():
        return cat([R.xo[cc] for cc in range(4)]).astype(f32)

    def norm_parts(v):
        mean = jnp.sum(v, axis=1, keepdims=True) * (1.0 / D)
        cen = v - mean
        var = jnp.sum(cen * cen, axis=1, keepdims=True) * (1.0 / D)
        inv = lax.rsqrt(var + EPS)
        return cen * inv, inv

    standard, _ = norm_parts(xrows())
    n1 = (standard * vec_row(0) + vec_row(1)).astype(bf16)
    R.n1[...] = n1
    R.xn[pl.ds(lo_row, 128), :] = n1[0:128]
    R.xn[pl.ds(hi_row, 128), :] = n1[128:256]
    R.xn[1024:1280, :] = n1[256:512]
    here = [R.xn.at[pl.ds(lo_row, 128), :], R.xn.at[pl.ds(hi_row, 128), :]]
    to_z = [send(s, s, zside) for s in here]
    to_core = [send(s, s, core) for s in here]
    w_z("d1")
    w_3("og")
    w_2("d0")
    w_4("qkv")
    w_3("up")
    qz = q + 2 - 4 * (q // 2)
    for cp in to_z:
        cp.wait_recv()
    there = [R.xn.at[pl.ds(pl.multiple_of(qz * 128, 128), 128), :],
             R.xn.at[pl.ds(pl.multiple_of((7 - qz) * 128, 128), 128), :]]
    to_core += [send(s, s, core) for s in there]
    w_f("d1")
    for cp in to_core:
        cp.wait_recv()

    def qkv_pair(p):
        w = weight("qkv", p)
        R.qp[p] = (dot(R.n1[...], w[:, 0:128], 1, 0).astype(bf16).astype(f32) * 0.125).astype(bf16)
        R.kv[p] = dot(R.xn[...], w[:, 128:384], 1, 0).astype(bf16)
    loop(4, qkv_pair)
    cot_sends, cot_wait = rows_in(R.cot, R.co, 1)
    w_1("d1")

    lane = lax.broadcasted_iota(jnp.int32, (T, 128), 1)
    key_at = lax.broadcasted_iota(jnp.int32, (512, 128), 0)
    col_at = lax.broadcasted_iota(jnp.int32, (512, 128), 1)
    lo_ok = key_at <= col_at + q * 128
    hi_ok = key_at + 512 <= col_at + (7 - q) * 128
    own_ok = (key_at <= col_at)[0:128]

    def attend_pair(p):
        for h in range(2):
            keys = R.kv[p, :, 0:128]
            vals = R.kv[p, :, 128:256]
            qm = jnp.where(lane // 64 == h, R.qp[p], jnp.zeros((), bf16))
            s1 = dot(keys[0:512], qm, 1, 1)
            s2 = dot(keys[512:1024], qm[128:512], 1, 1)
            sa = jnp.where(own_ok, dot(keys[1024:1152], qm[256:384], 1, 1), MASKED)
            sb = jnp.where(own_ok, dot(keys[1152:1280], qm[384:512], 1, 1), MASKED)
            s1 = cat([jnp.where(lo_ok, s1[:, 0:128], MASKED), s1[:, 128:512]])
            s2 = cat([jnp.where(hi_ok, s2[:, 0:128], MASKED), s2[:, 128:384]])
            top = lambda v: jnp.max(v, axis=0, keepdims=True)
            add = lambda v: jnp.sum(v, axis=0, keepdims=True)
            m1 = top(s1)
            m2 = jnp.maximum(m1[:, 128:512], top(s2))
            m = cat([m1[:, 0:128], m2[:, 0:128], jnp.maximum(m2[:, 128:384], cat([top(sa), top(sb)]))])
            e1 = jnp.exp(s1 - m)
            e2 = jnp.exp(s2 - m[:, 128:512])
            ea = jnp.exp(sa - m[:, 256:384])
            eb = jnp.exp(sb - m[:, 384:512])
            l1 = add(e1)
            l2 = l1[:, 128:512] + add(e2)
            total = cat([l1[:, 0:128], l2[:, 0:128], l2[:, 128:384] + cat([add(ea), add(eb)])])
            e1, e2, ea, eb = (v.astype(bf16) for v in (e1, e2, ea, eb))
            R.p1[2 * p + h] = e1
            R.p2[2 * p + h] = e2
            R.po[2 * p + h, :, 0:128] = ea
            R.po[2 * p + h, :, 128:256] = eb
            o1 = dot(vals[0:512], e1, 0, 0)
            o2 = dot(vals[512:1024], e2, 0, 0)
            oa = dot(vals[1024:1152], ea, 0, 0)
            ob = dot(vals[1152:1280], eb, 0, 0)
            o2 = o1[:, 128:512] + o2
            o = cat([o1[:, 0:128], o2[:, 0:128], o2[:, 128:384] + cat([oa, ob])])
            inv = 1.0 / total
            R.li[p, h:h + 1, :] = inv
            R.att[p, 64 * h:64 * h + 64, :] = (o[64 * h:64 * h + 64] * inv).astype(bf16)
    def attend_step(p):
        attend_pair(p)

        @pl.when(p == 0)
        def _():
            w_3("d0")

        @pl.when(p == 1)
        def _():
            w_2("d1")
    loop(4, attend_step)
    w_4("og")

    def lanes(cc):
        return pl.ds(pl.multiple_of(cc * 128, 128), 128)

    def wide(cc):
        return pl.ds(pl.multiple_of(cc * 256, 256), 256)

    def out_block(cc):
        w = R.w_og[:, :, cc].reshape(512, 256)
        br = dot(R.att[...].reshape(512, T), w, 0, 0)
        ao = br[:, 0:128]
        gate = sigmoid(br[:, 128:256] + R.vecs[cc, 2:3, :])
        R.ao[cc] = ao
        R.g1[cc] = gate
        R.mid[cc] = R.xo[cc].astype(f32) + gate * ao
    loop(4, out_block)

    def midrows():
        return cat([R.mid[cc] for cc in range(4)])

    standard, _ = norm_parts(midrows())
    R.n2[...] = (standard * vec_row(3) + vec_row(4)).astype(bf16)
    w_4("up")

    def up_block(rr):
        pre = dot(R.n2[...], weight("up", rr), 1, 0) + cat([R.vecr[rr, 8 + i:9 + i, :] for i in range(4)])
        s = sigmoid(pre)
        R.hid[rr] = (pre * s).astype(bf16)
        R.slp[rr] = (s * (1.0 + pre * (1.0 - s))).astype(bf16)
    loop(4, up_block)
    w_3("d1")
    w_4("d0")
    w_4("d1")
    cot_wait()

    def down_block(cc):
        br = 0.0
        for rr in range(4):
            for j in range(2):
                w = getattr(R, "w_d%d" % j)[rr // 2, rr % 2, cc].reshape(256, 256)
                br = br + dot(R.hid[rr, :, 256 * j:256 * j + 256], w, 1, 0)
        ffn = br[:, 0:128] + R.vecs[cc, 5:6, :]
        gate = sigmoid(br[:, 128:256] + R.vecs[cc, 6:7, :])
        R.out[cc] = (R.mid[cc] + gate * ffn).astype(bf16)
        g = R.co[cc].astype(f32)
        gf = (g * gate).astype(bf16)
        gg = (g * ffn * gate * (1.0 - gate)).astype(bf16)
        R.pair[:, wide(cc)] = cat([gf, gg])
        R.svb[pl.ds(12 + cc, 1), :] = jnp.sum(gf.astype(f32), axis=0, keepdims=True)
        R.svb[pl.ds(16 + cc, 1), :] = jnp.sum(gg.astype(f32), axis=0, keepdims=True)
    loop(4, down_block)
    out_sends, out_wait = rows_out(R.out, R.out_o, 2)

    def grad_down(j, kk):
        for yy in range(2):
            g = dot(R.hid[2 * yy + kk, :, 256 * j:256 * j + 256], R.pair[...], 0, 0).astype(bf16)
            for cc in range(4):
                getattr(R, "g_d%d" % j)[yy, kk, cc] = g[:, 256 * cc:256 * cc + 256].reshape(2, 2, 64, 256)
    for j in range(2):
        grad_down(j, 1 - k)
        g_0("d%d" % j)
        grad_down(j, k)
    g_1("d0")

    def back_up(rr):
        gh = 0.0
        for cc in range(4):
            w = [getattr(R, "w_d%d" % j)[rr // 2, rr % 2, cc].reshape(256, 256) for j in range(2)]
            gh = gh + dot(R.pair[:, 256 * cc:256 * cc + 256], cat(w, 0), 1, 1)
        gp = (gh * R.slp[rr].astype(f32)).astype(bf16)
        R.slp[rr] = gp
        tot = jnp.sum(gp.astype(f32), axis=0, keepdims=True)
        for i in range(4):
            R.svb[pl.ds(20 + 4 * rr + i, 1), :] = tot[:, 128 * i:128 * i + 128]
    loop(4, back_up)
    g_1("d1")

    def grad_up(yy, kk):
        g = dot(R.n2[...], R.slp[2 * yy + kk], 0, 0).astype(bf16)
        R.g_up[yy, kk] = g.reshape(4, 2, 2, 32, 512)
    grad_up(0, 1 - k)
    grad_up(1, 1 - k)
    g_0("up")
    grad_up(0, k)
    grad_up(1, k)

    gn = dot(R.slp[0], weight("up", 0), 1, 1)
    for rr in range(1, 4):
        gn = gn + dot(R.slp[rr], weight("up", rr), 1, 1)

    def norm_back(v, grad, gain_row):
        std, inv = norm_parts(v)
        gs = jnp.sum(grad * std, axis=0, keepdims=True)
        gb = jnp.sum(grad, axis=0, keepdims=True)
        s = grad * vec_row(gain_row)
        f = jnp.sum(s, axis=1, keepdims=True) * (1.0 / D)
        e = jnp.sum(s * std, axis=1, keepdims=True) * (1.0 / D)
        return inv * (s - f - std * e), gs, gb

    def put_sums(to, gs, gb):
        for cc in range(4):
            to[cc:cc + 1, :] = gs[:, 128 * cc:128 * cc + 128]
            to[4 + cc:5 + cc, :] = gb[:, 128 * cc:128 * cc + 128]

    def small_1(v, parts):
        parts[c] = v[...]
        return [send(v, lambda: parts.at[c], (a, r, cc)) for cc in others]

    def small_2(sent, parts, mine, alls):
        for cp in sent:
            cp.wait_recv()
        mine[...] = (parts[0] + parts[1]) + (parts[2] + parts[3])
        alls[slot] = mine[...]
        return [send(mine, lambda: alls.at[slot], dev) for dev in corners]

    def small_3(sent, alls, total):
        for cp in sent:
            cp.wait_recv()
        v = alls[0]
        for i in range(1, 8 if use_x else 4):
            v = v + alls[i]
        total[...] = v

    gm, gs, gb = norm_back(midrows(), gn, 3)
    put_sums(R.svb, gs, gb)
    for cc in range(4):
        g_mid = R.co[cc].astype(f32) + gm[:, 128 * cc:128 * cc + 128]
        R.gm[cc] = g_mid
        gate = R.g1[cc]
        ga = (g_mid * gate).astype(bf16)
        gg = (g_mid * R.ao[cc] * gate * (1.0 - gate)).astype(bf16)
        R.pair[:, 256 * cc:256 * cc + 256] = cat([ga, gg])
        R.svb[8 + cc:9 + cc, :] = jnp.sum(gg.astype(f32), axis=0, keepdims=True)
    g_2("d0")
    g_1("up")

    def grad_out(cc):
        R.g_og[:, :, cc] = dot(R.att[...].reshape(512, T), R.pair[:, wide(cc)], 1, 0).astype(bf16).reshape(2, 2, 2, 2, 32, 256)
    loop(4, grad_out)
    g_0("og")
    do = 0.0
    for cc in range(4):
        do = do + dot(R.w_og[:, :, cc].reshape(512, 256), R.pair[:, 256 * cc:256 * cc + 256], 1, 1)
    for cc in range(4):
        R.mid[cc] = do[:, 128 * cc:128 * cc + 128]
    for i in range(2):
        R.hid[i] = R.xn[512 * i:512 * i + 512, :].T
    R.hid[2, :, 0:256] = R.xn[1024:1280, :].T
    R.hid[3] = R.n1[...].T
    g_1("og")
    svb_1 = small_1(R.svb, R.svb_parts)

    row_of = lax.broadcasted_iota(jnp.int32, (128, T), 0)

    def back_pair(p):
        rows = pl.ds(pl.multiple_of(p * 128, 128), 128)
        dot_t = cat([R.mid[cc, rows, :] for cc in range(4)])
        dot_t = dot_t * jnp.where(row_of < 64, R.li[p, 0:1, :], R.li[p, 1:2, :])
        prod = dot_t * R.att[p].astype(f32)
        dot_t = dot_t.astype(bf16)
        dot_n = dot_t.T
        keys = R.kv[p, :, 0:128]
        vals = R.kv[p, :, 128:256]
        grads = []
        queries = []
        for h in range(2):
            delta = jnp.sum(prod[64 * h:64 * h + 64], axis=0, keepdims=True)
            qm = jnp.where(lane // 64 == h, R.qp[p], jnp.zeros((), bf16))
            om = jnp.where(lane // 64 == h, dot_n, jnp.zeros((), bf16))
            omt = jnp.where(row_of // 64 == h, dot_t, jnp.zeros((), bf16))
            e1, e2 = R.p1[2 * p + h], R.p2[2 * p + h]
            ea, eb = R.po[2 * p + h, :, 0:128], R.po[2 * p + h, :, 128:256]
            d1 = (e1.astype(f32) * (dot(vals[0:512], omt, 1, 0) - delta)).astype(bf16)
            d2 = (e2.astype(f32) * (dot(vals[512:1024], omt[:, 128:512], 1, 0) - delta[:, 128:512])).astype(bf16)
            da = (ea.astype(f32) * (dot(vals[1024:1152], omt[:, 256:384], 1, 0) - delta[:, 256:384])).astype(bf16)
            db = (eb.astype(f32) * (dot(vals[1152:1280], omt[:, 384:512], 1, 0) - delta[:, 384:512])).astype(bf16)
            dk = cat([dot(d1, qm, 1, 0), dot(d2, qm[128:512], 1, 0), dot(da, qm[256:384], 1, 0), dot(db, qm[384:512], 1, 0)], 0)
            dv = cat([dot(e1, om, 1, 0), dot(e2, om[128:512], 1, 0), dot(ea, om[256:384], 1, 0), dot(eb, om[384:512], 1, 0)], 0)
            grads.append((dk, dv))
            x1 = dot(keys[0:512], d1, 0, 0)
            x2 = x1[:, 128:512] + dot(keys[512:1024], d2, 0, 0)
            xab = cat([dot(keys[1024:1152], da, 0, 0), dot(keys[1152:1280], db, 0, 0)])
            dq = cat([x1[:, 0:128], x2[:, 0:128], x2[:, 128:384] + xab])
            queries.append(dq[64 * h:64 * h + 64])
        R.kv[p, :, 0:128] = (grads[0][0] + grads[1][0]).astype(bf16)
        R.kv[p, :, 128:256] = (grads[0][1] + grads[1][1]).astype(bf16)
        R.qp[p] = (cat(queries, 0) * 0.125).astype(bf16).T
        gk = dot(R.hid[0], R.kv[p, 0:512, :], 1, 0) + dot(R.hid[1], R.kv[p, 512:1024, :], 1, 0)
        gk = gk + dot(R.hid[2, :, 0:256], R.kv[p, 1024:1280, :], 1, 0)
        g = cat([dot(R.hid[3], R.qp[p], 1, 0), gk]).astype(bf16)
        R.g_qkv[p // 2, p % 2] = g.reshape(4, 2, 2, 32, 384)

    def qkv_copy(yy):
        return pltpu.make_async_remote_copy(
            src_ref=R.g_qkv.at[yy, 1 - k], dst_ref=R.b0_qkv.at[yy], send_sem=R.qsem.at[0, yy], recv_sem=R.qsem.at[1, yy],
            device_id=core, device_id_type=MESH)

    def back_step(p):
        back_pair(p)

        @pl.when(p % 2 != k)
        def _():
            qkv_copy(p // 2).start()

        @pl.when(p == 0)
        def _():
            g_2("d1")

        @pl.when(p == 1)
        def _():
            g_3("d0")
    loop(4, back_step)
    g_2("up")
    g_4("d0")

    def back_rows(first, count):
        rows = pl.ds(first, count)
        total = dot(R.kv[0, rows, :], weight("qkv", 0)[:, 128:384], 1, 1)
        for p in range(1, 4):
            total = total + dot(R.kv[p, rows, :], weight("qkv", p)[:, 128:384], 1, 1)
        return total

    def chunk_rows(qq):
        return (pl.multiple_of(qq * 128, 128), pl.multiple_of((7 - qq) * 128, 128))

    q1 = q + 1 - 2 * k
    q2 = qz
    q3 = q2 + 1 - 2 * k
    for i, row in enumerate(chunk_rows(q1)):
        R.ex[0, 128 * i:128 * i + 128, :] = back_rows(row, 128).astype(bf16)
    for i, row in enumerate(chunk_rows(q3)):
        R.ex[1, 128 * i:128 * i + 128, :] = back_rows(row, 128).astype(bf16)
    part_core = send(R.ex, R.exr, core)
    for yy in range(2):
        qkv_copy(yy).wait_recv()
    mine2 = [back_rows(row, 128) for row in chunk_rows(q2)]
    part_core.wait_recv()
    for i in range(2):
        R.ez[128 * i:128 * i + 128, :] = (mine2[i] + R.exr[1, 128 * i:128 * i + 128, :].astype(f32)).astype(bf16)
    part_z = send(R.ez, R.ezr, zside)
    g_2("og")
    g_1("qkv")
    svb_2 = small_2(svb_1, R.svb_parts, R.svb_mine, R.svb_all)

    def x_rows(at, n):
        return cat([R.xo[cc, at:at + n, :] for cc in range(4)]).astype(f32)

    def own_rows(row, n, at):
        own = back_rows(row, n)
        for cc in range(4):
            R.mid[cc, at:at + n, :] = own[:, 128 * cc:128 * cc + 128]

    def add_queries(p):
        more = dot(R.qp[p], weight("qkv", p)[:, 0:128], 1, 1)
        for cc in range(4):
            R.mid[cc] = R.mid[cc] + more[:, 128 * cc:128 * cc + 128]

    def to_input(at, n):
        gx, gs, gb = norm_back(x_rows(at, n), cat([R.mid[cc, at:at + n, :] for cc in range(4)]), 0)
        for cc in range(4):
            R.ing[cc, at:at + n, :] = (R.gm[cc, at:at + n, :] + gx[:, 128 * cc:128 * cc + 128]).astype(bf16)
        return gs, gb

    own_rows(lo_row, 128, 0)
    own_rows(hi_row, 128, 128)
    own_rows(1024, 256, 256)
    loop(4, add_queries)
    g_3("d1")
    gs2, gb2 = to_input(256, 256)
    g_3("up")
    ing_sends2, _ = rows_out(R.ing, R.ing_o, 3, (2,))
    g_3("og")
    g_4("d1")
    part_z.wait_recv()
    for cc in range(4):
        here = slice(128 * cc, 128 * cc + 128)
        R.mid[cc, 0:256, :] = R.mid[cc, 0:256, :] + (R.exr[0, :, here].astype(f32) + R.ezr[:, here].astype(f32))
    gs, gb = to_input(0, 256)
    put_sums(R.sva, gs + gs2, gb + gb2)
    sva_1 = small_1(R.sva, R.sva_parts)
    ing_sends, ing_wait = rows_out(R.ing, R.ing_o, 3, (0, 1))
    g_2("qkv")
    g_5("d0")
    g_4("up")

    sva_2 = small_2(sva_1, R.sva_parts, R.sva_mine, R.sva_all)
    g_5("d1")
    g_4("og")
    g_3("qkv")
    g_5("up")
    g_5("og")
    g_4("qkv")
    small_3(svb_2, R.svb_all, R.svb_total)
    small_3(sva_2, R.sva_all, R.sva_total)
    R.small_o[...] = jnp.zeros((16, 128), f32)
    for i in range(2):
        R.small_o[i:i + 1, :] = R.sva_total[pl.ds(4 * i + c, 1), :]
    for i in range(5):
        R.small_o[2 + i:3 + i, :] = R.svb_total[pl.ds(4 * i + c, 1), :]
    for i in range(4):
        R.small_o[8 + i:9 + i, :] = R.svb_total[pl.ds(20 + 4 * r + i, 1), :]
    g_5("qkv")
    for name in NAMES:
        g_6(name)

    out_wait()
    ing_wait()
    for yy in range(2):
        qkv_copy(yy).wait_send()
    for cp in pending:
        cp.wait_send()
    for sends in (tok_sends, cot_sends, out_sends, ing_sends2, ing_sends):
        finish_sends(sends)


def body(use_x, tokens, cotangent, norm1_gain, norm1_bias, qkv_weight, out_weight, gate1_weight,
         gate1_bias, norm2_gain, norm2_bias, up_weight, up_bias, down_weight, down_bias,
         gate2_weight, gate2_bias):
    hbm = pl.BlockSpec(memory_space=pl.ANY)
    vmem = pl.BlockSpec(memory_space=pltpu.VMEM)
    ins = {"tok": tokens, "cot": cotangent, "i_qkv": qkv_weight, "i_out": out_weight, "i_gate1": gate1_weight,
           "i_up": up_weight, "i_down": down_weight, "i_gate2": gate2_weight,
           "norm1_gain": norm1_gain, "norm1_bias": norm1_bias, "gate1_bias": gate1_bias, "norm2_gain": norm2_gain,
           "norm2_bias": norm2_bias, "down_bias": down_bias, "gate2_bias": gate2_bias, "up_bias": up_bias}
    outs = {"out_o": ((2048, 128), bf16, hbm), "ing_o": ((2048, 128), bf16, hbm)}
    for name in NAMES:
        outs[name + "_o"] = (BLOCK[name], bf16, vmem)
    outs["small_o"] = ((16, 128), f32, vmem)
    scr = {}
    for name in NAMES:
        rows, cols = BLOCK[name]
        rq = rows // 4
        scr["w_" + name] = ((2, 2, 4, 2, 2, rq, cols), bf16)
        scr["g_" + name] = ((2, 2, 4, 2, 2, rq, cols), bf16)
        scr["b0_" + name] = ((2, 4, 2, 2, rq, cols), bf16)
        if use_x:
            scr["b1_" + name] = ((4, 2, rq, cols), bf16)
            scr["b2_" + name] = ((2, 4, rq, cols), bf16)
            scr["b3_" + name] = ((4, rq, cols), bf16)
            scr["b4_" + name] = ((4, rq, cols), bf16)
            scr["z_" + name] = ((4, 2, rq, cols), bf16)
            scr["b5_" + name] = ((2, 2, rq, cols), bf16)
            scr["b6_" + name] = ((2, rq, cols), bf16)
        else:
            scr["b1_" + name] = ((4, 2, 2, rq, cols), bf16)
            scr["b5_" + name] = ((2, 2, 2, rq, cols), bf16)
            scr["b6_" + name] = ((2, 2, rq, cols), bf16)
        scr["fin_" + name] = ((2, 2, rq, cols), bf16)
    scr.update({
        "qstage": ((128, 384), bf16), "vec": ((16, 128), f32), "vecs": ((4, 16, 128), f32), "vecr": ((4, 16, 128), f32),
        "xo": ((4, T, 128), bf16), "co": ((4, T, 128), bf16), "n1": ((T, D), bf16),
        "xn": ((1280, D), bf16), "qp": ((4, T, 128), bf16), "kv": ((4, 1280, 256), bf16),
        "p1": ((8, 512, 512), bf16), "p2": ((8, 512, 384), bf16), "po": ((8, 128, 256), bf16),
        "li": ((4, 8, T), f32), "att": ((4, 128, T), bf16), "ao": ((4, T, 128), f32),
        "g1": ((4, T, 128), f32), "mid": ((4, T, 128), f32), "n2": ((T, D), bf16),
        "hid": ((4, T, 512), bf16), "slp": ((4, T, 512), bf16), "out": ((4, T, 128), bf16),
        "pair": ((T, 1024), bf16), "gm": ((4, T, 128), f32), "ing": ((4, T, 128), bf16),
        "ex": ((2, 256, D), bf16), "exr": ((2, 256, D), bf16), "ez": ((256, D), bf16), "ezr": ((256, D), bf16),
        "sva": ((8, 128), f32), "sva_parts": ((4, 8, 128), f32), "sva_mine": ((8, 128), f32), "sva_total": ((8, 128), f32), "sva_all": ((8, 8, 128), f32),
        "svb": ((40, 128), f32), "svb_parts": ((4, 40, 128), f32), "svb_mine": ((40, 128), f32), "svb_total": ((40, 128), f32), "svb_all": ((8, 40, 128), f32),
    })
    shapes = [pltpu.VMEM(s, d) for s, d in scr.values()]
    names_scr = tuple(scr) + ("ssem", "rsem", "issem", "irsem", "lsem", "qsem")
    n_sem = 160
    dma = pltpu.SemaphoreType.DMA
    shapes += [dma((n_sem,)), dma((n_sem,)), dma((4, 4, 3)), dma((4, 4, 3)), dma((20,)), dma((2, 2))]
    res = pl.pallas_call(
        partial(kernel, use_x, tuple(ins), tuple(outs), names_scr),
        out_shape=[jax.ShapeDtypeStruct(s, d) for s, d, _ in outs.values()],
        in_specs=[hbm] * 8 + [vmem] * 8,
        out_specs=[sp for _, _, sp in outs.values()],
        scratch_shapes=shapes,
        compiler_params=pltpu.CompilerParams(collective_id=0, has_side_effects=True, vmem_limit_bytes=60 * 1024 * 1024),
    )(*ins.values())
    if not use_x:
        summed = lax.psum(tuple(v.astype(f32) for v in res[2:]), "grp")
        res = list(res[:2]) + list(summed)
    flat = {"out": (2048, 128), "ing": (2048, 128), "n1g": (128,), "n1b": (128,), "qkv": (128, 384),
            "w_out": (128, 128), "w_gate1": (128, 128), "g1b": (128,), "n2g": (128,), "n2b": (128,),
            "up": (128, 512), "upb": (512,), "w_down": (512, 128), "db": (128,), "w_gate2": (512, 128), "g2b": (128,)}
    kinds = {name: bf16 if name in ("out", "ing") else f32 for name in flat}
    return pl.pallas_call(
        finish,
        out_shape=[jax.ShapeDtypeStruct(shape, kinds[name]) for name, shape in flat.items()],
        in_specs=[vmem] * 8,
        out_specs=[vmem] * 16,
    )(*res)


def finish(out_i, ing_i, qkv_i, og_i, up_i, d0_i, d1_i, small_i, out, ing, n1g, n1b, qkv, w_out, w_gate1, g1b, n2g, n2b,
           up, upb, w_down, db, w_gate2, g2b):
    out[...] = out_i[...]
    ing[...] = ing_i[...]
    g = qkv_i[...].astype(f32)
    qkv[...] = cat([g[:, (2 * j + h) * 64:(2 * j + h + 1) * 64] for h in range(2) for j in range(3)])
    w_out[...] = og_i[:, 0:128].astype(f32)
    w_gate1[...] = og_i[:, 128:256].astype(f32)
    up[...] = up_i[...].astype(f32)
    w_down[0:256, :] = d0_i[:, 0:128].astype(f32)
    w_down[256:512, :] = d1_i[:, 0:128].astype(f32)
    w_gate2[0:256, :] = d0_i[:, 128:256].astype(f32)
    w_gate2[256:512, :] = d1_i[:, 128:256].astype(f32)
    for i, ref in enumerate((n1g, n1b, n2g, n2b, g1b, db, g2b)):
        ref[...] = small_i[i:i + 1, :].reshape(128)
    for i in range(4):
        upb[128 * i:128 * i + 128] = small_i[8 + i:9 + i, :].reshape(128)


def solution(mesh):
    act = P(("grp", "row"), "col")
    col, row = P("col"), P("row")
    cr, rc = P("col", "row"), P("row", "col")
    return jax.shard_map(
        partial(body, mesh.shape["grp"] == 2),
        mesh=mesh,
        in_specs=(act, act, col, col, cr, rc, rc, col, col, col, cr, row, rc, col, rc, col),
        out_specs=(act, act, col, col, cr, rc, rc, col, col, col, cr, row, rc, col, rc, col),
        check_vma=False,
    )
```
